128 devices in a mesh: seq: 4 (over x), mod: 2 (over core), tp: 16 (over y, z).
Axes of the slice: x: 4, y: 4, z: 4, core: 2. Of those that a mesh axis runs over, the one named last changes fastest.
Arguments:
- activations: bfloat16 [1536, 8192], P(('seq', 'mod')), may hold values from -12 to 12
- grad_attn: bfloat16 [1536, 6144], P(('seq', 'mod'), 'tp'), may hold values from -6 to 6
- weights: bfloat16 [2, 8192, 3, 6144], P('mod', None, None, 'tp'), may hold values from -0.049718446 to 0.049718446
- modality: int32 [1536], replicated, may hold values from 0 to 1, as said below
Outputs:
- grad_input: bfloat16 [1536, 8192], P(('seq', 'mod'), 'tp')
The draws below stay inside these ranges and needn't reach their ends.
Inputs may be any that keep to these rules, and one draw needn't show every extreme that they name: Tokens come in runs of 12 of one modality. In each aligned block of 192 tokens (the tokens of one index of seq+mod) each modality has at most 144 tokens. In every draw both blocks of some index of seq hold 144 image tokens each, and both blocks of another index hold 144 text tokens each.
All inputs are finite; a program needn't handle non-finite values.
Results may differ from the reference program's by a relative error of at most 0.013.
Values may be sent and summed in bfloat16 or wider, within the bound.
No kernel may reach another device: no remote copies, remote signals or barrier semaphores. Data moves between devices by JAX's collectives and lax.ppermute only.
A program may use at most 128 MiB of HBM per device.

```python
import jax
import jax.numpy as jnp
from jax import lax

D = 8192
HEADS = 48
HD = 128
SHARD_LEN = 384
LEN = 1536
SPAN = 12


def draw_activations(key, part):
    key = jax.random.fold_in(key, 11)
    base_noise = jax.random.truncated_normal(key, -3.0, 3.0, (LEN, D), jnp.float32)
    values = base_noise
    return values.astype(jnp.bfloat16)


def draw_weights(key, part):
    key = jax.random.fold_in(key, 12)
    values = jax.random.truncated_normal(key, -4.0, 4.0, (2, D, 3, HEADS * HD), jnp.float32) / jnp.sqrt(jnp.float32(D))
    return values.astype(jnp.bfloat16)


def draw_modality(key, part):
    key = jax.random.fold_in(key, 13)
    count_key, full_key, other_key, score_key = jax.random.split(key, 4)
    shard_total = LEN // SHARD_LEN
    block_total = 2 * shard_total
    counts = jax.random.randint(count_key, (block_total,), 4, 13)
    full_shard = jax.random.randint(full_key, (), 0, shard_total)
    other_shard = (full_shard + 1 + jax.random.randint(other_key, (), 0, shard_total - 1)) % shard_total
    shard_of = jnp.arange(block_total, dtype=jnp.int32) // 2
    counts = jnp.where(shard_of == full_shard, 12, jnp.where(shard_of == other_shard, 4, counts))
    scores = jax.random.randint(score_key, (block_total, 16), 0, 65536) * 16 + jnp.arange(16, dtype=jnp.int32)[None, :]
    span_rank = jnp.argsort(jnp.argsort(scores, axis=1), axis=1)
    image_span = (span_rank < counts[:, None]).astype(jnp.int32)
    return jnp.repeat(image_span, SPAN, axis=1).reshape(LEN)


def steps_of(own_key, shape, pieces, least, largest):
    def one(dim, shards_of):
        draws = jax.random.uniform(jax.random.fold_in(jax.random.fold_in(own_key, 6), dim), (shards_of,), jnp.float32, least / len(pieces), largest / len(pieces))
        return jnp.repeat(jnp.exp(draws), shape[dim] // shards_of).reshape((-1,) + (1,) * (len(shape) - dim - 1))

    level = one(*pieces[0])
    for cut in pieces[1:]:
        level = level * one(*cut)
    return level


def noise(stream_key, extent, scale, bound, pieces=(), held_as=jnp.bfloat16):
    result = scale * jax.random.normal(stream_key, extent, jnp.float32)
    if pieces:
        result = result * steps_of(stream_key, extent, pieces, -0.22, 0.18)
    return jnp.clip(result, -bound, bound).astype(held_as)


def setup_inputs(seed: int = 0) -> dict:
    keys = jax.random.split(jax.random.key(seed), 5)
    return {
        "activations": draw_activations(jax.random.fold_in(keys[4], 71), 0),
        "grad_attn": noise(keys[1], (LEN, HEADS * HD), 1.0, 6.0, ((0, 8), (1, 16))),
        "weights": draw_weights(jax.random.fold_in(keys[4], 71), 0),
        "modality": draw_modality(jax.random.fold_in(keys[4], 71), 0),
    }


def split_heads(columns):
    return columns.reshape(LEN, HEADS, HD).transpose(1, 0, 2)


def merge_heads(columns):
    return columns.transpose(1, 0, 2).reshape(LEN, HEADS * HD)


def reference(activations, grad_attn, weights, modality):
    head_cols = HEADS * HD
    weight_mats = weights.reshape(2, D, 3 * head_cols)
    is_image = (modality == 1)[:, None]
    text_part = jnp.dot(activations, weight_mats[0], preferred_element_type=jnp.float32)
    image_part = jnp.dot(activations, weight_mats[1], preferred_element_type=jnp.float32)
    projected = jnp.where(is_image, image_part, text_part).astype(jnp.bfloat16)
    queries = split_heads(projected[:, :head_cols])
    keys_all = split_heads(projected[:, head_cols:2 * head_cols])
    values_all = split_heads(projected[:, 2 * head_cols:])
    grads_all = split_heads(grad_attn)
    position = jnp.arange(LEN, dtype=jnp.int32)
    causal = position[:, None] >= position[None, :]
    score_scale = HD ** -0.5

    def one_head(operands):
        query_rows, key_rows, value_rows, grad_rows = operands
        scores = jnp.dot(query_rows, key_rows.T, preferred_element_type=jnp.float32) * score_scale
        scores = jnp.where(causal, scores, -jnp.inf)
        row_max = jnp.max(scores, axis=1, keepdims=True)
        lifted = jnp.exp(scores - row_max)
        attn_probs = lifted / jnp.sum(lifted, axis=1, keepdims=True)
        probs_low = attn_probs.astype(jnp.bfloat16)
        dprobs = jnp.dot(grad_rows, value_rows.T, preferred_element_type=jnp.float32)
        row_dot = jnp.sum(attn_probs * dprobs, axis=1, keepdims=True)
        dscores = (attn_probs * (dprobs - row_dot)).astype(jnp.bfloat16)
        grad_query = jnp.dot(dscores, key_rows, preferred_element_type=jnp.float32) * score_scale
        grad_key = jnp.dot(dscores.T, query_rows, preferred_element_type=jnp.float32) * score_scale
        grad_value = jnp.dot(probs_low.T, grad_rows, preferred_element_type=jnp.float32)
        return grad_query.astype(jnp.bfloat16), grad_key.astype(jnp.bfloat16), grad_value.astype(jnp.bfloat16)

    grad_query, grad_key, grad_value = lax.map(one_head, (queries, keys_all, values_all, grads_all))
    grad_qkv = jnp.concatenate([merge_heads(grad_query), merge_heads(grad_key), merge_heads(grad_value)], axis=1)
    dims = (((1,), (1,)), ((), ()))
    text_back = lax.dot_general(grad_qkv, weight_mats[0], dims, preferred_element_type=jnp.float32)
    image_back = lax.dot_general(grad_qkv, weight_mats[1], dims, preferred_element_type=jnp.float32)
    return jnp.where(is_image, image_back, text_back).astype(jnp.bfloat16)
```

```python
import functools

import jax
import jax.numpy as jnp
from jax import lax
from jax.experimental import pallas as pl
from jax.experimental.pallas import tpu as pltpu
from jax.sharding import PartitionSpec as P

HD = 128
NH = 3
RING = 4
SCALE = HD**-0.5
AXES = ("seq", "mod", "tp")
MIB = 1024 * 1024


def core_swap(x):
    return lax.ppermute(x, "mod", [(0, 1), (1, 0)])


def project_kernel(a_ref, w_ref, out_ref, acc_ref):
    step = pl.program_id(0)
    w = jnp.concatenate([w_ref[0], w_ref[1], w_ref[2]], axis=1)
    part = jnp.dot(a_ref[...], w, preferred_element_type=jnp.float32)

    @pl.when(step == 0)
    def _():
        acc_ref[...] = part

    @pl.when(step > 0)
    def _():
        acc_ref[...] += part

    @pl.when(step == pl.num_programs(0) - 1)
    def _():
        for h in range(NH):
            for c in range(3):
                lo = c * NH * HD + h * HD
                out_ref[h, :, c * HD : (c + 1) * HD] = acc_ref[:, lo : lo + HD].astype(jnp.bfloat16)


def project(a, w3):
    rows, depth = a.shape
    block = 1024
    return pl.pallas_call(
        project_kernel,
        grid=(depth // block,),
        in_specs=[
            pl.BlockSpec((rows, block), lambda i: (0, i)),
            pl.BlockSpec((3, block, NH * HD), lambda i: (0, i, 0)),
        ],
        out_specs=pl.BlockSpec((NH, rows, 3 * HD), lambda i: (0, 0, 0)),
        out_shape=jax.ShapeDtypeStruct((NH, rows, 3 * HD), jnp.bfloat16),
        scratch_shapes=[pltpu.VMEM((rows, 3 * NH * HD), jnp.float32)],
        compiler_params=pltpu.CompilerParams(vmem_limit_bytes=24 * MIB),
        cost_estimate=pl.CostEstimate(
            flops=2 * rows * depth * 9 * HD, bytes_accessed=depth * 9 * HD * 2, transcendentals=0
        ),
        name="project",
    )(a, w3)


def attention_kernel(where_ref, r0, r1, r2, r3, kvo_ref, own_ref, oth_ref, q_s, g_s, k_s, v_s, dk_s, dv_s):
    chip = where_ref[0]
    core = where_ref[1]
    rows = r0.shape[0]
    both = 2 * rows
    for k, r in enumerate((r0, r1, r2, r3)):
        shard = (chip - k + RING) % RING
        q_s[shard] = r[:, 0:HD]
        g_s[shard] = r[:, 3 * HD : 4 * HD]
        mine = pl.ds(pl.multiple_of((2 * shard + core) * rows, rows), rows)
        other = pl.ds(pl.multiple_of((2 * shard + 1 - core) * rows, rows), rows)
        k_s[mine, :] = r[:, HD : 2 * HD]
        v_s[mine, :] = r[:, 2 * HD : 3 * HD]
        k_s[other, :] = kvo_ref[k, :, 0:HD]
        v_s[other, :] = kvo_ref[k, :, HD : 2 * HD]
    nt = (((1,), (1,)), ((), ()))
    tn = (((0,), (0,)), ((), ()))
    for s in range(RING - 1, -1, -1):
        width = both * (s + 1)
        q = q_s[s]
        g = g_s[s]
        kk = k_s[0:width, :]
        vv = v_s[0:width, :]
        scores = lax.dot_general(q, kk, nt, preferred_element_type=jnp.float32) * SCALE
        row = lax.broadcasted_iota(jnp.int32, (rows, width), 0) + (2 * s + core) * rows
        col = lax.broadcasted_iota(jnp.int32, (rows, width), 1)
        scores = jnp.where(col <= row, scores, -jnp.inf)
        lifted = jnp.exp(scores - jnp.max(scores, axis=1, keepdims=True))
        probs = lifted / jnp.sum(lifted, axis=1, keepdims=True)
        low = probs.astype(jnp.bfloat16)
        dprobs = lax.dot_general(g, vv, nt, preferred_element_type=jnp.float32)
        row_dot = jnp.sum(probs * dprobs, axis=1, keepdims=True)
        ds = (probs * (dprobs - row_dot)).astype(jnp.bfloat16)
        dq = jnp.dot(ds, kk, preferred_element_type=jnp.float32) * SCALE
        dk = lax.dot_general(ds, q, tn, preferred_element_type=jnp.float32) * SCALE
        dv = lax.dot_general(low, g, tn, preferred_element_type=jnp.float32)
        if s == RING - 1:
            dk_s[...] = dk
            dv_s[...] = dv
        else:
            dk_s[0:width, :] += dk
            dv_s[0:width, :] += dv
        own_ref[(chip - s + RING) % RING, :, 0:HD] = dq
    for k in range(RING):
        shard = (chip - k + RING) % RING
        mine = pl.ds(pl.multiple_of((2 * shard + core) * rows, rows), rows)
        other = pl.ds(pl.multiple_of((2 * shard + 1 - core) * rows, rows), rows)
        own_ref[k, :, HD : 2 * HD] = dk_s[mine, :]
        own_ref[k, :, 2 * HD : 3 * HD] = dv_s[mine, :]
        oth_ref[k, :, 0:HD] = dk_s[other, :].astype(jnp.bfloat16)
        oth_ref[k, :, HD : 2 * HD] = dv_s[other, :].astype(jnp.bfloat16)


def attention(where, parts, kv_other):
    rows = parts[0].shape[0]
    total = 2 * RING * rows
    vmem = pl.BlockSpec(memory_space=pltpu.VMEM)
    return pl.pallas_call(
        attention_kernel,
        in_specs=[pl.BlockSpec(memory_space=pltpu.SMEM)] + [vmem] * 5,
        out_specs=[vmem, vmem],
        out_shape=[
            jax.ShapeDtypeStruct((RING, rows, 3 * HD), jnp.float32),
            jax.ShapeDtypeStruct((RING, rows, 2 * HD), jnp.bfloat16),
        ],
        scratch_shapes=[
            pltpu.VMEM((RING, rows, HD), jnp.bfloat16),
            pltpu.VMEM((RING, rows, HD), jnp.bfloat16),
            pltpu.VMEM((total, HD), jnp.bfloat16),
            pltpu.VMEM((total, HD), jnp.bfloat16),
            pltpu.VMEM((total, HD), jnp.float32),
            pltpu.VMEM((total, HD), jnp.float32),
        ],
        compiler_params=pltpu.CompilerParams(vmem_limit_bytes=32 * MIB),
        cost_estimate=pl.CostEstimate(flops=10**9, bytes_accessed=4 * 10**6, transcendentals=10**6),
        name="attention",
    )(where, *parts, kv_other)


def collect_kernel(where_ref, own_ref, oth_ref, r0, r1, r2, r3, mine_ref, send_ref):
    chip = where_ref[0]
    for k, r in enumerate((r0, r1, r2, r3)):
        head = (chip + k) % RING

        @pl.when(head < NH)
        def _():
            x = r[...]
            zero = jnp.zeros_like(x)
            mine_ref[head] = jnp.where(own_ref[...] > 0, x, zero)
            send_ref[head] = jnp.where(oth_ref[...] > 0, x, zero)


def collect(where, own, oth, parts):
    rows, width = parts[0].shape
    vmem = pl.BlockSpec(memory_space=pltpu.VMEM)
    shape = jax.ShapeDtypeStruct((NH, rows, width), jnp.bfloat16)
    return pl.pallas_call(
        collect_kernel,
        in_specs=[pl.BlockSpec(memory_space=pltpu.SMEM)] + [vmem] * 6,
        out_specs=[vmem, vmem],
        out_shape=[shape, shape],
        cost_estimate=pl.CostEstimate(flops=10**6, bytes_accessed=2 * 10**6, transcendentals=0),
        name="collect",
    )(where, own, oth, *parts)


def back_kernel(place_ref, mine_ref, oth_ref, w_ref, own_out, oth_out, g_s):
    rows = mine_ref.shape[1]

    @pl.when(pl.program_id(0) == 0)
    def _():
        for h in range(NH):
            for c in range(3):
                lo = c * NH * HD + h * HD
                g_s[0:rows, lo : lo + HD] = mine_ref[h, :, c * HD : (c + 1) * HD]
                g_s[rows : 2 * rows, lo : lo + HD] = oth_ref[h, :, c * HD : (c + 1) * HD]

    w = jnp.concatenate([w_ref[0, 0, 0], w_ref[1, 0, 0], w_ref[2, 0, 0]], axis=1)
    res = lax.dot_general(
        g_s[...], w, (((1,), (1,)), ((), ())), preferred_element_type=jnp.float32
    ).astype(jnp.bfloat16)
    own_out[0] = res[0:rows]
    oth_out[0] = res[rows : 2 * rows]


def back(place, mine, oth, w3, stream, streams):
    _, rows, _ = mine.shape
    depth = w3.shape[1]
    dests = RING * RING
    cols = depth // dests // streams
    w5 = w3.reshape(3, dests, streams, cols, NH * HD)
    shape = jax.ShapeDtypeStruct((dests, rows, cols), jnp.bfloat16)
    return pl.pallas_call(
        back_kernel,
        grid_spec=pltpu.PrefetchScalarGridSpec(
            num_scalar_prefetch=1,
            grid=(dests,),
            in_specs=[
                pl.BlockSpec((NH, rows, 3 * HD), lambda i, p: (0, 0, 0)),
                pl.BlockSpec((NH, rows, 3 * HD), lambda i, p: (0, 0, 0)),
                pl.BlockSpec((3, 1, 1, cols, NH * HD), lambda i, p: (0, i, stream, 0, 0)),
            ],
            out_specs=[
                pl.BlockSpec((1, rows, cols), lambda i, p: (p[0, i], 0, 0)),
                pl.BlockSpec((1, rows, cols), lambda i, p: (p[1, i], 0, 0)),
            ],
            scratch_shapes=[pltpu.VMEM((2 * rows, 9 * HD), jnp.bfloat16)],
        ),
        out_shape=[shape, shape],
        compiler_params=pltpu.CompilerParams(vmem_limit_bytes=24 * MIB),
        cost_estimate=pl.CostEstimate(
            flops=2 * 2 * rows * dests * cols * 9 * HD,
            bytes_accessed=dests * cols * (9 * HD * 2 + 4 * rows),
            transcendentals=0,
        ),
        name="back",
    )(place, mine, oth, w5)


def ring_perm(first, hop):
    pairs = []
    for s in range(RING):
        for m in range(2):
            for y in range(RING):
                for z in range(RING):
                    if (m == 0) == first:
                        to = (y, (z + hop) % RING)
                    else:
                        to = ((y + hop) % RING, z)
                    base = (s * 2 + m) * RING * RING
                    pairs.append((base + y * RING + z, base + to[0] * RING + to[1]))
    return pairs


def per_device(activations, grad_attn, weights, modality):
    rows, depth = activations.shape
    chip = lax.axis_index("seq")
    core = lax.axis_index("mod")
    tp = lax.axis_index("tp")
    where = jnp.stack([chip, core]).astype(jnp.int32)
    w3 = jnp.transpose(weights[0], (1, 0, 2))

    own_mod = lax.dynamic_slice_in_dim(modality, (2 * chip + core) * rows, rows)
    is_mine = (own_mod == core).astype(jnp.int32)[:, None]
    is_other = 1 - is_mine

    act_other = core_swap(activations)
    proj_own = project(activations, w3)
    proj_other = project(act_other, w3)
    proj_back = core_swap(proj_other)
    g_heads = grad_attn.reshape(rows, NH, HD).transpose(1, 0, 2)
    heads = jnp.where((is_mine > 0)[None], proj_own, proj_back)
    heads = jnp.concatenate([heads, g_heads], axis=2)

    parts = []
    for hop in range(RING):
        head = jnp.minimum((chip + hop) % RING, NH - 1)
        x = lax.dynamic_index_in_dim(heads, head, 0, keepdims=False)
        if hop:
            pairs = [(i, (i + hop) % RING) for i in range(RING) if (i + hop) % RING < NH]
            x = lax.ppermute(x, "seq", pairs)
        parts.append(x)
    kv_mine = jnp.stack([x[:, HD : 3 * HD] for x in parts])
    kv_other = core_swap(kv_mine)
    own, oth = attention(where, parts, kv_other)
    from_other = core_swap(oth)

    grads = []
    for hop in range(RING):
        kv = own[hop, :, HD:] + from_other[hop].astype(jnp.float32)
        x = jnp.concatenate([own[hop, :, :HD], kv], axis=1).astype(jnp.bfloat16)
        if hop:
            pairs = [(i, (i - hop) % RING) for i in range(NH)]
            x = lax.ppermute(x, "seq", pairs)
        grads.append(x)

    mine, send = collect(where, is_mine, is_other, grads)
    other = core_swap(send)

    dest = jnp.arange(RING * RING, dtype=jnp.int32)
    dy = (dest // RING - tp // RING + RING) % RING
    dz = (dest % RING - tp % RING + RING) % RING
    z_first = dz * RING + dy
    y_first = dy * RING + dz
    place = jnp.stack(
        [jnp.where(core == 0, z_first, y_first), jnp.where(core == 0, y_first, z_first)]
    ).astype(jnp.int32)

    streams = 1
    quarter = RING
    seconds = []
    for stream in range(streams):
        own_rows, other_rows = back(place, mine, other, w3, stream, streams)
        returned = core_swap(other_rows)

        def piece(k):
            cut = slice(k * quarter, (k + 1) * quarter)
            return own_rows[cut].astype(jnp.float32) + returned[cut].astype(jnp.float32)

        total = piece(0)
        for hop in (2, 1, 3):
            got = lax.ppermute(piece(hop).astype(jnp.bfloat16), AXES, ring_perm(True, hop))
            total = total + got.astype(jnp.float32)
        seconds.append(total)
    total = jnp.concatenate(seconds, axis=2) if streams > 1 else seconds[0]
    result = total[0]
    for hop in (2, 1, 3):
        got = lax.ppermute(total[hop].astype(jnp.bfloat16), AXES, ring_perm(False, hop))
        result = result + got.astype(jnp.float32)
    return result.astype(jnp.bfloat16)


def solution(mesh):
    in_specs = (P(("seq", "mod"), None), P(("seq", "mod"), "tp"), P("mod", None, None, "tp"), P())
    out_specs = P(("seq", "mod"), "tp")
    return jax.shard_map(
        per_device, mesh=mesh, in_specs=in_specs, out_specs=out_specs, check_vma=False
    )
```

```python
import functools

import jax
import jax.numpy as jnp
from jax import lax
from jax.experimental import pallas as pl
from jax.experimental.pallas import tpu as pltpu
from jax.sharding import PartitionSpec as P

HD = 128
NH = 3
RING = 4
SCALE = HD**-0.5
AXES = ("seq", "mod", "tp")
MIB = 1024 * 1024
VMEM = 60 * MIB


def core_swap(x):
    return lax.ppermute(x, "mod", [(0, 1), (1, 0)])


def own_kernel(a_ref, w_ref, out_ref):
    step = pl.program_id(0)
    w = jnp.concatenate([w_ref[0], w_ref[1], w_ref[2]], axis=1)
    part = jnp.dot(a_ref[...], w, preferred_element_type=jnp.float32)

    @pl.when(step == 0)
    def _():
        out_ref[...] = part

    @pl.when(step > 0)
    def _():
        out_ref[...] += part


def project_own(a, w3, steps, block):
    rows = a.shape[0]
    return pl.pallas_call(
        own_kernel,
        grid=(steps,),
        in_specs=[
            pl.BlockSpec((rows, block), lambda i: (0, i)),
            pl.BlockSpec((3, block, NH * HD), lambda i: (0, i, 0)),
        ],
        out_specs=pl.BlockSpec((rows, 9 * HD), lambda i: (0, 0)),
        out_shape=jax.ShapeDtypeStruct((rows, 9 * HD), jnp.float32),
        compiler_params=pltpu.CompilerParams(vmem_limit_bytes=VMEM),
        cost_estimate=pl.CostEstimate(
            flops=2 * rows * steps * block * 9 * HD,
            bytes_accessed=steps * block * 9 * HD * 2,
            transcendentals=0,
        ),
        name="project_own",
    )(a, w3)


def project_kernel(early, part_ref, own_ref, oth_ref, w_ref, own_out, oth_out, acc_ref):
    step = pl.program_id(0)
    rows = own_ref.shape[0]
    w = jnp.concatenate([w_ref[0], w_ref[1], w_ref[2]], axis=1)

    @pl.when(step == 0)
    def _():
        acc_ref[0:rows] = part_ref[...]
        acc_ref[rows:] = jnp.dot(oth_ref[...], w, preferred_element_type=jnp.float32)

    @pl.when((step > 0) & (step < early))
    def _():
        acc_ref[rows:] += jnp.dot(oth_ref[...], w, preferred_element_type=jnp.float32)

    @pl.when(step >= early)
    def _():
        a = jnp.concatenate([own_ref[...], oth_ref[...]], axis=0)
        acc_ref[...] += jnp.dot(a, w, preferred_element_type=jnp.float32)

    @pl.when(step == pl.num_programs(0) - 1)
    def _():
        for h in range(NH):
            for c in range(3):
                lo = c * NH * HD + h * HD
                x = acc_ref[:, lo : lo + HD].astype(jnp.bfloat16)
                own_out[h, :, c * HD : (c + 1) * HD] = x[0:rows]
                oth_out[h, :, c * HD : (c + 1) * HD] = x[rows:]


def project(part, own, other, w3, early, block):
    rows, depth = own.shape
    shape = jax.ShapeDtypeStruct((NH, rows, 3 * HD), jnp.bfloat16)
    out_spec = pl.BlockSpec((NH, rows, 3 * HD), lambda i: (0, 0, 0))
    return pl.pallas_call(
        functools.partial(project_kernel, early),
        grid=(depth // block,),
        in_specs=[
            pl.BlockSpec((rows, 9 * HD), lambda i: (0, 0)),
            pl.BlockSpec((rows, block), lambda i: (0, jnp.maximum(i, early))),
            pl.BlockSpec((rows, block), lambda i: (0, i)),
            pl.BlockSpec((3, block, NH * HD), lambda i: (0, i, 0)),
        ],
        out_specs=[out_spec, out_spec],
        out_shape=[shape, shape],
        scratch_shapes=[pltpu.VMEM((2 * rows, 9 * HD), jnp.float32)],
        compiler_params=pltpu.CompilerParams(vmem_limit_bytes=VMEM),
        cost_estimate=pl.CostEstimate(
            flops=3 * rows * depth * 9 * HD, bytes_accessed=depth * 9 * HD * 2, transcendentals=0
        ),
        name="project",
    )(part, own, other, w3)


def attention_kernel(
    where_ref, a0, a1, a2, a3, b0, b1, b2, b3, g_ref0, g_ref1, g_ref2, g_ref3, own_ref, oth_ref, q_s, g_s, k_s, v_s, dk_s, dv_s
):
    chip = where_ref[0]
    core = where_ref[1]
    rows = a0.shape[0]
    both = 2 * rows
    own = (a0, a1, a2, a3)
    oth = (b0, b1, b2, b3)
    grads = (g_ref0, g_ref1, g_ref2, g_ref3)
    for k, (r, o, g) in enumerate(zip(own, oth, grads)):
        shard = (chip - k + RING) % RING
        q_s[shard] = r[:, 0:HD]
        g_s[shard] = g[...]
        mine = pl.ds(pl.multiple_of((2 * shard + core) * rows, rows), rows)
        other = pl.ds(pl.multiple_of((2 * shard + 1 - core) * rows, rows), rows)
        k_s[mine, :] = r[:, HD : 2 * HD]
        v_s[mine, :] = r[:, 2 * HD : 3 * HD]
        k_s[other, :] = o[:, HD : 2 * HD]
        v_s[other, :] = o[:, 2 * HD : 3 * HD]
    nt = (((1,), (1,)), ((), ()))
    tn = (((0,), (0,)), ((), ()))
    for s in range(RING - 1, -1, -1):
        width = both * (s + 1)
        q = q_s[s]
        g = g_s[s]
        kk = k_s[0:width, :]
        vv = v_s[0:width, :]
        scores = lax.dot_general(q, kk, nt, preferred_element_type=jnp.float32) * SCALE
        row = lax.broadcasted_iota(jnp.int32, (rows, width), 0) + (2 * s + core) * rows
        col = lax.broadcasted_iota(jnp.int32, (rows, width), 1)
        scores = jnp.where(col <= row, scores, -jnp.inf)
        lifted = jnp.exp(scores - jnp.max(scores, axis=1, keepdims=True))
        probs = lifted / jnp.sum(lifted, axis=1, keepdims=True)
        low = probs.astype(jnp.bfloat16)
        dprobs = lax.dot_general(g, vv, nt, preferred_element_type=jnp.float32)
        row_dot = jnp.sum(probs * dprobs, axis=1, keepdims=True)
        ds = (probs * (dprobs - row_dot)).astype(jnp.bfloat16)
        dq = jnp.dot(ds, kk, preferred_element_type=jnp.float32) * SCALE
        dk = lax.dot_general(ds, q, tn, preferred_element_type=jnp.float32) * SCALE
        dv = lax.dot_general(low, g, tn, preferred_element_type=jnp.float32)
        if s == RING - 1:
            dk_s[...] = dk
            dv_s[...] = dv
        else:
            dk_s[0:width, :] += dk
            dv_s[0:width, :] += dv
        own_ref[(chip - s + RING) % RING, :, 0:HD] = dq
    for k in range(RING):
        shard = (chip - k + RING) % RING
        mine = pl.ds(pl.multiple_of((2 * shard + core) * rows, rows), rows)
        other = pl.ds(pl.multiple_of((2 * shard + 1 - core) * rows, rows), rows)
        own_ref[k, :, HD : 2 * HD] = dk_s[mine, :]
        own_ref[k, :, 2 * HD : 3 * HD] = dv_s[mine, :]
        oth_ref[k, :, 0:HD] = dk_s[other, :].astype(jnp.bfloat16)
        oth_ref[k, :, HD : 2 * HD] = dv_s[other, :].astype(jnp.bfloat16)


def attention(where, parts, others, grads):
    rows = parts[0].shape[0]
    total = 2 * RING * rows
    vmem = pl.BlockSpec(memory_space=pltpu.VMEM)
    return pl.pallas_call(
        attention_kernel,
        in_specs=[pl.BlockSpec(memory_space=pltpu.SMEM)] + [vmem] * 12,
        out_specs=[vmem, vmem],
        out_shape=[
            jax.ShapeDtypeStruct((RING, rows, 3 * HD), jnp.float32),
            jax.ShapeDtypeStruct((RING, rows, 2 * HD), jnp.bfloat16),
        ],
        scratch_shapes=[
            pltpu.VMEM((RING, rows, HD), jnp.bfloat16),
            pltpu.VMEM((RING, rows, HD), jnp.bfloat16),
            pltpu.VMEM((total, HD), jnp.bfloat16),
            pltpu.VMEM((total, HD), jnp.bfloat16),
            pltpu.VMEM((total, HD), jnp.float32),
            pltpu.VMEM((total, HD), jnp.float32),
        ],
        compiler_params=pltpu.CompilerParams(vmem_limit_bytes=32 * MIB),
        cost_estimate=pl.CostEstimate(flops=10**9, bytes_accessed=4 * 10**6, transcendentals=10**6),
        name="attention",
    )(where, *parts, *others, *grads)


def back_kernel(
    chunk, place_ref, mask_ref, a0, a1, a2, a3, b0, b1, b2, b3, w_hbm, own_hbm, oth_hbm, w_s, g_s, o_s, w_sem, o_sem
):
    chip = place_ref[2, 0]
    rows = a0.shape[0]
    steps = w_s.shape[0]
    cols = w_s.shape[3]

    def fetch(i):
        return pltpu.make_async_copy(w_hbm.at[:, pl.ds(i * chunk, chunk)], w_s.at[i], w_sem.at[i])

    def put(i, j, side):
        out = (own_hbm, oth_hbm)[side]
        dest = place_ref[side, i * chunk + j]
        return pltpu.make_async_copy(o_s.at[side, i * chunk + j], out.at[dest], o_sem.at[side, i * chunk + j])

    for i in range(steps):
        fetch(i).start()
    for k, (own, oth) in enumerate(((a0, b0), (a1, b1), (a2, b2), (a3, b3))):
        head = (chip + k) % RING

        @pl.when(head < NH)
        def _():
            for side, x_ref in enumerate((own, oth)):
                x = x_ref[...]
                x = jnp.where(mask_ref[side] > 0, x, jnp.zeros_like(x))
                for c in range(3):
                    lo = pl.multiple_of((c * NH + head) * HD, HD)
                    g_s[side * rows : (side + 1) * rows, pl.ds(lo, HD)] = x[:, c * HD : (c + 1) * HD]

    for i in range(steps):
        fetch(i).wait()
        w = jnp.concatenate([w_s[i, c].reshape(chunk * cols, NH * HD) for c in range(3)], axis=1)
        res = lax.dot_general(
            g_s[...], w, (((1,), (1,)), ((), ())), preferred_element_type=jnp.float32
        ).astype(jnp.bfloat16)
        for j in range(chunk):
            for side in range(2):
                o_s[side, i * chunk + j] = res[side * rows : (side + 1) * rows, j * cols : (j + 1) * cols]
                put(i, j, side).start()
    for i in range(steps):
        for j in range(chunk):
            for side in range(2):
                put(i, j, side).wait()


def back(place, masks, own, oth, w3, stream, streams):
    rows, _ = own[0].shape
    depth = w3.shape[1]
    dests = RING * RING
    cols = depth // dests // streams
    chunk = 1024 // cols
    w4 = w3.reshape(3, dests, streams, cols, NH * HD)
    shape = jax.ShapeDtypeStruct((dests, rows, cols), jnp.bfloat16)
    vmem = pl.BlockSpec(memory_space=pltpu.VMEM)
    anywhere = pl.BlockSpec(memory_space=pl.ANY)

    def kernel(place_ref, mask_ref, *refs):
        w_ref = refs[8].at[:, :, stream]
        back_kernel(chunk, place_ref, mask_ref, *refs[:8], w_ref, *refs[9:])

    return pl.pallas_call(
        kernel,
        in_specs=[pl.BlockSpec(memory_space=pltpu.SMEM), vmem] + [vmem] * 8 + [anywhere],
        out_specs=[anywhere, anywhere],
        out_shape=[shape, shape],
        scratch_shapes=[
            pltpu.VMEM((dests // chunk, 3, chunk, cols, NH * HD), jnp.bfloat16),
            pltpu.VMEM((2 * rows, 9 * HD), jnp.bfloat16),
            pltpu.VMEM((2, dests, rows, cols), jnp.bfloat16),
            pltpu.SemaphoreType.DMA((dests // chunk,)),
            pltpu.SemaphoreType.DMA((2, dests)),
        ],
        compiler_params=pltpu.CompilerParams(vmem_limit_bytes=VMEM),
        cost_estimate=pl.CostEstimate(
            flops=2 * 2 * rows * dests * cols * 9 * HD,
            bytes_accessed=dests * cols * (9 * HD * 2 + 4 * rows),
            transcendentals=0,
        ),
        name="back",
    )(place, masks, *own, *oth, w4)


def ring_perm(first, hop):
    pairs = []
    for s in range(RING):
        for m in range(2):
            for y in range(RING):
                for z in range(RING):
                    if (m == 0) == first:
                        to = (y, (z + hop) % RING)
                    else:
                        to = ((y + hop) % RING, z)
                    base = (s * 2 + m) * RING * RING
                    pairs.append((base + y * RING + z, base + to[0] * RING + to[1]))
    return pairs


def per_device(activations, grad_attn, weights, modality):
    rows, depth = activations.shape
    chip = lax.axis_index("seq")
    core = lax.axis_index("mod")
    tp = lax.axis_index("tp")
    where = jnp.stack([chip, core]).astype(jnp.int32)
    w3 = jnp.transpose(weights[0], (1, 0, 2))

    own_mod = lax.dynamic_slice_in_dim(modality, (2 * chip + core) * rows, rows)
    other_mod = lax.dynamic_slice_in_dim(modality, (2 * chip + 1 - core) * rows, rows)
    masks = (jnp.stack([own_mod, other_mod]) == core).astype(jnp.int32)[:, :, None]

    def to_heads(hop):
        return [(i, (i + hop) % RING) for i in range(RING) if (i + hop) % RING < NH]

    def head_part(x, hop):
        head = jnp.minimum((chip + hop) % RING, NH - 1)
        return lax.dynamic_index_in_dim(x, head, 0, keepdims=False)

    act_other = core_swap(activations)
    g_heads = grad_attn.reshape(rows, NH, HD).transpose(1, 0, 2)
    g_parts = []
    for hop in (0, 2, 1, 3):
        x = head_part(g_heads, hop)
        g_parts.append(lax.ppermute(x, "seq", to_heads(hop)) if hop else x)
    g_parts = [g_parts[0], g_parts[2], g_parts[1], g_parts[3]]

    block, early = 2048, 2
    part = project_own(activations, w3, early, block)
    proj_own, proj_other = project(part, activations, act_other, w3, early, block)
    proj_back = core_swap(proj_other)
    is_mine = (masks[0] > 0)[None]
    heads = jnp.where(is_mine, proj_own, proj_back)

    parts = [None] * RING
    others = [None] * RING
    for hop in (2, 1, 3, 0):
        x = head_part(heads, hop)
        parts[hop] = lax.ppermute(x, "seq", to_heads(hop)) if hop else x
        others[hop] = core_swap(parts[hop])
    own, oth = attention(where, parts, others, g_parts)
    from_other = core_swap(oth)

    grads = [None] * RING
    other_grads = [None] * RING
    for hop in (2, 1, 3, 0):
        kv = own[hop, :, HD:] + from_other[hop].astype(jnp.float32)
        x = jnp.concatenate([own[hop, :, :HD], kv], axis=1).astype(jnp.bfloat16)
        if hop:
            x = lax.ppermute(x, "seq", [(i, (i - hop) % RING) for i in range(NH)])
        grads[hop] = x
        other_grads[hop] = core_swap(x)

    dest = jnp.arange(RING * RING, dtype=jnp.int32)
    dy = (dest // RING - tp // RING + RING) % RING
    dz = (dest % RING - tp % RING + RING) % RING
    z_first = dz * RING + dy
    y_first = dy * RING + dz
    place = jnp.stack(
        [
            jnp.where(core == 0, z_first, y_first),
            jnp.where(core == 0, y_first, z_first),
            jnp.full_like(dest, chip),
        ]
    ).astype(jnp.int32)

    streams = 2
    quarter = RING
    seconds = []
    for stream in range(streams):
        own_rows, other_rows = back(place, masks, grads, other_grads, w3, stream, streams)
        returned = core_swap(other_rows)

        def piece(k):
            cut = slice(k * quarter, (k + 1) * quarter)
            return own_rows[cut].astype(jnp.float32) + returned[cut].astype(jnp.float32)

        total = piece(0)
        for hop in (2, 1, 3):
            got = lax.ppermute(piece(hop).astype(jnp.bfloat16), AXES, ring_perm(True, hop))
            total = total + got.astype(jnp.float32)
        seconds.append(total)
    total = jnp.concatenate(seconds, axis=2) if streams > 1 else seconds[0]
    result = total[0]
    for hop in (2, 1, 3):
        got = lax.ppermute(total[hop].astype(jnp.bfloat16), AXES, ring_perm(False, hop))
        result = result + got.astype(jnp.float32)
    return result.astype(jnp.bfloat16)


def solution(mesh):
    in_specs = (P(("seq", "mod"), None), P(("seq", "mod"), "tp"), P("mod", None, None, "tp"), P())
    out_specs = P(("seq", "mod"), "tp")
    return jax.shard_map(
        per_device, mesh=mesh, in_specs=in_specs, out_specs=out_specs, check_vma=False
    )
```

```python
import functools

import jax
import jax.numpy as jnp
from jax import lax
from jax.experimental import pallas as pl
from jax.experimental.pallas import tpu as pltpu
from jax.sharding import PartitionSpec as P

HD = 128
NH = 3
RING = 4
SCALE = HD**-0.5
AXES = ("seq", "mod", "tp")
MIB = 1024 * 1024


def core_swap(x):
    return lax.ppermute(x, "mod", [(0, 1), (1, 0)])


def own_kernel(early, a_ref, w_hbm, part_ref, w_ref, sem):
    chunks = w_ref.shape[1] // 2
    block = 2 * 2 * w_ref.shape[3]

    def fetch(i):
        return pltpu.make_async_copy(w_hbm.at[:, 2 * i : 2 * i + 2], w_ref.at[:, 2 * i : 2 * i + 2], sem.at[i])

    for i in range(chunks):
        fetch(i).start()
    for i in range(chunks):
        fetch(i).wait()
        if i < early:
            part = jnp.dot(
                a_ref[:, i * block : (i + 1) * block], weight_block(w_ref, i), preferred_element_type=jnp.float32
            )
            if i == 0:
                part_ref[...] = part
            else:
                part_ref[...] += part


def weight_block(w_ref, i):
    size = 4 * w_ref.shape[3]
    return jnp.concatenate([w_ref[c, 2 * i : 2 * i + 2].reshape(size, NH * HD) for c in range(3)], axis=1)


def project_own(a, w5, early):
    rows = a.shape[0]
    vmem = pl.BlockSpec(memory_space=pltpu.VMEM)
    anywhere = pl.BlockSpec(memory_space=pl.ANY)
    return pl.pallas_call(
        functools.partial(own_kernel, early),
        in_specs=[vmem, anywhere],
        out_specs=[vmem, vmem],
        out_shape=[
            jax.ShapeDtypeStruct((rows, 9 * HD), jnp.float32),
            pltpu.VMEM(w5.shape, jnp.bfloat16),
        ],
        scratch_shapes=[pltpu.SemaphoreType.DMA((w5.shape[1] // 2,))],
        compiler_params=pltpu.CompilerParams(vmem_limit_bytes=44 * MIB),
        cost_estimate=pl.CostEstimate(flops=4 * 10**9, bytes_accessed=2 * 10**7, transcendentals=0),
        name="project_own",
    )(a, w5)


def project_kernel(early, where_ref, part_ref, own_hbm, oth_hbm, w_ref, own_out, oth_out, half_hbm, a_s, acc_ref, sem, half_sem):
    rows = part_ref.shape[0]
    chunks = w_ref.shape[1] // 2
    block = 2 * 2 * w_ref.shape[3]

    def fetch(i):
        cut = pl.ds(i * block, block)
        return pltpu.make_async_copy(oth_hbm.at[:, cut], a_s.at[i, rows : 2 * rows], sem.at[1, i])

    def fetch_own(i):
        cut = pl.ds(i * block, block)
        return pltpu.make_async_copy(own_hbm.at[:, cut], a_s.at[i, 0:rows], sem.at[0, i])

    half = pltpu.make_async_copy(w_ref.at[:, :, 1 - where_ref[1]], half_hbm, half_sem)
    for i in range(chunks):
        fetch(i).start()
        if i >= early:
            fetch_own(i).start()
    half.start()
    acc_ref[0:rows] = part_ref[...]
    for i in range(chunks):
        fetch(i).wait()
        w = weight_block(w_ref, i)
        if i < early:
            part = jnp.dot(a_s[i, rows:], w, preferred_element_type=jnp.float32)
            if i == 0:
                acc_ref[rows:] = part
            else:
                acc_ref[rows:] += part
        else:
            fetch_own(i).wait()
            acc_ref[...] += jnp.dot(a_s[i], w, preferred_element_type=jnp.float32)
    for h in range(NH):
        for c in range(3):
            lo = c * NH * HD + h * HD
            x = acc_ref[:, lo : lo + HD].astype(jnp.bfloat16)
            own_out[h, :, c * HD : (c + 1) * HD] = x[0:rows]
            oth_out[h, :, c * HD : (c + 1) * HD] = x[rows:]
    half.wait()


def project(where, part, own, other, w5, early):
    rows, depth = own.shape
    chunks = w5.shape[1] // 2
    shape = jax.ShapeDtypeStruct((NH, rows, 3 * HD), jnp.bfloat16)
    vmem = pl.BlockSpec(memory_space=pltpu.VMEM)
    anywhere = pl.BlockSpec(memory_space=pl.ANY)
    return pl.pallas_call(
        functools.partial(project_kernel, early),
        in_specs=[pl.BlockSpec(memory_space=pltpu.SMEM), vmem, anywhere, anywhere, vmem],
        out_specs=[vmem, vmem, anywhere],
        out_shape=[shape, shape, jax.ShapeDtypeStruct((3,) + w5.shape[1:2] + w5.shape[3:], jnp.bfloat16)],
        scratch_shapes=[
            pltpu.VMEM((chunks, 2 * rows, depth // chunks), jnp.bfloat16),
            pltpu.VMEM((2 * rows, 9 * HD), jnp.float32),
            pltpu.SemaphoreType.DMA((2, chunks)),
            pltpu.SemaphoreType.DMA,
        ],
        compiler_params=pltpu.CompilerParams(vmem_limit_bytes=44 * MIB),
        cost_estimate=pl.CostEstimate(flops=7 * 10**9, bytes_accessed=10**7, transcendentals=0),
        name="project",
    )(where, part, own, other, w5)


def attention_kernel(
    where_ref, a0, a1, a2, a3, b0, b1, b2, b3, own_ref, oth_ref, q_s, g_s, k_s, v_s, dk_s, dv_s
):
    chip = where_ref[0]
    core = where_ref[1]
    rows = a0.shape[0]
    both = 2 * rows
    own = (a0, a1, a2, a3)
    oth = (b0, b1, b2, b3)
    for k, (r, o) in enumerate(zip(own, oth)):
        shard = (chip - k + RING) % RING
        q_s[shard] = r[:, 0:HD]
        g_s[shard] = r[:, 3 * HD : 4 * HD]
        mine = pl.ds(pl.multiple_of((2 * shard + core) * rows, rows), rows)
        other = pl.ds(pl.multiple_of((2 * shard + 1 - core) * rows, rows), rows)
        k_s[mine, :] = r[:, HD : 2 * HD]
        v_s[mine, :] = r[:, 2 * HD : 3 * HD]
        k_s[other, :] = o[:, HD : 2 * HD]
        v_s[other, :] = o[:, 2 * HD : 3 * HD]
    nt = (((1,), (1,)), ((), ()))
    tn = (((0,), (0,)), ((), ()))
    for s in range(RING - 1, -1, -1):
        width = both * (s + 1)
        q = q_s[s]
        g = g_s[s]
        kk = k_s[0:width, :]
        vv = v_s[0:width, :]
        scores = lax.dot_general(q, kk, nt, preferred_element_type=jnp.float32) * SCALE
        row = lax.broadcasted_iota(jnp.int32, (rows, width), 0) + (2 * s + core) * rows
        col = lax.broadcasted_iota(jnp.int32, (rows, width), 1)
        scores = jnp.where(col <= row, scores, -jnp.inf)
        lifted = jnp.exp(scores - jnp.max(scores, axis=1, keepdims=True))
        probs = lifted / jnp.sum(lifted, axis=1, keepdims=True)
        low = probs.astype(jnp.bfloat16)
        dprobs = lax.dot_general(g, vv, nt, preferred_element_type=jnp.float32)
        row_dot = jnp.sum(probs * dprobs, axis=1, keepdims=True)
        ds = (probs * (dprobs - row_dot)).astype(jnp.bfloat16)
        dq = jnp.dot(ds, kk, preferred_element_type=jnp.float32) * SCALE
        dk = lax.dot_general(ds, q, tn, preferred_element_type=jnp.float32) * SCALE
        dv = lax.dot_general(low, g, tn, preferred_element_type=jnp.float32)
        if s == RING - 1:
            dk_s[...] = dk
            dv_s[...] = dv
        else:
            dk_s[0:width, :] += dk
            dv_s[0:width, :] += dv
        own_ref[(chip - s + RING) % RING, :, 0:HD] = dq
    for k in range(RING):
        shard = (chip - k + RING) % RING
        mine = pl.ds(pl.multiple_of((2 * shard + core) * rows, rows), rows)
        other = pl.ds(pl.multiple_of((2 * shard + 1 - core) * rows, rows), rows)
        own_ref[k, :, HD : 2 * HD] = dk_s[mine, :]
        own_ref[k, :, 2 * HD : 3 * HD] = dv_s[mine, :]
        oth_ref[k, :, 0:HD] = dk_s[other, :].astype(jnp.bfloat16)
        oth_ref[k, :, HD : 2 * HD] = dv_s[other, :].astype(jnp.bfloat16)


def attention(where, parts, others):
    rows = parts[0].shape[0]
    total = 2 * RING * rows
    vmem = pl.BlockSpec(memory_space=pltpu.VMEM)
    return pl.pallas_call(
        attention_kernel,
        in_specs=[pl.BlockSpec(memory_space=pltpu.SMEM)] + [vmem] * 8,
        out_specs=[vmem, vmem],
        out_shape=[
            jax.ShapeDtypeStruct((RING, rows, 3 * HD), jnp.float32),
            jax.ShapeDtypeStruct((RING, rows, 2 * HD), jnp.bfloat16),
        ],
        scratch_shapes=[
            pltpu.VMEM((RING, rows, HD), jnp.bfloat16),
            pltpu.VMEM((RING, rows, HD), jnp.bfloat16),
            pltpu.VMEM((total, HD), jnp.bfloat16),
            pltpu.VMEM((total, HD), jnp.bfloat16),
            pltpu.VMEM((total, HD), jnp.float32),
            pltpu.VMEM((total, HD), jnp.float32),
        ],
        compiler_params=pltpu.CompilerParams(vmem_limit_bytes=32 * MIB),
        cost_estimate=pl.CostEstimate(flops=10**9, bytes_accessed=4 * 10**6, transcendentals=10**6),
        name="attention",
    )(where, *parts, *others)


def gather(chip, mask_ref, own, oth, out_ref):
    rows = own[0].shape[0]
    for k in range(RING):
        head = (chip + k) % RING

        @pl.when(head < NH)
        def _():
            for block, x_ref in enumerate((own[k], oth[k])):
                x = x_ref[...]
                zero = jnp.zeros_like(x)
                for side in range(2):
                    kept = jnp.where(mask_ref[block] == 1 - side, x, zero)
                    for c in range(3):
                        lo = pl.multiple_of(((side * 3 + c) * NH + head) * HD, HD)
                        out_ref[block * rows : (block + 1) * rows, pl.ds(lo, HD)] = kept[:, c * HD : (c + 1) * HD]


def back_kernel(hop, first, place_ref, *refs):
    if first:
        mask_ref, *parts, own_hbm, other_hbm, out_ref, token_ref, g_ref, w_s, sem = refs
    else:
        _, g_ref, own_hbm, other_hbm, out_ref, token_ref, w_s, sem = refs
    core = place_ref[RING * RING]
    chip = place_ref[RING * RING + 1]
    cols = w_s.shape[3]

    def fetch(side, j):
        dest = place_ref[hop * RING + j]
        src = other_hbm.at[:, dest] if side else own_hbm.at[:, dest, core]
        return pltpu.make_async_copy(src, w_s.at[side, j], sem.at[side, j])

    for j in range(RING):
        for side in range(2):
            fetch(side, j).start()
    token_ref[...] = jnp.zeros_like(token_ref)
    if first:
        gather(chip, mask_ref, parts[:RING], parts[RING:], g_ref)
    pair = 2
    for j in range(0, RING, pair):
        for side in range(2):
            for i in range(pair):
                fetch(side, j + i).wait()
        w = [w_s[side, j : j + pair, c].reshape(pair * cols, NH * HD) for side in range(2) for c in range(3)]
        res = lax.dot_general(
            g_ref[...], jnp.concatenate(w, axis=1), (((1,), (1,)), ((), ())), preferred_element_type=jnp.float32
        ).astype(jnp.bfloat16)
        for i in range(pair):
            out_ref[j + i] = res[:, i * cols : (i + 1) * cols]


def back(place, w5, other_half, hop, token=None, grads=None, gather_from=None):
    cols = w5.shape[3]
    vmem = pl.BlockSpec(memory_space=pltpu.VMEM)
    anywhere = pl.BlockSpec(memory_space=pl.ANY)
    first = grads is None
    if first:
        masks, own, oth = gather_from
        rows = 2 * own[0].shape[0]
        extra = [masks, *own, *oth]
        extra_specs = [vmem] * 9
    else:
        rows = grads.shape[0]
        extra = [token, grads]
        extra_specs = [anywhere, vmem]
    out_shape = [
        jax.ShapeDtypeStruct((RING, rows, cols), jnp.bfloat16),
        jax.ShapeDtypeStruct((8, HD), jnp.float32),
    ]
    if first:
        out_shape.append(pltpu.VMEM((rows, 18 * HD), jnp.bfloat16))
    return pl.pallas_call(
        functools.partial(back_kernel, hop, first),
        in_specs=[pl.BlockSpec(memory_space=pltpu.SMEM)] + extra_specs + [anywhere, anywhere],
        out_specs=[vmem] * len(out_shape),
        out_shape=out_shape,
        scratch_shapes=[
            pltpu.VMEM((2, RING, 3, cols, NH * HD), jnp.bfloat16),
            pltpu.SemaphoreType.DMA((2, RING)),
        ],
        compiler_params=pltpu.CompilerParams(vmem_limit_bytes=50 * MIB),
        cost_estimate=pl.CostEstimate(flops=10**6, bytes_accessed=10**4, transcendentals=0),
        name="back",
    )(place, *extra, w5, other_half)


def ring_perm(first, hop):
    pairs = []
    for s in range(RING):
        for m in range(2):
            for y in range(RING):
                for z in range(RING):
                    if (m == 0) == first:
                        to = (y, (z + hop) % RING)
                    else:
                        to = ((y + hop) % RING, z)
                    base = (s * 2 + m) * RING * RING
                    pairs.append((base + y * RING + z, base + to[0] * RING + to[1]))
    return pairs


def per_device(activations, grad_attn, weights, modality):
    rows, depth = activations.shape
    chip = lax.axis_index("seq")
    core = lax.axis_index("mod")
    tp = lax.axis_index("tp")
    where = jnp.stack([chip, core]).astype(jnp.int32)
    dests = RING * RING
    cols = depth // dests // 2
    w5 = jnp.transpose(weights[0], (1, 0, 2)).reshape(3, dests, 2, cols, NH * HD)

    own_mod = lax.dynamic_slice_in_dim(modality, (2 * chip + core) * rows, rows)
    other_mod = lax.dynamic_slice_in_dim(modality, (2 * chip + 1 - core) * rows, rows)
    masks = (jnp.stack([own_mod, other_mod]) == core).astype(jnp.int32)[:, :, None]

    act_other = core_swap(activations)
    early = 5
    part, w_vmem = project_own(activations, w5, early)
    w_vmem = pltpu.with_memory_space_constraint(w_vmem, pltpu.VMEM)
    proj_own, proj_other, half = project(where, part, activations, act_other, w_vmem, early)
    proj_back = core_swap(proj_other)
    other_half = core_swap(half)
    g_heads = grad_attn.reshape(rows, NH, HD).transpose(1, 0, 2)
    heads = jnp.concatenate([jnp.where((masks[0] > 0)[None], proj_own, proj_back), g_heads], axis=2)

    parts = [None] * RING
    others = [None] * RING
    for hop in (2, 1, 3, 0):
        head = jnp.minimum((chip + hop) % RING, NH - 1)
        x = lax.dynamic_index_in_dim(heads, head, 0, keepdims=False)
        if hop:
            x = lax.ppermute(x, "seq", [(i, (i + hop) % RING) for i in range(RING) if (i + hop) % RING < NH])
        parts[hop] = x
        others[hop] = core_swap(x)
    own, oth = attention(where, parts, others)
    from_other = core_swap(oth)

    grads = [None] * RING
    other_grads = [None] * RING
    for hop in (2, 1, 3, 0):
        kv = own[hop, :, HD:] + from_other[hop].astype(jnp.float32)
        x = jnp.concatenate([own[hop, :, :HD], kv], axis=1).astype(jnp.bfloat16)
        if hop:
            x = lax.ppermute(x, "seq", [(i, (i - hop) % RING) for i in range(NH)])
        grads[hop] = x
        other_grads[hop] = core_swap(x)
    i = jnp.arange(dests, dtype=jnp.int32) // RING
    j = jnp.arange(dests, dtype=jnp.int32) % RING
    y, z = tp // RING, tp % RING
    place = jnp.where(
        core == 0,
        (y + j) % RING * RING + (z + i) % RING,
        (y + i) % RING * RING + (z + j) % RING,
    )
    place = jnp.concatenate([place, jnp.stack([core, chip])]).astype(jnp.int32)

    pieces = {}
    token = g = None
    for hop in (2, 1, 3, 0):
        if g is None:
            x, token, g = back(place, w5, other_half, hop, gather_from=(masks, grads, other_grads))
            g = pltpu.with_memory_space_constraint(g, pltpu.VMEM)
        else:
            x, token = back(place, w5, other_half, hop, token, g)
        pieces[hop] = lax.ppermute(x, AXES, ring_perm(True, hop)) if hop else x
    total = pieces[0].astype(jnp.float32)
    for hop in (2, 1, 3):
        total = lax.optimization_barrier(total) + pieces[hop].astype(jnp.float32)
    result = total[0]
    for hop in (2, 1, 3):
        got = lax.ppermute(total[hop].astype(jnp.bfloat16), AXES, ring_perm(False, hop))
        result = result + got.astype(jnp.float32)
    result = result.astype(jnp.bfloat16)
    mine = result[:rows]
    theirs = core_swap(result[rows:])
    return jnp.where(
        core == 0, jnp.concatenate([mine, theirs], axis=1), jnp.concatenate([theirs, mine], axis=1)
    )


def solution(mesh):
    in_specs = (P(("seq", "mod"), None), P(("seq", "mod"), "tp"), P("mod", None, None, "tp"), P())
    out_specs = P(("seq", "mod"), "tp")
    return jax.shard_map(
        per_device, mesh=mesh, in_specs=in_specs, out_specs=out_specs, check_vma=False
    )
```

```python
import functools

import jax
import jax.numpy as jnp
from jax import lax
from jax.experimental import pallas as pl
from jax.experimental.pallas import tpu as pltpu
from jax.sharding import PartitionSpec as P

HD = 128
NH = 3
RING = 4
SCALE = HD**-0.5
AXES = ("seq", "mod", "tp")
MIB = 1024 * 1024


def core_swap(x):
    return lax.ppermute(x, "mod", [(0, 1), (1, 0)])


def weight_block(w_ref, i):
    size = 4 * w_ref.shape[3]
    return jnp.concatenate([w_ref[c, 2 * i : 2 * i + 2].reshape(size, NH * HD) for c in range(3)], axis=1)


def own_kernel(a_hbm, w_hbm, part_ref, w_ref, a_s, a_sem, w_sem):
    chunks = w_ref.shape[1] // 2
    block = 4 * w_ref.shape[3]

    def fetch(i):
        pair = slice(2 * i, 2 * i + 2)
        return (
            pltpu.make_async_copy(a_hbm.at[:, pl.ds(i * block, block)], a_s.at[i], a_sem.at[i]),
            pltpu.make_async_copy(w_hbm.at[:, pair], w_ref.at[:, pair], w_sem.at[i]),
        )

    for i in range(chunks):
        for copy in fetch(i):
            copy.start()
    for i in range(chunks):
        for copy in fetch(i):
            copy.wait()
        part = jnp.dot(a_s[i], weight_block(w_ref, i), preferred_element_type=jnp.float32)
        if i == 0:
            part_ref[...] = part
        else:
            part_ref[...] += part


def project_own(a, w5, early):
    rows = a.shape[0]
    block = 4 * w5.shape[3]
    vmem = pl.BlockSpec(memory_space=pltpu.VMEM)
    hbm = pl.BlockSpec(memory_space=pltpu.HBM)
    return pl.pallas_call(
        own_kernel,
        in_specs=[hbm, hbm],
        out_specs=[vmem, vmem],
        out_shape=[
            jax.ShapeDtypeStruct((rows, 9 * HD), jnp.float32),
            pltpu.VMEM((3, 2 * early) + w5.shape[2:], jnp.bfloat16),
        ],
        scratch_shapes=[
            pltpu.VMEM((early, rows, block), jnp.bfloat16),
            pltpu.SemaphoreType.DMA((early,)),
            pltpu.SemaphoreType.DMA((early,)),
        ],
        compiler_params=pltpu.CompilerParams(vmem_limit_bytes=20 * MIB),
        cost_estimate=pl.CostEstimate(flops=4 * 10**9, bytes_accessed=10**7, transcendentals=0),
        name="project_own",
    )(a, w5)


def project_kernel(
    early, where_ref, part_ref, own_hbm, oth_ref, w_ref, w_hbm, own_out, oth_out, half_hbm, a_s, w_s, acc_ref,
    own_sem, w_sem, half_sem
):
    rows = part_ref.shape[0]
    chunks = half_hbm.shape[1] // 2
    block = 4 * w_ref.shape[3]
    side = 1 - where_ref[1]

    def fetch_own(i):
        return pltpu.make_async_copy(own_hbm.at[:, pl.ds(i * block, block)], a_s.at[i - early], own_sem.at[i])

    def other(i):
        return oth_ref[:, i * block : (i + 1) * block]

    def fetch_weights(i):
        src = w_hbm.at[:, 2 * i : 2 * i + 2]
        return pltpu.make_async_copy(src, w_s.at[:, 2 * (i - early) : 2 * (i - early) + 2], w_sem.at[i])

    def put_half(i):
        if i < early:
            src = w_ref.at[:, 2 * i : 2 * i + 2, side]
        else:
            src = w_s.at[:, 2 * (i - early) : 2 * (i - early) + 2, side]
        return pltpu.make_async_copy(src, half_hbm.at[:, 2 * i : 2 * i + 2], half_sem.at[i])

    for i in range(early, chunks):
        fetch_weights(i).start()
        fetch_own(i).start()
    for i in range(early):
        put_half(i).start()
    acc_ref[0:rows] = part_ref[...]
    for i in range(chunks):
        if i < early:
            part = jnp.dot(other(i), weight_block(w_ref, i), preferred_element_type=jnp.float32)
            if i == 0:
                acc_ref[rows:] = part
            else:
                acc_ref[rows:] += part
        else:
            fetch_own(i).wait()
            fetch_weights(i).wait()
            put_half(i).start()
            a = jnp.concatenate([a_s[i - early], other(i)], axis=0)
            acc_ref[...] += jnp.dot(a, weight_block(w_s, i - early), preferred_element_type=jnp.float32)
    for h in range(NH):
        for c in range(3):
            lo = c * NH * HD + h * HD
            x = acc_ref[:, lo : lo + HD].astype(jnp.bfloat16)
            own_out[h, :, c * HD : (c + 1) * HD] = x[0:rows]
            oth_out[h, :, c * HD : (c + 1) * HD] = x[rows:]
    for i in range(chunks):
        put_half(i).wait()


def project(where, part, own, other, w_early, w5):
    rows, depth = own.shape
    chunks = w5.shape[1] // 2
    early = w_early.shape[1] // 2
    shape = jax.ShapeDtypeStruct((NH, rows, 3 * HD), jnp.bfloat16)
    vmem = pl.BlockSpec(memory_space=pltpu.VMEM)
    hbm = pl.BlockSpec(memory_space=pltpu.HBM)
    dma = pltpu.SemaphoreType.DMA((chunks,))
    return pl.pallas_call(
        functools.partial(project_kernel, early),
        in_specs=[pl.BlockSpec(memory_space=pltpu.SMEM), vmem, hbm, vmem, vmem, hbm],
        out_specs=[vmem, vmem, hbm],
        out_shape=[shape, shape, pltpu.HBM((3,) + w5.shape[1:2] + w5.shape[3:], jnp.bfloat16)],
        scratch_shapes=[
            pltpu.VMEM((chunks - early, rows, depth // chunks), jnp.bfloat16),
            pltpu.VMEM((3, 2 * (chunks - early)) + w5.shape[2:], jnp.bfloat16),
            pltpu.VMEM((2 * rows, 9 * HD), jnp.float32),
            dma,
            dma,
            dma,
        ],
        compiler_params=pltpu.CompilerParams(vmem_limit_bytes=26 * MIB),
        cost_estimate=pl.CostEstimate(flops=7 * 10**9, bytes_accessed=10**7, transcendentals=0),
        name="project",
    )(where, part, own, other, w_early, w5)


def attention_kernel(
    where_ref, a0, a1, a2, a3, b0, b1, b2, b3, own_ref, oth_ref, q_s, g_s, k_s, v_s, dk_s, dv_s
):
    chip = where_ref[0]
    core = where_ref[1]
    rows = a0.shape[0]
    both = 2 * rows
    own = (a0, a1, a2, a3)
    oth = (b0, b1, b2, b3)
    for k, (r, o) in enumerate(zip(own, oth)):
        shard = (chip - k + RING) % RING
        q_s[shard] = r[:, 0:HD]
        g_s[shard] = r[:, 3 * HD : 4 * HD]
        mine = pl.ds(pl.multiple_of((2 * shard + core) * rows, rows), rows)
        other = pl.ds(pl.multiple_of((2 * shard + 1 - core) * rows, rows), rows)
        k_s[mine, :] = r[:, HD : 2 * HD]
        v_s[mine, :] = r[:, 2 * HD : 3 * HD]
        k_s[other, :] = o[:, HD : 2 * HD]
        v_s[other, :] = o[:, 2 * HD : 3 * HD]
    nt = (((1,), (1,)), ((), ()))
    tn = (((0,), (0,)), ((), ()))
    for s in range(RING - 1, -1, -1):
        width = both * (s + 1)
        q = q_s[s]
        g = g_s[s]
        kk = k_s[0:width, :]
        vv = v_s[0:width, :]
        scores = lax.dot_general(q, kk, nt, preferred_element_type=jnp.float32) * SCALE
        row = lax.broadcasted_iota(jnp.int32, (rows, width), 0) + (2 * s + core) * rows
        col = lax.broadcasted_iota(jnp.int32, (rows, width), 1)
        scores = jnp.where(col <= row, scores, -jnp.inf)
        lifted = jnp.exp(scores - jnp.max(scores, axis=1, keepdims=True))
        probs = lifted / jnp.sum(lifted, axis=1, keepdims=True)
        low = probs.astype(jnp.bfloat16)
        dprobs = lax.dot_general(g, vv, nt, preferred_element_type=jnp.float32)
        row_dot = jnp.sum(probs * dprobs, axis=1, keepdims=True)
        ds = (probs * (dprobs - row_dot)).astype(jnp.bfloat16)
        dq = jnp.dot(ds, kk, preferred_element_type=jnp.float32) * SCALE
        dk = lax.dot_general(ds, q, tn, preferred_element_type=jnp.float32) * SCALE
        dv = lax.dot_general(low, g, tn, preferred_element_type=jnp.float32)
        if s == RING - 1:
            dk_s[...] = dk
            dv_s[...] = dv
        else:
            dk_s[0:width, :] += dk
            dv_s[0:width, :] += dv
        own_ref[(chip - s + RING) % RING, :, 0:HD] = dq
    for k in range(RING):
        shard = (chip - k + RING) % RING
        mine = pl.ds(pl.multiple_of((2 * shard + core) * rows, rows), rows)
        other = pl.ds(pl.multiple_of((2 * shard + 1 - core) * rows, rows), rows)
        own_ref[k, :, HD : 2 * HD] = dk_s[mine, :]
        own_ref[k, :, 2 * HD : 3 * HD] = dv_s[mine, :]
        oth_ref[k, :, 0:HD] = dk_s[other, :].astype(jnp.bfloat16)
        oth_ref[k, :, HD : 2 * HD] = dv_s[other, :].astype(jnp.bfloat16)


def attention(where, parts, others):
    rows = parts[0].shape[0]
    total = 2 * RING * rows
    vmem = pl.BlockSpec(memory_space=pltpu.VMEM)
    return pl.pallas_call(
        attention_kernel,
        in_specs=[pl.BlockSpec(memory_space=pltpu.SMEM)] + [vmem] * 8,
        out_specs=[vmem, vmem],
        out_shape=[
            jax.ShapeDtypeStruct((RING, rows, 3 * HD), jnp.float32),
            jax.ShapeDtypeStruct((RING, rows, 2 * HD), jnp.bfloat16),
        ],
        scratch_shapes=[
            pltpu.VMEM((RING, rows, HD), jnp.bfloat16),
            pltpu.VMEM((RING, rows, HD), jnp.bfloat16),
            pltpu.VMEM((total, HD), jnp.bfloat16),
            pltpu.VMEM((total, HD), jnp.bfloat16),
            pltpu.VMEM((total, HD), jnp.float32),
            pltpu.VMEM((total, HD), jnp.float32),
        ],
        compiler_params=pltpu.CompilerParams(vmem_limit_bytes=32 * MIB),
        cost_estimate=pl.CostEstimate(flops=10**9, bytes_accessed=4 * 10**6, transcendentals=10**6),
        name="attention",
    )(where, *parts, *others)


def gather(chip, mask_ref, own, oth, out_ref):
    rows = own[0].shape[0]
    for k in range(RING):
        head = (chip + k) % RING

        @pl.when(head < NH)
        def _():
            for block, x_ref in enumerate((own[k], oth[k])):
                x = x_ref[...]
                zero = jnp.zeros_like(x)
                for side in range(2):
                    kept = jnp.where(mask_ref[block] == 1 - side, x, zero)
                    for c in range(3):
                        lo = pl.multiple_of(((side * 3 + c) * NH + head) * HD, HD)
                        out_ref[block * rows : (block + 1) * rows, pl.ds(lo, HD)] = kept[:, c * HD : (c + 1) * HD]


def weight_copies(place_ref, own_hbm, other_hbm, to_ref, sem, hop):
    core = place_ref[RING * RING]
    copies = []
    for j in range(RING):
        dest = place_ref[hop * RING + j]
        copies.append(pltpu.make_async_copy(own_hbm.at[:, dest, core], to_ref.at[0, :, j], sem.at[0, j]))
        copies.append(pltpu.make_async_copy(other_hbm.at[:, dest], to_ref.at[1, :, j], sem.at[1, j]))
    return copies


def fetch_kernel(hop, place_ref, after_ref, own_hbm, other_hbm, w_out, sem):
    for copy in weight_copies(place_ref, own_hbm, other_hbm, w_out, sem, hop):
        copy.start()
    for copy in weight_copies(place_ref, own_hbm, other_hbm, w_out, sem, hop):
        copy.wait()


def fetch_weights(place, after, w5, other_half, hop):
    vmem = pl.BlockSpec(memory_space=pltpu.VMEM)
    hbm = pl.BlockSpec(memory_space=pltpu.HBM)
    anywhere = pl.BlockSpec(memory_space=pl.ANY)
    return pl.pallas_call(
        functools.partial(fetch_kernel, hop),
        in_specs=[pl.BlockSpec(memory_space=pltpu.SMEM), vmem, hbm, anywhere],
        out_specs=vmem,
        out_shape=pltpu.VMEM((2, 3, RING) + w5.shape[3:], jnp.bfloat16),
        scratch_shapes=[pltpu.SemaphoreType.DMA((2, RING))],
        compiler_params=pltpu.CompilerParams(vmem_limit_bytes=20 * MIB),
        cost_estimate=pl.CostEstimate(flops=10**6, bytes_accessed=5 * 10**6, transcendentals=0),
        name="fetch_weights",
    )(place, after, w5, other_half)


def back_kernel(first, following, place_ref, *refs):
    if first:
        mask_ref, *parts, w_ref, own_hbm, other_hbm, out_ref, g_ref, w_out, sem = refs
    elif following is None:
        g_ref, w_ref, own_hbm, other_hbm, out_ref = refs
    else:
        g_ref, w_ref, own_hbm, other_hbm, out_ref, w_out, sem = refs
    chip = place_ref[RING * RING + 1]
    cols = w_ref.shape[3]
    if following is not None:
        for copy in weight_copies(place_ref, own_hbm, other_hbm, w_out, sem, following):
            copy.start()
    if first:
        gather(chip, mask_ref, parts[:RING], parts[RING:], g_ref)
    w = [w_ref[side, c].reshape(RING * cols, NH * HD) for side in range(2) for c in range(3)]
    res = lax.dot_general(
        g_ref[...], jnp.concatenate(w, axis=1), (((1,), (1,)), ((), ())), preferred_element_type=jnp.float32
    ).astype(jnp.bfloat16)
    for j in range(RING):
        out_ref[j] = res[:, j * cols : (j + 1) * cols]
    if following is not None:
        for copy in weight_copies(place_ref, own_hbm, other_hbm, w_out, sem, following):
            copy.wait()


def back(place, w_here, w5, other_half, following, grads=None, gather_from=None):
    cols = w5.shape[3]
    vmem = pl.BlockSpec(memory_space=pltpu.VMEM)
    hbm = pl.BlockSpec(memory_space=pltpu.HBM)
    anywhere = pl.BlockSpec(memory_space=pl.ANY)
    first = grads is None
    if first:
        masks, own, oth = gather_from
        rows = 2 * own[0].shape[0]
        extra = [masks, *own, *oth]
    else:
        rows = grads.shape[0]
        extra = [grads]
    out_shape = [jax.ShapeDtypeStruct((RING, rows, cols), jnp.bfloat16)]
    scratch = []
    if first:
        out_shape.append(pltpu.VMEM((rows, 18 * HD), jnp.bfloat16))
    if following is not None:
        out_shape.append(pltpu.VMEM(w_here.shape, jnp.bfloat16))
        scratch.append(pltpu.SemaphoreType.DMA((2, RING)))
    out = pl.pallas_call(
        functools.partial(back_kernel, first, following),
        in_specs=[pl.BlockSpec(memory_space=pltpu.SMEM)] + [vmem] * (len(extra) + 1) + [hbm, anywhere],
        out_specs=[vmem] * len(out_shape),
        out_shape=out_shape,
        scratch_shapes=scratch,
        compiler_params=pltpu.CompilerParams(vmem_limit_bytes=24 * MIB),
        cost_estimate=pl.CostEstimate(flops=10**6, bytes_accessed=10**4, transcendentals=0),
        name="back",
    )(place, *extra, w_here, w5, other_half)
    return [out[0]] + [pltpu.with_memory_space_constraint(x, pltpu.VMEM) for x in out[1:]]


def ring_perm(first, hop):
    pairs = []
    for s in range(RING):
        for m in range(2):
            for y in range(RING):
                for z in range(RING):
                    if (m == 0) == first:
                        to = (y, (z + hop) % RING)
                    else:
                        to = ((y + hop) % RING, z)
                    base = (s * 2 + m) * RING * RING
                    pairs.append((base + y * RING + z, base + to[0] * RING + to[1]))
    return pairs


def per_device(activations, grad_attn, weights, modality):
    rows, depth = activations.shape
    chip = lax.axis_index("seq")
    core = lax.axis_index("mod")
    tp = lax.axis_index("tp")
    where = jnp.stack([chip, core]).astype(jnp.int32)
    dests = RING * RING
    cols = depth // dests // 2
    w5 = jnp.transpose(weights[0], (1, 0, 2)).reshape(3, dests, 2, cols, NH * HD)

    own_mod = lax.dynamic_slice_in_dim(modality, (2 * chip + core) * rows, rows)
    other_mod = lax.dynamic_slice_in_dim(modality, (2 * chip + 1 - core) * rows, rows)
    masks = (jnp.stack([own_mod, other_mod]) == core).astype(jnp.int32)[:, :, None]

    w5 = pltpu.with_memory_space_constraint(w5, pltpu.HBM)
    activations = pltpu.with_memory_space_constraint(activations, pltpu.HBM)
    act_other = pltpu.with_memory_space_constraint(core_swap(activations), pltpu.VMEM)
    part, w_early = project_own(activations, w5, 4)
    w_early = pltpu.with_memory_space_constraint(w_early, pltpu.VMEM)
    proj_own, proj_other, half = project(where, part, activations, act_other, w_early, w5)
    proj_back = core_swap(proj_other)
    proj_back, half = lax.optimization_barrier((proj_back, half))
    other_half = core_swap(half)
    g_heads = grad_attn.reshape(rows, NH, HD).transpose(1, 0, 2)
    heads = jnp.concatenate([jnp.where((masks[0] > 0)[None], proj_own, proj_back), g_heads], axis=2)

    parts = [None] * RING
    others = [None] * RING
    for hop in (2, 1, 3, 0):
        head = jnp.minimum((chip + hop) % RING, NH - 1)
        x = lax.dynamic_index_in_dim(heads, head, 0, keepdims=False)
        if hop:
            x = lax.ppermute(x, "seq", [(i, (i + hop) % RING) for i in range(RING) if (i + hop) % RING < NH])
        parts[hop] = x
        others[hop] = core_swap(x)
    own, oth = attention(where, parts, others)
    from_other = core_swap(oth)

    grads = [None] * RING
    other_grads = [None] * RING
    for hop in (2, 1, 3, 0):
        kv = own[hop, :, HD:] + from_other[hop].astype(jnp.float32)
        x = jnp.concatenate([own[hop, :, :HD], kv], axis=1).astype(jnp.bfloat16)
        if hop:
            x = lax.ppermute(x, "seq", [(i, (i - hop) % RING) for i in range(NH)])
        grads[hop] = x
        other_grads[hop] = core_swap(x)
    i = jnp.arange(dests, dtype=jnp.int32) // RING
    j = jnp.arange(dests, dtype=jnp.int32) % RING
    y, z = tp // RING, tp % RING
    place = jnp.where(
        core == 0,
        (y + j) % RING * RING + (z + i) % RING,
        (y + i) % RING * RING + (z + j) % RING,
    )
    place = jnp.concatenate([place, jnp.stack([core, chip])]).astype(jnp.int32)

    pieces = {}
    w_here = fetch_weights(place, grads[0], w5, other_half, 2)
    w_here = pltpu.with_memory_space_constraint(w_here, pltpu.VMEM)
    x, g, w_here = back(place, w_here, w5, other_half, 1, gather_from=(masks, grads, other_grads))
    pieces[2] = lax.ppermute(x, AXES, ring_perm(True, 2))
    x, w_here = back(place, w_here, w5, other_half, 3, grads=g)
    pieces[1] = lax.ppermute(x, AXES, ring_perm(True, 1))
    x, w_here = back(place, w_here, w5, other_half, 0, grads=g)
    pieces[3] = lax.ppermute(x, AXES, ring_perm(True, 3))
    (pieces[0],) = back(place, w_here, w5, other_half, None, grads=g)
    total = pieces[0].astype(jnp.float32)
    for hop in (2, 1, 3):
        total = lax.optimization_barrier(total) + pieces[hop].astype(jnp.float32)
    result = total[0]
    for hop in (2, 1, 3):
        got = lax.ppermute(total[hop].astype(jnp.bfloat16), AXES, ring_perm(False, hop))
        result = result + got.astype(jnp.float32)
    result = result.astype(jnp.bfloat16)
    mine = result[:rows]
    theirs = core_swap(result[rows:])
    return jnp.where(
        core == 0, jnp.concatenate([mine, theirs], axis=1), jnp.concatenate([theirs, mine], axis=1)
    )


def solution(mesh):
    in_specs = (P(("seq", "mod"), None), P(("seq", "mod"), "tp"), P("mod", None, None, "tp"), P())
    out_specs = P(("seq", "mod"), "tp")
    return jax.shard_map(
        per_device, mesh=mesh, in_specs=in_specs, out_specs=out_specs, check_vma=False
    )
```

```python
import functools

import jax
import jax.numpy as jnp
from jax import lax
from jax.experimental import pallas as pl
from jax.experimental.pallas import tpu as pltpu
from jax.sharding import PartitionSpec as P

HD = 128
NH = 3
RING = 4
SCALE = HD**-0.5
AXES = ("seq", "mod", "tp")
MIB = 1024 * 1024


def core_swap(x):
    return lax.ppermute(x, "mod", [(0, 1), (1, 0)])


def weight_block(w_ref, i):
    size = 4 * w_ref.shape[3]
    return jnp.concatenate([w_ref[c, 2 * i : 2 * i + 2].reshape(size, NH * HD) for c in range(3)], axis=1)


def own_kernel(a_hbm, w_hbm, part_ref, w_ref, a_s, a_sem, w_sem):
    chunks = w_ref.shape[1] // 2
    block = 4 * w_ref.shape[3]

    def fetch(i):
        pair = slice(2 * i, 2 * i + 2)
        return (
            pltpu.make_async_copy(a_hbm.at[:, pl.ds(i * block, block)], a_s.at[i], a_sem.at[i]),
            pltpu.make_async_copy(w_hbm.at[:, pair], w_ref.at[:, pair], w_sem.at[i]),
        )

    for i in range(chunks):
        for copy in fetch(i):
            copy.start()
    for i in range(chunks):
        for copy in fetch(i):
            copy.wait()
        part = jnp.dot(a_s[i], weight_block(w_ref, i), preferred_element_type=jnp.float32)
        if i == 0:
            part_ref[...] = part
        else:
            part_ref[...] += part


def project_own(a, w5, early):
    rows = a.shape[0]
    block = 4 * w5.shape[3]
    vmem = pl.BlockSpec(memory_space=pltpu.VMEM)
    hbm = pl.BlockSpec(memory_space=pltpu.HBM)
    return pl.pallas_call(
        own_kernel,
        in_specs=[hbm, hbm],
        out_specs=[vmem, vmem],
        out_shape=[
            jax.ShapeDtypeStruct((rows, 9 * HD), jnp.float32),
            pltpu.VMEM((3, 2 * early) + w5.shape[2:], jnp.bfloat16),
        ],
        scratch_shapes=[
            pltpu.VMEM((early, rows, block), jnp.bfloat16),
            pltpu.SemaphoreType.DMA((early,)),
            pltpu.SemaphoreType.DMA((early,)),
        ],
        compiler_params=pltpu.CompilerParams(vmem_limit_bytes=20 * MIB),
        cost_estimate=pl.CostEstimate(flops=4 * 10**9, bytes_accessed=10**7, transcendentals=0),
        name="project_own",
    )(a, w5)


def project_kernel(
    early, where_ref, part_ref, own_hbm, oth_ref, w_ref, w_hbm, own_out, oth_out, half_hbm, a_s, w_s, acc_ref,
    own_sem, w_sem, half_sem
):
    rows = part_ref.shape[0]
    chunks = half_hbm.shape[1] // 2
    block = 4 * w_ref.shape[3]
    side = 1 - where_ref[1]

    def fetch_own(i):
        return pltpu.make_async_copy(own_hbm.at[:, pl.ds(i * block, block)], a_s.at[i - early], own_sem.at[i])

    def other(i):
        return oth_ref[:, i * block : (i + 1) * block]

    def fetch_weights(i):
        src = w_hbm.at[:, 2 * i : 2 * i + 2]
        return pltpu.make_async_copy(src, w_s.at[:, 2 * (i - early) : 2 * (i - early) + 2], w_sem.at[i])

    def put_half(i):
        if i < early:
            src = w_ref.at[:, 2 * i : 2 * i + 2, side]
        else:
            src = w_s.at[:, 2 * (i - early) : 2 * (i - early) + 2, side]
        return pltpu.make_async_copy(src, half_hbm.at[:, 2 * i : 2 * i + 2], half_sem.at[i])

    for i in range(early, chunks):
        fetch_weights(i).start()
        fetch_own(i).start()
    for i in range(early):
        put_half(i).start()
    acc_ref[0:rows] = part_ref[...]
    for i in range(chunks):
        if i < early:
            part = jnp.dot(other(i), weight_block(w_ref, i), preferred_element_type=jnp.float32)
            if i == 0:
                acc_ref[rows:] = part
            else:
                acc_ref[rows:] += part
        else:
            fetch_own(i).wait()
            fetch_weights(i).wait()
            put_half(i).start()
            a = jnp.concatenate([a_s[i - early], other(i)], axis=0)
            acc_ref[...] += jnp.dot(a, weight_block(w_s, i - early), preferred_element_type=jnp.float32)
    for h in range(NH):
        for c in range(3):
            lo = c * NH * HD + h * HD
            x = acc_ref[:, lo : lo + HD].astype(jnp.bfloat16)
            own_out[h, :, c * HD : (c + 1) * HD] = x[0:rows]
            oth_out[h, :, c * HD : (c + 1) * HD] = x[rows:]
    for i in range(chunks):
        put_half(i).wait()


def project(where, part, own, other, w_early, w5):
    rows, depth = own.shape
    chunks = w5.shape[1] // 2
    early = w_early.shape[1] // 2
    shape = jax.ShapeDtypeStruct((NH, rows, 3 * HD), jnp.bfloat16)
    vmem = pl.BlockSpec(memory_space=pltpu.VMEM)
    hbm = pl.BlockSpec(memory_space=pltpu.HBM)
    dma = pltpu.SemaphoreType.DMA((chunks,))
    return pl.pallas_call(
        functools.partial(project_kernel, early),
        in_specs=[pl.BlockSpec(memory_space=pltpu.SMEM), vmem, hbm, vmem, vmem, hbm],
        out_specs=[vmem, vmem, hbm],
        out_shape=[shape, shape, pltpu.HBM((3,) + w5.shape[1:2] + w5.shape[3:], jnp.bfloat16)],
        scratch_shapes=[
            pltpu.VMEM((chunks - early, rows, depth // chunks), jnp.bfloat16),
            pltpu.VMEM((3, 2 * (chunks - early)) + w5.shape[2:], jnp.bfloat16),
            pltpu.VMEM((2 * rows, 9 * HD), jnp.float32),
            dma,
            dma,
            dma,
        ],
        compiler_params=pltpu.CompilerParams(vmem_limit_bytes=26 * MIB),
        cost_estimate=pl.CostEstimate(flops=7 * 10**9, bytes_accessed=10**7, transcendentals=0),
        name="project",
    )(where, part, own, other, w_early, w5)


def attention_kernel(
    where_ref, a0, a1, a2, a3, b0, b1, b2, b3, w_hbm, own_ref, oth_ref, w_ref, q_s, g_s, k_s, v_s, dk_s, dv_s, w_sem
):
    chip = where_ref[0]
    core = where_ref[1]
    fetch = pltpu.make_async_copy(w_hbm.at[:, :, core], w_ref, w_sem)
    fetch.start()
    rows = a0.shape[0]
    both = 2 * rows
    own = (a0, a1, a2, a3)
    oth = (b0, b1, b2, b3)
    for k, (r, o) in enumerate(zip(own, oth)):
        shard = (chip - k + RING) % RING
        q_s[shard] = r[:, 0:HD]
        g_s[shard] = r[:, 3 * HD : 4 * HD]
        mine = pl.ds(pl.multiple_of((2 * shard + core) * rows, rows), rows)
        other = pl.ds(pl.multiple_of((2 * shard + 1 - core) * rows, rows), rows)
        k_s[mine, :] = r[:, HD : 2 * HD]
        v_s[mine, :] = r[:, 2 * HD : 3 * HD]
        k_s[other, :] = o[:, HD : 2 * HD]
        v_s[other, :] = o[:, 2 * HD : 3 * HD]
    nt = (((1,), (1,)), ((), ()))
    tn = (((0,), (0,)), ((), ()))
    for s in range(RING - 1, -1, -1):
        width = both * (s + 1)
        q = q_s[s]
        g = g_s[s]
        kk = k_s[0:width, :]
        vv = v_s[0:width, :]
        scores = lax.dot_general(q, kk, nt, preferred_element_type=jnp.float32) * SCALE
        row = lax.broadcasted_iota(jnp.int32, (rows, width), 0) + (2 * s + core) * rows
        col = lax.broadcasted_iota(jnp.int32, (rows, width), 1)
        scores = jnp.where(col <= row, scores, -jnp.inf)
        lifted = jnp.exp(scores - jnp.max(scores, axis=1, keepdims=True))
        probs = lifted / jnp.sum(lifted, axis=1, keepdims=True)
        low = probs.astype(jnp.bfloat16)
        dprobs = lax.dot_general(g, vv, nt, preferred_element_type=jnp.float32)
        row_dot = jnp.sum(probs * dprobs, axis=1, keepdims=True)
        ds = (probs * (dprobs - row_dot)).astype(jnp.bfloat16)
        dq = jnp.dot(ds, kk, preferred_element_type=jnp.float32) * SCALE
        dk = lax.dot_general(ds, q, tn, preferred_element_type=jnp.float32) * SCALE
        dv = lax.dot_general(low, g, tn, preferred_element_type=jnp.float32)
        if s == RING - 1:
            dk_s[...] = dk
            dv_s[...] = dv
        else:
            dk_s[0:width, :] += dk
            dv_s[0:width, :] += dv
        own_ref[(chip - s + RING) % RING, :, 0:HD] = dq
    for k in range(RING):
        shard = (chip - k + RING) % RING
        mine = pl.ds(pl.multiple_of((2 * shard + core) * rows, rows), rows)
        other = pl.ds(pl.multiple_of((2 * shard + 1 - core) * rows, rows), rows)
        own_ref[k, :, HD : 2 * HD] = dk_s[mine, :]
        own_ref[k, :, 2 * HD : 3 * HD] = dv_s[mine, :]
        oth_ref[k, :, 0:HD] = dk_s[other, :].astype(jnp.bfloat16)
        oth_ref[k, :, HD : 2 * HD] = dv_s[other, :].astype(jnp.bfloat16)
    fetch.wait()


def attention(where, parts, others, w5):
    rows = parts[0].shape[0]
    total = 2 * RING * rows
    vmem = pl.BlockSpec(memory_space=pltpu.VMEM)
    return pl.pallas_call(
        attention_kernel,
        in_specs=[pl.BlockSpec(memory_space=pltpu.SMEM)] + [vmem] * 8 + [pl.BlockSpec(memory_space=pltpu.HBM)],
        out_specs=[vmem, vmem, vmem],
        out_shape=[
            jax.ShapeDtypeStruct((RING, rows, 3 * HD), jnp.float32),
            jax.ShapeDtypeStruct((RING, rows, 2 * HD), jnp.bfloat16),
            pltpu.VMEM(w5.shape[:2] + w5.shape[3:], jnp.bfloat16),
        ],
        scratch_shapes=[
            pltpu.VMEM((RING, rows, HD), jnp.bfloat16),
            pltpu.VMEM((RING, rows, HD), jnp.bfloat16),
            pltpu.VMEM((total, HD), jnp.bfloat16),
            pltpu.VMEM((total, HD), jnp.bfloat16),
            pltpu.VMEM((total, HD), jnp.float32),
            pltpu.VMEM((total, HD), jnp.float32),
            pltpu.SemaphoreType.DMA,
        ],
        compiler_params=pltpu.CompilerParams(vmem_limit_bytes=24 * MIB),
        cost_estimate=pl.CostEstimate(flops=10**9, bytes_accessed=4 * 10**6, transcendentals=10**6),
        name="attention",
    )(where, *parts, *others, w5)


def gather(chip, mask_ref, own, oth, out_ref):
    rows = own[0].shape[0]
    for k in range(RING):
        head = (chip + k) % RING

        @pl.when(head < NH)
        def _():
            for block, x_ref in enumerate((own[k], oth[k])):
                x = x_ref[...]
                zero = jnp.zeros_like(x)
                for side in range(2):
                    kept = jnp.where(mask_ref[block] == 1 - side, x, zero)
                    for c in range(3):
                        lo = pl.multiple_of(((side * 3 + c) * NH + head) * HD, HD)
                        out_ref[block * rows : (block + 1) * rows, pl.ds(lo, HD)] = kept[:, c * HD : (c + 1) * HD]


def back_kernel(hop, first, place_ref, *refs):
    if first:
        mask_ref, *parts, own_ref, other_ref, out_ref, g_ref = refs
        gather(place_ref[RING * RING], mask_ref, parts[:RING], parts[RING:], g_ref)
    else:
        g_ref, own_ref, other_ref, out_ref = refs
    cols = own_ref.shape[2]
    dests = [place_ref[hop * RING + j] for j in range(RING)]
    w = [
        jnp.concatenate([w_ref[c, dest] for dest in dests], axis=0) for w_ref in (own_ref, other_ref) for c in range(3)
    ]
    res = lax.dot_general(
        g_ref[...], jnp.concatenate(w, axis=1), (((1,), (1,)), ((), ())), preferred_element_type=jnp.float32
    ).astype(jnp.bfloat16)
    for j in range(RING):
        out_ref[j] = res[:, j * cols : (j + 1) * cols]


def back(place, own_half, other_half, hop, grads=None, gather_from=None):
    cols = own_half.shape[2]
    vmem = pl.BlockSpec(memory_space=pltpu.VMEM)
    first = grads is None
    if first:
        masks, own, oth = gather_from
        rows = 2 * own[0].shape[0]
        extra = [masks, *own, *oth]
    else:
        rows = grads.shape[0]
        extra = [grads]
    out_shape = [jax.ShapeDtypeStruct((RING, rows, cols), jnp.bfloat16)]
    if first:
        out_shape.append(pltpu.VMEM((rows, 18 * HD), jnp.bfloat16))
    return pl.pallas_call(
        functools.partial(back_kernel, hop, first),
        in_specs=[pl.BlockSpec(memory_space=pltpu.SMEM)] + [vmem] * (len(extra) + 2),
        out_specs=[vmem] * len(out_shape),
        out_shape=out_shape,
        compiler_params=pltpu.CompilerParams(vmem_limit_bytes=24 * MIB),
        cost_estimate=pl.CostEstimate(flops=10**6, bytes_accessed=10**4, transcendentals=0),
        name="back",
    )(place, *extra, own_half, other_half)


def ring_perm(first, hop):
    pairs = []
    for s in range(RING):
        for m in range(2):
            for y in range(RING):
                for z in range(RING):
                    if (m == 0) == first:
                        to = (y, (z + hop) % RING)
                    else:
                        to = ((y + hop) % RING, z)
                    base = (s * 2 + m) * RING * RING
                    pairs.append((base + y * RING + z, base + to[0] * RING + to[1]))
    return pairs


def per_device(activations, grad_attn, weights, modality):
    rows, depth = activations.shape
    chip = lax.axis_index("seq")
    core = lax.axis_index("mod")
    tp = lax.axis_index("tp")
    where = jnp.stack([chip, core]).astype(jnp.int32)
    dests = RING * RING
    cols = depth // dests // 2
    w5 = jnp.transpose(weights[0], (1, 0, 2)).reshape(3, dests, 2, cols, NH * HD)

    own_mod = lax.dynamic_slice_in_dim(modality, (2 * chip + core) * rows, rows)
    other_mod = lax.dynamic_slice_in_dim(modality, (2 * chip + 1 - core) * rows, rows)
    masks = (jnp.stack([own_mod, other_mod]) == core).astype(jnp.int32)[:, :, None]

    w5 = pltpu.with_memory_space_constraint(w5, pltpu.HBM)
    activations = pltpu.with_memory_space_constraint(activations, pltpu.HBM)
    act_other = pltpu.with_memory_space_constraint(core_swap(activations), pltpu.VMEM)
    part, w_early = project_own(activations, w5, 4)
    w_early = pltpu.with_memory_space_constraint(w_early, pltpu.VMEM)
    proj_own, proj_other, half = project(where, part, activations, act_other, w_early, w5)
    proj_back = core_swap(proj_other)
    proj_back, half = lax.optimization_barrier((proj_back, half))
    other_half = pltpu.with_memory_space_constraint(core_swap(half), pltpu.VMEM)
    g_heads = grad_attn.reshape(rows, NH, HD).transpose(1, 0, 2)
    heads = jnp.concatenate([jnp.where((masks[0] > 0)[None], proj_own, proj_back), g_heads], axis=2)

    parts = [None] * RING
    others = [None] * RING
    for hop in (2, 1, 3, 0):
        head = jnp.minimum((chip + hop) % RING, NH - 1)
        x = lax.dynamic_index_in_dim(heads, head, 0, keepdims=False)
        if hop:
            x = lax.ppermute(x, "seq", [(i, (i + hop) % RING) for i in range(RING) if (i + hop) % RING < NH])
        parts[hop] = x
        others[hop] = core_swap(x)
    own, oth, own_half = attention(where, parts, others, w5)
    own_half = pltpu.with_memory_space_constraint(own_half, pltpu.VMEM)
    from_other = core_swap(oth)

    grads = [None] * RING
    other_grads = [None] * RING
    for hop in (2, 1, 3, 0):
        kv = own[hop, :, HD:] + from_other[hop].astype(jnp.float32)
        x = jnp.concatenate([own[hop, :, :HD], kv], axis=1).astype(jnp.bfloat16)
        if hop:
            x = lax.ppermute(x, "seq", [(i, (i - hop) % RING) for i in range(NH)])
        grads[hop] = x
        other_grads[hop] = core_swap(x)
    i = jnp.arange(dests, dtype=jnp.int32) // RING
    j = jnp.arange(dests, dtype=jnp.int32) % RING
    y, z = tp // RING, tp % RING
    place = jnp.where(
        core == 0,
        (y + j) % RING * RING + (z + i) % RING,
        (y + i) % RING * RING + (z + j) % RING,
    )
    place = jnp.concatenate([place, jnp.stack([chip])]).astype(jnp.int32)

    pieces = {}
    x, g = back(place, own_half, other_half, 2, gather_from=(masks, grads, other_grads))
    g = pltpu.with_memory_space_constraint(g, pltpu.VMEM)
    pieces[2] = lax.ppermute(x, AXES, ring_perm(True, 2))
    for hop in (1, 3, 0):
        (x,) = back(place, own_half, other_half, hop, grads=g)
        pieces[hop] = lax.ppermute(x, AXES, ring_perm(True, hop)) if hop else x
    total = pieces[0].astype(jnp.float32)
    for hop in (2, 1, 3):
        total = lax.optimization_barrier(total) + pieces[hop].astype(jnp.float32)
    result = total[0]
    for hop in (2, 1, 3):
        got = lax.ppermute(total[hop].astype(jnp.bfloat16), AXES, ring_perm(False, hop))
        result = result + got.astype(jnp.float32)
    result = result.astype(jnp.bfloat16)
    mine = result[:rows]
    theirs = core_swap(result[rows:])
    return jnp.where(
        core == 0, jnp.concatenate([mine, theirs], axis=1), jnp.concatenate([theirs, mine], axis=1)
    )


def solution(mesh):
    in_specs = (P(("seq", "mod"), None), P(("seq", "mod"), "tp"), P("mod", None, None, "tp"), P())
    out_specs = P(("seq", "mod"), "tp")
    return jax.shard_map(
        per_device, mesh=mesh, in_specs=in_specs, out_specs=out_specs, check_vma=False
    )
```

```python
import functools

import jax
import jax.numpy as jnp
from jax import lax
from jax.experimental import pallas as pl
from jax.experimental.pallas import tpu as pltpu
from jax.sharding import PartitionSpec as P

HD = 128
NH = 3
RING = 4
SCALE = HD**-0.5
AXES = ("seq", "mod", "tp")
MIB = 1024 * 1024


def core_swap(x):
    return lax.ppermute(x, "mod", [(0, 1), (1, 0)])


def weight_block(w_ref, i):
    size = 4 * w_ref.shape[3]
    return jnp.concatenate([w_ref[c, 2 * i : 2 * i + 2].reshape(size, NH * HD) for c in range(3)], axis=1)


def own_kernel(a_hbm, w_hbm, part_ref, w_ref, a_s, a_sem, w_sem):
    chunks = w_ref.shape[1] // 2
    block = 4 * w_ref.shape[3]

    def fetch(i):
        pair = slice(2 * i, 2 * i + 2)
        return (
            pltpu.make_async_copy(a_hbm.at[:, pl.ds(i * block, block)], a_s.at[i], a_sem.at[i]),
            pltpu.make_async_copy(w_hbm.at[:, pair], w_ref.at[:, pair], w_sem.at[i]),
        )

    for i in range(chunks):
        for copy in fetch(i):
            copy.start()
    for i in range(chunks):
        for copy in fetch(i):
            copy.wait()
        part = jnp.dot(a_s[i], weight_block(w_ref, i), preferred_element_type=jnp.float32)
        if i == 0:
            part_ref[...] = part
        else:
            part_ref[...] += part


def project_own(a, w5, early):
    rows = a.shape[0]
    block = 4 * w5.shape[3]
    vmem = pl.BlockSpec(memory_space=pltpu.VMEM)
    hbm = pl.BlockSpec(memory_space=pltpu.HBM)
    return pl.pallas_call(
        own_kernel,
        in_specs=[hbm, hbm],
        out_specs=[vmem, vmem],
        out_shape=[
            jax.ShapeDtypeStruct((rows, 9 * HD), jnp.float32),
            pltpu.VMEM((3, 2 * early) + w5.shape[2:], jnp.bfloat16),
        ],
        scratch_shapes=[
            pltpu.VMEM((early, rows, block), jnp.bfloat16),
            pltpu.SemaphoreType.DMA((early,)),
            pltpu.SemaphoreType.DMA((early,)),
        ],
        compiler_params=pltpu.CompilerParams(vmem_limit_bytes=20 * MIB),
        cost_estimate=pl.CostEstimate(flops=4 * 10**9, bytes_accessed=10**7, transcendentals=0),
        name="project_own",
    )(a, w5)


def project_kernel(
    early, where_ref, part_ref, own_hbm, oth_ref, w_ref, w_hbm, own_out, oth_out, half_hbm, a_s, w_s, acc_ref,
    own_sem, w_sem, half_sem
):
    rows = part_ref.shape[0]
    chunks = half_hbm.shape[1] // 2
    block = 4 * w_ref.shape[3]
    side = 1 - where_ref[1]

    def fetch_own(i):
        return pltpu.make_async_copy(own_hbm.at[:, pl.ds(i * block, block)], a_s.at[i - early], own_sem.at[i])

    def other(i):
        return oth_ref[:, i * block : (i + 1) * block]

    def fetch_weights(i):
        src = w_hbm.at[:, 2 * i : 2 * i + 2]
        return pltpu.make_async_copy(src, w_s.at[:, 2 * (i - early) : 2 * (i - early) + 2], w_sem.at[i])

    def put_half(i):
        if i < early:
            src = w_ref.at[:, 2 * i : 2 * i + 2, side]
        else:
            src = w_s.at[:, 2 * (i - early) : 2 * (i - early) + 2, side]
        return pltpu.make_async_copy(src, half_hbm.at[:, 2 * i : 2 * i + 2], half_sem.at[i])

    for i in range(early, chunks):
        fetch_weights(i).start()
        fetch_own(i).start()
    for i in range(early):
        put_half(i).start()
    acc_ref[0:rows] = part_ref[...]
    for i in range(chunks):
        if i < early:
            part = jnp.dot(other(i), weight_block(w_ref, i), preferred_element_type=jnp.float32)
            if i == 0:
                acc_ref[rows:] = part
            else:
                acc_ref[rows:] += part
        else:
            fetch_own(i).wait()
            fetch_weights(i).wait()
            put_half(i).start()
            a = jnp.concatenate([a_s[i - early], other(i)], axis=0)
            acc_ref[...] += jnp.dot(a, weight_block(w_s, i - early), preferred_element_type=jnp.float32)
    for h in range(NH):
        for c in range(3):
            lo = c * NH * HD + h * HD
            x = acc_ref[:, lo : lo + HD].astype(jnp.bfloat16)
            own_out[h, :, c * HD : (c + 1) * HD] = x[0:rows]
            oth_out[h, :, c * HD : (c + 1) * HD] = x[rows:]
    for i in range(chunks):
        put_half(i).wait()


def project(where, part, own, other, w_early, w5):
    rows, depth = own.shape
    chunks = w5.shape[1] // 2
    early = w_early.shape[1] // 2
    shape = jax.ShapeDtypeStruct((NH, rows, 3 * HD), jnp.bfloat16)
    vmem = pl.BlockSpec(memory_space=pltpu.VMEM)
    hbm = pl.BlockSpec(memory_space=pltpu.HBM)
    dma = pltpu.SemaphoreType.DMA((chunks,))
    return pl.pallas_call(
        functools.partial(project_kernel, early),
        in_specs=[pl.BlockSpec(memory_space=pltpu.SMEM), vmem, hbm, vmem, vmem, hbm],
        out_specs=[vmem, vmem, hbm],
        out_shape=[shape, shape, pltpu.HBM((3,) + w5.shape[1:2] + w5.shape[3:], jnp.bfloat16)],
        scratch_shapes=[
            pltpu.VMEM((chunks - early, rows, depth // chunks), jnp.bfloat16),
            pltpu.VMEM((3, 2 * (chunks - early)) + w5.shape[2:], jnp.bfloat16),
            pltpu.VMEM((2 * rows, 9 * HD), jnp.float32),
            dma,
            dma,
            dma,
        ],
        compiler_params=pltpu.CompilerParams(vmem_limit_bytes=26 * MIB),
        cost_estimate=pl.CostEstimate(flops=7 * 10**9, bytes_accessed=10**7, transcendentals=0),
        name="project",
    )(where, part, own, other, w_early, w5)


def attention_kernel(
    where_ref, a0, a1, a2, a3, b0, b1, b2, b3, own_ref, oth_ref, q_s, g_s, k_s, v_s, dk_s, dv_s
):
    chip = where_ref[0]
    core = where_ref[1]
    rows = a0.shape[0]
    both = 2 * rows
    own = (a0, a1, a2, a3)
    oth = (b0, b1, b2, b3)
    for k, (r, o) in enumerate(zip(own, oth)):
        shard = (chip - k + RING) % RING
        q_s[shard] = r[:, 0:HD]
        g_s[shard] = r[:, 3 * HD : 4 * HD]
        mine = pl.ds(pl.multiple_of((2 * shard + core) * rows, rows), rows)
        other = pl.ds(pl.multiple_of((2 * shard + 1 - core) * rows, rows), rows)
        k_s[mine, :] = r[:, HD : 2 * HD]
        v_s[mine, :] = r[:, 2 * HD : 3 * HD]
        k_s[other, :] = o[:, HD : 2 * HD]
        v_s[other, :] = o[:, 2 * HD : 3 * HD]
    nt = (((1,), (1,)), ((), ()))
    tn = (((0,), (0,)), ((), ()))
    for s in range(RING - 1, -1, -1):
        width = both * (s + 1)
        q = q_s[s]
        g = g_s[s]
        kk = k_s[0:width, :]
        vv = v_s[0:width, :]
        scores = lax.dot_general(q, kk, nt, preferred_element_type=jnp.float32) * SCALE
        row = lax.broadcasted_iota(jnp.int32, (rows, width), 0) + (2 * s + core) * rows
        col = lax.broadcasted_iota(jnp.int32, (rows, width), 1)
        scores = jnp.where(col <= row, scores, -jnp.inf)
        lifted = jnp.exp(scores - jnp.max(scores, axis=1, keepdims=True))
        probs = lifted / jnp.sum(lifted, axis=1, keepdims=True)
        low = probs.astype(jnp.bfloat16)
        dprobs = lax.dot_general(g, vv, nt, preferred_element_type=jnp.float32)
        row_dot = jnp.sum(probs * dprobs, axis=1, keepdims=True)
        ds = (probs * (dprobs - row_dot)).astype(jnp.bfloat16)
        dq = jnp.dot(ds, kk, preferred_element_type=jnp.float32) * SCALE
        dk = lax.dot_general(ds, q, tn, preferred_element_type=jnp.float32) * SCALE
        dv = lax.dot_general(low, g, tn, preferred_element_type=jnp.float32)
        if s == RING - 1:
            dk_s[...] = dk
            dv_s[...] = dv
        else:
            dk_s[0:width, :] += dk
            dv_s[0:width, :] += dv
        own_ref[(chip - s + RING) % RING, :, 0:HD] = dq
    for k in range(RING):
        shard = (chip - k + RING) % RING
        mine = pl.ds(pl.multiple_of((2 * shard + core) * rows, rows), rows)
        other = pl.ds(pl.multiple_of((2 * shard + 1 - core) * rows, rows), rows)
        own_ref[k, :, HD : 2 * HD] = dk_s[mine, :]
        own_ref[k, :, 2 * HD : 3 * HD] = dv_s[mine, :]
        oth_ref[k, :, 0:HD] = dk_s[other, :].astype(jnp.bfloat16)
        oth_ref[k, :, HD : 2 * HD] = dv_s[other, :].astype(jnp.bfloat16)


def attention(where, parts, others):
    rows = parts[0].shape[0]
    total = 2 * RING * rows
    vmem = pl.BlockSpec(memory_space=pltpu.VMEM)
    return pl.pallas_call(
        attention_kernel,
        in_specs=[pl.BlockSpec(memory_space=pltpu.SMEM)] + [vmem] * 8,
        out_specs=[vmem, vmem],
        out_shape=[
            jax.ShapeDtypeStruct((RING, rows, 3 * HD), jnp.float32),
            jax.ShapeDtypeStruct((RING, rows, 2 * HD), jnp.bfloat16),
        ],
        scratch_shapes=[
            pltpu.VMEM((RING, rows, HD), jnp.bfloat16),
            pltpu.VMEM((RING, rows, HD), jnp.bfloat16),
            pltpu.VMEM((total, HD), jnp.bfloat16),
            pltpu.VMEM((total, HD), jnp.bfloat16),
            pltpu.VMEM((total, HD), jnp.float32),
            pltpu.VMEM((total, HD), jnp.float32),
        ],
        compiler_params=pltpu.CompilerParams(vmem_limit_bytes=32 * MIB),
        cost_estimate=pl.CostEstimate(flops=10**9, bytes_accessed=4 * 10**6, transcendentals=10**6),
        name="attention",
    )(where, *parts, *others)


def gather(chip, mask_ref, own, oth, out_ref):
    rows = own[0].shape[0]
    for k in range(RING):
        head = (chip + k) % RING

        @pl.when(head < NH)
        def _():
            for block, x_ref in enumerate((own[k], oth[k])):
                x = x_ref[...]
                zero = jnp.zeros_like(x)
                for side in range(2):
                    kept = jnp.where(mask_ref[block] == 1 - side, x, zero)
                    for c in range(3):
                        lo = pl.multiple_of(((side * 3 + c) * NH + head) * HD, HD)
                        out_ref[block * rows : (block + 1) * rows, pl.ds(lo, HD)] = kept[:, c * HD : (c + 1) * HD]


def weight_copies(place_ref, own_hbm, other_hbm, to_ref, sem, hop):
    core = place_ref[RING * RING]
    copies = []
    for j in range(RING):
        dest = place_ref[hop * RING + j]
        copies.append(pltpu.make_async_copy(own_hbm.at[:, dest, core], to_ref.at[0, :, j], sem.at[0, j]))
        copies.append(pltpu.make_async_copy(other_hbm.at[:, dest], to_ref.at[1, :, j], sem.at[1, j]))
    return copies


def fetch_kernel(hops, place_ref, after_ref, own_hbm, other_hbm, *refs):
    copies = []
    for i, hop in enumerate(hops):
        copies += weight_copies(place_ref, own_hbm, other_hbm, refs[i], refs[len(hops) + i], hop)
    for copy in copies:
        copy.start()
    for copy in copies:
        copy.wait()


def fetch_weights(place, after, w5, other_half, hops):
    vmem = pl.BlockSpec(memory_space=pltpu.VMEM)
    hbm = pl.BlockSpec(memory_space=pltpu.HBM)
    anywhere = pl.BlockSpec(memory_space=pl.ANY)
    return pl.pallas_call(
        functools.partial(fetch_kernel, hops),
        in_specs=[pl.BlockSpec(memory_space=pltpu.SMEM), vmem, hbm, anywhere],
        out_specs=[vmem for _ in hops],
        out_shape=[pltpu.VMEM((2, 3, RING) + w5.shape[3:], jnp.bfloat16) for _ in hops],
        scratch_shapes=[pltpu.SemaphoreType.DMA((2, RING)) for _ in hops],
        compiler_params=pltpu.CompilerParams(vmem_limit_bytes=20 * MIB),
        cost_estimate=pl.CostEstimate(flops=10**6, bytes_accessed=10**7, transcendentals=0),
        name="fetch_weights",
    )(place, after, w5, other_half)


def product(g_ref, w_ref, out_ref, j, count):
    cols = w_ref.shape[3]
    w = [w_ref[side, c, j : j + count].reshape(count * cols, NH * HD) for side in range(2) for c in range(3)]
    res = lax.dot_general(
        g_ref[...], jnp.concatenate(w, axis=1), (((1,), (1,)), ((), ())), preferred_element_type=jnp.float32
    ).astype(jnp.bfloat16)
    for i in range(count):
        out_ref[j + i] = res[:, i * cols : (i + 1) * cols]


def back_first_kernel(following, place_ref, mask_ref, *refs):
    *parts, w_ref, own_hbm, other_hbm, out_ref, g_ref, next_ref, sem = refs
    for copy in weight_copies(place_ref, own_hbm, other_hbm, next_ref, sem, following):
        copy.start()
    gather(place_ref[RING * RING + 1], mask_ref, parts[:RING], parts[RING:], g_ref)
    product(g_ref, w_ref, out_ref, 0, RING)
    for copy in weight_copies(place_ref, own_hbm, other_hbm, next_ref, sem, following):
        copy.wait()


def back_middle_kernel(g_ref, w_ref, out_ref):
    product(g_ref, w_ref, out_ref, 0, RING)


def back_last_kernel(hop, place_ref, g_ref, own_hbm, other_hbm, out_ref, w_s, sem):
    copies = weight_copies(place_ref, own_hbm, other_hbm, w_s, sem, hop)
    for copy in copies:
        copy.start()
    for j in range(0, RING, 2):
        for copy in copies[2 * j : 2 * j + 4]:
            copy.wait()
        product(g_ref, w_s, out_ref, j, 2)


def back_call(kernel, operands, in_specs, out_shape, scratch):
    vmem = pl.BlockSpec(memory_space=pltpu.VMEM)
    return pl.pallas_call(
        kernel,
        in_specs=in_specs,
        out_specs=[vmem] * len(out_shape),
        out_shape=out_shape,
        scratch_shapes=scratch,
        compiler_params=pltpu.CompilerParams(vmem_limit_bytes=24 * MIB),
        cost_estimate=pl.CostEstimate(flops=10**6, bytes_accessed=10**4, transcendentals=0),
        name="back",
    )(*operands)


def back_products(place, masks, own, oth, weights, w5, other_half, send):
    rows = 2 * own[0].shape[0]
    cols = w5.shape[3]
    smem = pl.BlockSpec(memory_space=pltpu.SMEM)
    vmem = pl.BlockSpec(memory_space=pltpu.VMEM)
    hbm = pl.BlockSpec(memory_space=pltpu.HBM)
    anywhere = pl.BlockSpec(memory_space=pl.ANY)
    piece = jax.ShapeDtypeStruct((RING, rows, cols), jnp.bfloat16)
    w_shape = (2, 3, RING) + w5.shape[3:]
    sem = pltpu.SemaphoreType.DMA((2, RING))
    w_two, w_one = weights
    x, g, w_three = back_call(
        functools.partial(back_first_kernel, 3),
        (place, masks, *own, *oth, w_two, w5, other_half),
        [smem] + [vmem] * 10 + [hbm, anywhere],
        [piece, pltpu.VMEM((rows, 18 * HD), jnp.bfloat16), pltpu.VMEM(w_shape, jnp.bfloat16)],
        [sem],
    )
    g = pltpu.with_memory_space_constraint(g, pltpu.VMEM)
    w_three = pltpu.with_memory_space_constraint(w_three, pltpu.VMEM)
    pieces = {2: send(x, 2)}
    for hop, w in ((1, w_one), (3, w_three)):
        (x,) = back_call(back_middle_kernel, (g, w), [vmem, vmem], [piece], [])
        pieces[hop] = send(x, hop)
    (pieces[0],) = back_call(
        functools.partial(back_last_kernel, 0),
        (place, g, w5, other_half),
        [smem, vmem, hbm, anywhere],
        [piece],
        [pltpu.VMEM(w_shape, jnp.bfloat16), sem],
    )
    return pieces


def ring_perm(first, hop):
    pairs = []
    for s in range(RING):
        for m in range(2):
            for y in range(RING):
                for z in range(RING):
                    if (m == 0) == first:
                        to = (y, (z + hop) % RING)
                    else:
                        to = ((y + hop) % RING, z)
                    base = (s * 2 + m) * RING * RING
                    pairs.append((base + y * RING + z, base + to[0] * RING + to[1]))
    return pairs


def per_device(activations, grad_attn, weights, modality):
    rows, depth = activations.shape
    chip = lax.axis_index("seq")
    core = lax.axis_index("mod")
    tp = lax.axis_index("tp")
    where = jnp.stack([chip, core]).astype(jnp.int32)
    dests = RING * RING
    cols = depth // dests // 2
    w5 = jnp.transpose(weights[0], (1, 0, 2)).reshape(3, dests, 2, cols, NH * HD)

    own_mod = lax.dynamic_slice_in_dim(modality, (2 * chip + core) * rows, rows)
    other_mod = lax.dynamic_slice_in_dim(modality, (2 * chip + 1 - core) * rows, rows)
    masks = (jnp.stack([own_mod, other_mod]) == core).astype(jnp.int32)[:, :, None]

    w5 = pltpu.with_memory_space_constraint(w5, pltpu.HBM)
    activations = pltpu.with_memory_space_constraint(activations, pltpu.HBM)
    g_heads = grad_attn.reshape(rows, NH, HD).transpose(1, 0, 2)
    is_mine = jnp.broadcast_to(masks[0], (rows, HD))
    where, masks, is_mine, g_heads = lax.optimization_barrier((where, masks, is_mine, g_heads))
    act_other = pltpu.with_memory_space_constraint(core_swap(activations), pltpu.VMEM)
    part, w_early = project_own(activations, w5, 4)
    w_early = pltpu.with_memory_space_constraint(w_early, pltpu.VMEM)
    proj_own, proj_other, half = project(where, part, activations, act_other, w_early, w5)
    proj_back = core_swap(proj_other)
    proj_back, half = lax.optimization_barrier((proj_back, half))
    other_half = core_swap(half)
    heads = jnp.concatenate([jnp.where(jnp.concatenate([is_mine] * 3, axis=1)[None] > 0, proj_own, proj_back), g_heads], axis=2)

    parts = [None] * RING
    others = [None] * RING
    for hop in (2, 1, 3, 0):
        head = jnp.minimum((chip + hop) % RING, NH - 1)
        x = lax.dynamic_index_in_dim(heads, head, 0, keepdims=False)
        if hop:
            x = lax.ppermute(x, "seq", [(i, (i + hop) % RING) for i in range(RING) if (i + hop) % RING < NH])
        parts[hop] = x
        others[hop] = core_swap(x)
    own, oth = attention(where, parts, others)
    from_other = core_swap(oth)

    i = jnp.arange(dests, dtype=jnp.int32) // RING
    j = jnp.arange(dests, dtype=jnp.int32) % RING
    y, z = tp // RING, tp % RING
    place = jnp.where(
        core == 0,
        (y + j) % RING * RING + (z + i) % RING,
        (y + i) % RING * RING + (z + j) % RING,
    )
    place = jnp.concatenate([place, jnp.stack([core, chip])]).astype(jnp.int32)

    grads = [None] * RING
    for hop in (2, 1, 3, 0):
        kv = own[hop, :, HD:] + from_other[hop].astype(jnp.float32)
        x = jnp.concatenate([own[hop, :, :HD], kv], axis=1).astype(jnp.bfloat16)
        if hop:
            x = lax.ppermute(x, "seq", [(i, (i - hop) % RING) for i in range(NH)])
        grads[hop] = x
    w_first = fetch_weights(place, grads[0], w5, other_half, (2, 1))
    w_first = [pltpu.with_memory_space_constraint(w, pltpu.VMEM) for w in w_first]
    grads[1:], w_first = lax.optimization_barrier((grads[1:], w_first))
    other_grads = [None] * RING
    for hop in (2, 1, 3, 0):
        other_grads[hop] = core_swap(grads[hop])

    pieces = back_products(
        place,
        masks,
        grads,
        other_grads,
        w_first,
        w5,
        other_half,
        lambda x, hop: lax.ppermute(x, AXES, ring_perm(True, hop)),
    )
    total = pieces[0].astype(jnp.float32)
    for hop in (2, 1, 3):
        total = lax.optimization_barrier(total) + pieces[hop].astype(jnp.float32)
    result = total[0]
    for hop in (2, 1, 3):
        got = lax.ppermute(total[hop].astype(jnp.bfloat16), AXES, ring_perm(False, hop))
        result = result + got.astype(jnp.float32)
    result = result.astype(jnp.bfloat16)
    mine = result[:rows]
    theirs = core_swap(result[rows:])
    return jnp.where(
        core == 0, jnp.concatenate([mine, theirs], axis=1), jnp.concatenate([theirs, mine], axis=1)
    )


def solution(mesh):
    in_specs = (P(("seq", "mod"), None), P(("seq", "mod"), "tp"), P("mod", None, None, "tp"), P())
    out_specs = P(("seq", "mod"), "tp")
    return jax.shard_map(
        per_device, mesh=mesh, in_specs=in_specs, out_specs=out_specs, check_vma=False
    )
```

```python
import functools

import jax
import jax.numpy as jnp
from jax import lax
from jax.experimental import pallas as pl
from jax.experimental.pallas import tpu as pltpu
from jax.sharding import PartitionSpec as P

HD = 128
NH = 3
RING = 4
SCALE = HD**-0.5
AXES = ("seq", "mod", "tp")
MIB = 1024 * 1024


def core_swap(x):
    return lax.ppermute(x, "mod", [(0, 1), (1, 0)])


def weight_block(w_ref, i):
    size = 4 * w_ref.shape[3]
    return jnp.concatenate([w_ref[c, 2 * i : 2 * i + 2].reshape(size, NH * HD) for c in range(3)], axis=1)


def own_kernel(a_hbm, w_hbm, part_ref, w_ref, a_s, a_sem, w_sem):
    chunks = w_ref.shape[1] // 2
    block = 4 * w_ref.shape[3]

    def fetch(i):
        pair = slice(2 * i, 2 * i + 2)
        return (
            pltpu.make_async_copy(a_hbm.at[:, pl.ds(i * block, block)], a_s.at[i], a_sem.at[i]),
            pltpu.make_async_copy(w_hbm.at[:, pair], w_ref.at[:, pair], w_sem.at[i]),
        )

    for i in range(chunks):
        for copy in fetch(i):
            copy.start()
    for i in range(chunks):
        for copy in fetch(i):
            copy.wait()
        part = jnp.dot(a_s[i], weight_block(w_ref, i), preferred_element_type=jnp.float32)
        if i == 0:
            part_ref[...] = part
        else:
            part_ref[...] += part


def project_own(a, w5, early):
    rows = a.shape[0]
    block = 4 * w5.shape[3]
    vmem = pl.BlockSpec(memory_space=pltpu.VMEM)
    hbm = pl.BlockSpec(memory_space=pltpu.HBM)
    return pl.pallas_call(
        own_kernel,
        in_specs=[hbm, hbm],
        out_specs=[vmem, vmem],
        out_shape=[
            jax.ShapeDtypeStruct((rows, 9 * HD), jnp.float32),
            pltpu.VMEM((3, 2 * early) + w5.shape[2:], jnp.bfloat16),
        ],
        scratch_shapes=[
            pltpu.VMEM((early, rows, block), jnp.bfloat16),
            pltpu.SemaphoreType.DMA((early,)),
            pltpu.SemaphoreType.DMA((early,)),
        ],
        compiler_params=pltpu.CompilerParams(vmem_limit_bytes=20 * MIB),
        cost_estimate=pl.CostEstimate(flops=4 * 10**9, bytes_accessed=10**7, transcendentals=0),
        name="project_own",
    )(a, w5)


def project_kernel(
    early, where_ref, part_ref, own_hbm, oth_ref, w_ref, w_hbm, g_ref, own_out, send_out, half_hbm, a_s, w_s, acc_ref,
    own_sem, w_sem, half_sem
):
    rows = part_ref.shape[0]
    chunks = half_hbm.shape[1] // 2
    block = 4 * w_ref.shape[3]
    side = 1 - where_ref[1]

    def fetch_own(i):
        return pltpu.make_async_copy(own_hbm.at[:, pl.ds(i * block, block)], a_s.at[i - early], own_sem.at[i])

    def other(i):
        return oth_ref[:, i * block : (i + 1) * block]

    def fetch_weights(i):
        src = w_hbm.at[:, 2 * i : 2 * i + 2]
        return pltpu.make_async_copy(src, w_s.at[:, 2 * (i - early) : 2 * (i - early) + 2], w_sem.at[i])

    def put_half(i):
        if i < early:
            src = w_ref.at[:, 2 * i : 2 * i + 2, side]
        else:
            src = w_s.at[:, 2 * (i - early) : 2 * (i - early) + 2, side]
        return pltpu.make_async_copy(src, half_hbm.at[:, 2 * i : 2 * i + 2], half_sem.at[i])

    for i in range(early, chunks):
        fetch_weights(i).start()
        fetch_own(i).start()
    for i in range(early):
        put_half(i).start()
    acc_ref[0:rows] = part_ref[...]
    for i in range(chunks):
        if i < early:
            part = jnp.dot(other(i), weight_block(w_ref, i), preferred_element_type=jnp.float32)
            if i == 0:
                acc_ref[rows:] = part
            else:
                acc_ref[rows:] += part
        else:
            fetch_own(i).wait()
            fetch_weights(i).wait()
            put_half(i).start()
            a = jnp.concatenate([a_s[i - early], other(i)], axis=0)
            acc_ref[...] += jnp.dot(a, weight_block(w_s, i - early), preferred_element_type=jnp.float32)
    for h in range(NH):
        for c in range(3):
            lo = c * NH * HD + h * HD
            to = slice((h * 3 + c) * HD, (h * 3 + c + 1) * HD)
            x = acc_ref[:, lo : lo + HD].astype(jnp.bfloat16)
            own_out[:, to] = x[0:rows]
            send_out[:, to] = x[rows:]
    theirs = pair_head(where_ref[0], side)
    send_out[:, 9 * HD : 12 * HD] = own_out[:, head_columns(theirs, 3)]
    send_out[:, 12 * HD :] = g_ref[:, head_columns(theirs, 1)]
    for i in range(chunks):
        put_half(i).wait()


def project(where, part, own, other, w_early, w5, g):
    rows, depth = own.shape
    chunks = w5.shape[1] // 2
    early = w_early.shape[1] // 2
    vmem = pl.BlockSpec(memory_space=pltpu.VMEM)
    hbm = pl.BlockSpec(memory_space=pltpu.HBM)
    dma = pltpu.SemaphoreType.DMA((chunks,))
    return pl.pallas_call(
        functools.partial(project_kernel, early),
        in_specs=[pl.BlockSpec(memory_space=pltpu.SMEM), vmem, hbm, vmem, vmem, hbm, vmem],
        out_specs=[vmem, vmem, hbm],
        out_shape=[
            jax.ShapeDtypeStruct((rows, 9 * HD), jnp.bfloat16),
            jax.ShapeDtypeStruct((rows, 13 * HD), jnp.bfloat16),
            pltpu.HBM((3,) + w5.shape[1:2] + w5.shape[3:], jnp.bfloat16),
        ],
        scratch_shapes=[
            pltpu.VMEM((chunks - early, rows, depth // chunks), jnp.bfloat16),
            pltpu.VMEM((3, 2 * (chunks - early)) + w5.shape[2:], jnp.bfloat16),
            pltpu.VMEM((2 * rows, 9 * HD), jnp.float32),
            dma,
            dma,
            dma,
        ],
        compiler_params=pltpu.CompilerParams(vmem_limit_bytes=26 * MIB),
        cost_estimate=pl.CostEstimate(flops=7 * 10**9, bytes_accessed=10**7, transcendentals=0),
        name="project",
    )(where, part, own, other, w_early, w5, g)


def pair_head(chip, core):
    return jnp.minimum((chip + 1 + 2 * core) % RING, NH - 1)


def head_columns(head, width):
    return pl.ds(pl.multiple_of(head * (width * HD), width * HD), width * HD)


def section_rows(mod_ref, block, core):
    rows = mod_ref.shape[1]
    mine = (mod_ref[pl.ds(block, 1), :] == core).astype(jnp.float32)
    row = lax.broadcasted_iota(jnp.int32, (rows, rows), 0)
    col = lax.broadcasted_iota(jnp.int32, (rows, rows), 1)
    return jnp.sum(jnp.where(row == col, mine, 0.0), axis=1, keepdims=True)


def route_kernel(where_ref, mod_ref, own_ref, sent_ref, got_ref, g_ref, pair_out, far_out, stay_out):
    chip, core = where_ref[0], where_ref[1]
    mine = section_rows(mod_ref, 2 * chip + core, core) > 0
    others = section_rows(mod_ref, 2 * chip + 1 - core, core) > 0

    def own_rows(head):
        cols = head_columns(head, 3)
        return jnp.where(mine, own_ref[:, cols], got_ref[:, cols]), g_ref[:, head_columns(head, 1)]

    head = pair_head(chip, core)
    pair_out[0, :, : 3 * HD], pair_out[0, :, 3 * HD :] = own_rows(head)
    pair_out[1, :, : 3 * HD] = jnp.where(others, sent_ref[:, head_columns(head, 3)], got_ref[:, 9 * HD : 12 * HD])
    pair_out[1, :, 3 * HD :] = got_ref[:, 12 * HD :]
    far_out[:, : 3 * HD], far_out[:, 3 * HD :] = own_rows(jnp.minimum((chip + 2) % RING, NH - 1))
    stay_out[:, : 3 * HD], stay_out[:, 3 * HD :] = own_rows(jnp.minimum(chip, NH - 1))


def small_call(kernel, name, where, operands, out_shape):
    vmem = pl.BlockSpec(memory_space=pltpu.VMEM)
    return pl.pallas_call(
        kernel,
        in_specs=[pl.BlockSpec(memory_space=pltpu.SMEM)] + [vmem] * len(operands),
        out_specs=[vmem] * len(out_shape),
        out_shape=out_shape,
        compiler_params=pltpu.CompilerParams(vmem_limit_bytes=16 * MIB),
        cost_estimate=pl.CostEstimate(flops=10**6, bytes_accessed=3 * 10**6, transcendentals=0),
        name=name,
    )(where, *operands)


def attention_kernel(
    where_ref, stay, far, pair, stay_o, far_o, pair_o, keep_ref, send_ref, q_s, g_s, k_s, v_s, dq_s, dk_s, dv_s
):
    chip = where_ref[0]
    core = where_ref[1]
    rows = stay.shape[0]
    both = 2 * rows
    near = (chip + 3 + 2 * core) % RING
    across = (chip + 1 + 2 * core) % RING
    opposite = (chip + 2) % RING

    def block_rows(shard, side):
        return pl.ds(pl.multiple_of((2 * shard + side) * rows, rows), rows)

    for shard, r, o in (
        (chip, stay, stay_o),
        (opposite, far, far_o),
        (near, pair.at[0], pair.at[1]),
        (across, pair_o.at[1], pair_o.at[0]),
    ):
        q_s[shard] = r[:, 0:HD]
        g_s[shard] = r[:, 3 * HD : 4 * HD]
        k_s[block_rows(shard, core), :] = r[:, HD : 2 * HD]
        v_s[block_rows(shard, core), :] = r[:, 2 * HD : 3 * HD]
        k_s[block_rows(shard, 1 - core), :] = o[:, HD : 2 * HD]
        v_s[block_rows(shard, 1 - core), :] = o[:, 2 * HD : 3 * HD]
    nt = (((1,), (1,)), ((), ()))
    tn = (((0,), (0,)), ((), ()))
    for s in range(RING - 1, -1, -1):
        width = both * (s + 1)
        q = q_s[s]
        g = g_s[s]
        kk = k_s[0:width, :]
        vv = v_s[0:width, :]
        scores = lax.dot_general(q, kk, nt, preferred_element_type=jnp.float32) * SCALE
        row = lax.broadcasted_iota(jnp.int32, (rows, width), 0) + (2 * s + core) * rows
        col = lax.broadcasted_iota(jnp.int32, (rows, width), 1)
        scores = jnp.where(col <= row, scores, -jnp.inf)
        lifted = jnp.exp(scores - jnp.max(scores, axis=1, keepdims=True))
        probs = lifted / jnp.sum(lifted, axis=1, keepdims=True)
        low = probs.astype(jnp.bfloat16)
        dprobs = lax.dot_general(g, vv, nt, preferred_element_type=jnp.float32)
        row_dot = jnp.sum(probs * dprobs, axis=1, keepdims=True)
        ds = (probs * (dprobs - row_dot)).astype(jnp.bfloat16)
        dq = jnp.dot(ds, kk, preferred_element_type=jnp.float32) * SCALE
        dk = lax.dot_general(ds, q, tn, preferred_element_type=jnp.float32) * SCALE
        dv = lax.dot_general(low, g, tn, preferred_element_type=jnp.float32)
        if s == RING - 1:
            dk_s[...] = dk
            dv_s[...] = dv
        else:
            dk_s[0:width, :] += dk
            dv_s[0:width, :] += dv
        dq_s[s] = dq
    col = 0
    for shard, whole in ((near, True), (near, False), (chip, True), (opposite, True)):
        if whole:
            keep_ref[:, col : col + HD] = dq_s[shard]
            col += HD
        side = core if whole else 1 - core
        keep_ref[:, col : col + HD] = dk_s[block_rows(shard, side), :]
        keep_ref[:, col + HD : col + 2 * HD] = dv_s[block_rows(shard, side), :]
        col += 2 * HD
    col = 0
    for shard, whole in ((across, True), (across, False), (chip, False), (opposite, False)):
        if whole:
            send_ref[:, col : col + HD] = dq_s[shard].astype(jnp.bfloat16)
            col += HD
        side = core if whole else 1 - core
        send_ref[:, col : col + HD] = dk_s[block_rows(shard, side), :].astype(jnp.bfloat16)
        send_ref[:, col + HD : col + 2 * HD] = dv_s[block_rows(shard, side), :].astype(jnp.bfloat16)
        col += 2 * HD


def attention(where, parts):
    rows = parts[0].shape[0]
    total = 2 * RING * rows
    vmem = pl.BlockSpec(memory_space=pltpu.VMEM)
    return pl.pallas_call(
        attention_kernel,
        in_specs=[pl.BlockSpec(memory_space=pltpu.SMEM)] + [vmem] * 6,
        out_specs=[vmem, vmem],
        out_shape=[
            jax.ShapeDtypeStruct((rows, 11 * HD), jnp.float32),
            jax.ShapeDtypeStruct((rows, 9 * HD), jnp.bfloat16),
        ],
        scratch_shapes=[
            pltpu.VMEM((RING, rows, HD), jnp.bfloat16),
            pltpu.VMEM((RING, rows, HD), jnp.bfloat16),
            pltpu.VMEM((total, HD), jnp.bfloat16),
            pltpu.VMEM((total, HD), jnp.bfloat16),
            pltpu.VMEM((RING, rows, HD), jnp.float32),
            pltpu.VMEM((total, HD), jnp.float32),
            pltpu.VMEM((total, HD), jnp.float32),
        ],
        compiler_params=pltpu.CompilerParams(vmem_limit_bytes=32 * MIB),
        cost_estimate=pl.CostEstimate(flops=10**9, bytes_accessed=4 * 10**6, transcendentals=10**6),
        name="attention",
    )(where, *parts)


def combine_kernel(where_ref, keep, got, pair_out, far_out, stay_out):
    def put(out, query, kept, partner):
        out[:, 0:HD] = query.astype(jnp.bfloat16)
        kv = keep[:, kept : kept + 2 * HD] + got[:, partner : partner + 2 * HD].astype(jnp.float32)
        out[:, HD : 3 * HD] = kv.astype(jnp.bfloat16)

    put(pair_out.at[0], keep[:, 0:HD], HD, 3 * HD)
    put(pair_out.at[1], got[:, 0:HD], 3 * HD, HD)
    put(stay_out, keep[:, 5 * HD : 6 * HD], 6 * HD, 5 * HD)
    put(far_out, keep[:, 8 * HD : 9 * HD], 9 * HD, 7 * HD)


def gather(where, mod_ref, parts, out_ref):
    chip, core = where
    stay, far, pair, stay_o, far_o, pair_o = parts
    rows = stay.shape[0]
    mine = [section_rows(mod_ref, 2 * chip + core, core), section_rows(mod_ref, 2 * chip + 1 - core, core)]
    for head, refs in (
        (chip, (stay, stay_o)),
        ((chip + 2) % RING, (far, far_o)),
        ((chip + 1 + 2 * core) % RING, (pair.at[0], pair.at[1])),
        ((chip + 3 + 2 * core) % RING, (pair_o.at[1], pair_o.at[0])),
    ):

        @pl.when(head < NH)
        def _():
            for block, x_ref in enumerate(refs):
                x = x_ref[...]
                zero = jnp.zeros_like(x)
                for side in range(2):
                    kept = jnp.where(mine[block] == 1.0 - side, x, zero)
                    for c in range(3):
                        lo = pl.multiple_of(((side * 3 + c) * NH + head) * HD, HD)
                        out_ref[block * rows : (block + 1) * rows, pl.ds(lo, HD)] = kept[:, c * HD : (c + 1) * HD]


def weight_copies(place_ref, own_hbm, other_hbm, to_ref, sem, hop):
    core = place_ref[RING * RING]
    copies = []
    for j in range(RING):
        dest = place_ref[hop * RING + j]
        copies.append(pltpu.make_async_copy(own_hbm.at[:, dest, core], to_ref.at[0, :, j], sem.at[0, j]))
        copies.append(pltpu.make_async_copy(other_hbm.at[:, dest], to_ref.at[1, :, j], sem.at[1, j]))
    return copies


def fetch_kernel(hops, place_ref, after_ref, own_hbm, other_hbm, *refs):
    copies = []
    for i, hop in enumerate(hops):
        copies += weight_copies(place_ref, own_hbm, other_hbm, refs[i], refs[len(hops) + i], hop)
    for copy in copies:
        copy.start()
    for copy in copies:
        copy.wait()


def fetch_weights(place, after, w5, other_half, hops):
    vmem = pl.BlockSpec(memory_space=pltpu.VMEM)
    hbm = pl.BlockSpec(memory_space=pltpu.HBM)
    anywhere = pl.BlockSpec(memory_space=pl.ANY)
    return pl.pallas_call(
        functools.partial(fetch_kernel, hops),
        in_specs=[pl.BlockSpec(memory_space=pltpu.SMEM), vmem, hbm, anywhere],
        out_specs=[vmem for _ in hops],
        out_shape=[pltpu.VMEM((2, 3, RING) + w5.shape[3:], jnp.bfloat16) for _ in hops],
        scratch_shapes=[pltpu.SemaphoreType.DMA((2, RING)) for _ in hops],
        compiler_params=pltpu.CompilerParams(vmem_limit_bytes=20 * MIB),
        cost_estimate=pl.CostEstimate(flops=10**6, bytes_accessed=10**7, transcendentals=0),
        name="fetch_weights",
    )(place, after, w5, other_half)


def product(g_ref, w_ref, out_ref, j, count):
    cols = w_ref.shape[3]
    w = [w_ref[side, c, j : j + count].reshape(count * cols, NH * HD) for side in range(2) for c in range(3)]
    res = lax.dot_general(
        g_ref[...], jnp.concatenate(w, axis=1), (((1,), (1,)), ((), ())), preferred_element_type=jnp.float32
    ).astype(jnp.bfloat16)
    for i in range(count):
        out_ref[j + i] = res[:, i * cols : (i + 1) * cols]


def back_first_kernel(following, place_ref, mod_ref, *refs):
    *parts, w_ref, own_hbm, other_hbm, out_ref, g_ref, next_ref, sem = refs
    for copy in weight_copies(place_ref, own_hbm, other_hbm, next_ref, sem, following):
        copy.start()
    gather((place_ref[RING * RING + 1], place_ref[RING * RING]), mod_ref, parts, g_ref)
    product(g_ref, w_ref, out_ref, 0, RING)
    for copy in weight_copies(place_ref, own_hbm, other_hbm, next_ref, sem, following):
        copy.wait()


def back_middle_kernel(g_ref, w_ref, out_ref):
    product(g_ref, w_ref, out_ref, 0, RING)


def back_last_kernel(hop, place_ref, g_ref, own_hbm, other_hbm, out_ref, w_s, sem):
    copies = weight_copies(place_ref, own_hbm, other_hbm, w_s, sem, hop)
    for copy in copies:
        copy.start()
    for j in range(0, RING, 2):
        for copy in copies[2 * j : 2 * j + 4]:
            copy.wait()
        product(g_ref, w_s, out_ref, j, 2)


def back_call(kernel, operands, in_specs, out_shape, scratch):
    vmem = pl.BlockSpec(memory_space=pltpu.VMEM)
    return pl.pallas_call(
        kernel,
        in_specs=in_specs,
        out_specs=[vmem] * len(out_shape),
        out_shape=out_shape,
        scratch_shapes=scratch,
        compiler_params=pltpu.CompilerParams(vmem_limit_bytes=24 * MIB),
        cost_estimate=pl.CostEstimate(flops=10**6, bytes_accessed=10**4, transcendentals=0),
        name="back",
    )(*operands)


def back_products(place, mod, parts, weights, w5, other_half, send):
    rows = 2 * parts[0].shape[0]
    cols = w5.shape[3]
    smem = pl.BlockSpec(memory_space=pltpu.SMEM)
    vmem = pl.BlockSpec(memory_space=pltpu.VMEM)
    hbm = pl.BlockSpec(memory_space=pltpu.HBM)
    anywhere = pl.BlockSpec(memory_space=pl.ANY)
    piece = jax.ShapeDtypeStruct((RING, rows, cols), jnp.bfloat16)
    w_shape = (2, 3, RING) + w5.shape[3:]
    sem = pltpu.SemaphoreType.DMA((2, RING))
    w_two, w_one = weights
    x, g, w_three = back_call(
        functools.partial(back_first_kernel, 3),
        (place, mod, *parts, w_two, w5, other_half),
        [smem] + [vmem] * 8 + [hbm, anywhere],
        [piece, pltpu.VMEM((rows, 18 * HD), jnp.bfloat16), pltpu.VMEM(w_shape, jnp.bfloat16)],
        [sem],
    )
    g = pltpu.with_memory_space_constraint(g, pltpu.VMEM)
    w_three = pltpu.with_memory_space_constraint(w_three, pltpu.VMEM)
    pieces = {2: send(x, 2)}
    for hop, w in ((1, w_one), (3, w_three)):
        (x,) = back_call(back_middle_kernel, (g, w), [vmem, vmem], [piece], [])
        pieces[hop] = send(x, hop)
    (pieces[0],) = back_call(
        functools.partial(back_last_kernel, 0),
        (place, g, w5, other_half),
        [smem, vmem, hbm, anywhere],
        [piece],
        [pltpu.VMEM(w_shape, jnp.bfloat16), sem],
    )
    return pieces


def ring_perm(first, hop):
    pairs = []
    for s in range(RING):
        for m in range(2):
            for y in range(RING):
                for z in range(RING):
                    if (m == 0) == first:
                        to = (y, (z + hop) % RING)
                    else:
                        to = ((y + hop) % RING, z)
                    base = (s * 2 + m) * RING * RING
                    pairs.append((base + y * RING + z, base + to[0] * RING + to[1]))
    return pairs


def pair_perm(step):
    pairs = []
    for s in range(RING):
        for m in range(2):
            head = (s + (1 if m == 0 else -1)) % RING
            if step > 0 and head < NH:
                pairs.append((2 * s + m, 2 * head + m))
            if step < 0 and s < NH:
                pairs.append((2 * s + m, 2 * ((s + (-1 if m == 0 else 1)) % RING) + m))
    return pairs


def per_device(activations, grad_attn, weights, modality):
    rows, depth = activations.shape
    chip = lax.axis_index("seq")
    core = lax.axis_index("mod")
    tp = lax.axis_index("tp")
    where = jnp.stack([chip, core]).astype(jnp.int32)
    dests = RING * RING
    cols = depth // dests // 2
    w5 = jnp.transpose(weights[0], (1, 0, 2)).reshape(3, dests, 2, cols, NH * HD)

    mod = modality.reshape(2 * RING, rows)
    w5 = pltpu.with_memory_space_constraint(w5, pltpu.HBM)
    activations = pltpu.with_memory_space_constraint(activations, pltpu.HBM)
    act_other = pltpu.with_memory_space_constraint(core_swap(activations), pltpu.VMEM)
    part, w_early = project_own(activations, w5, 4)
    w_early = pltpu.with_memory_space_constraint(w_early, pltpu.VMEM)
    proj_own, sent, half = project(where, part, activations, act_other, w_early, w5, grad_attn)
    got = core_swap(sent)
    got, half = lax.optimization_barrier((got, half))
    other_half = core_swap(half)

    def part_shapes(width):
        block = jax.ShapeDtypeStruct((rows, width), jnp.bfloat16)
        return [jax.ShapeDtypeStruct((2, rows, width), jnp.bfloat16), block, block]

    pair, far, stay = small_call(
        route_kernel, "route", where, (mod, proj_own, sent, got, grad_attn), part_shapes(4 * HD)
    )
    pair = lax.ppermute(pair, ("seq", "mod"), pair_perm(1))
    far = lax.ppermute(far, "seq", [(i, (i + 2) % RING) for i in range(RING) if (i + 2) % RING < NH])
    parts = [stay, far, pair]
    keep, send = attention(where, parts + [core_swap(x) for x in parts])
    pair, far, stay = small_call(combine_kernel, "combine", where, (keep, core_swap(send)), part_shapes(3 * HD))

    i = jnp.arange(dests, dtype=jnp.int32) // RING
    j = jnp.arange(dests, dtype=jnp.int32) % RING
    y, z = tp // RING, tp % RING
    place = jnp.where(
        core == 0,
        (y + j) % RING * RING + (z + i) % RING,
        (y + i) % RING * RING + (z + j) % RING,
    )
    place = jnp.concatenate([place, jnp.stack([core, chip])]).astype(jnp.int32)

    w_first = fetch_weights(place, stay, w5, other_half, (2, 1))
    w_first = [pltpu.with_memory_space_constraint(w, pltpu.VMEM) for w in w_first]
    pair = lax.ppermute(pair, ("seq", "mod"), pair_perm(-1))
    far = lax.ppermute(far, "seq", [(i, (i + 2) % RING) for i in range(NH)])
    pair, far, w_first = lax.optimization_barrier((pair, far, w_first))
    parts = [stay, far, pair]
    parts += [core_swap(x) for x in parts]

    pieces = back_products(
        place,
        mod,
        parts,
        w_first,
        w5,
        other_half,
        lambda x, hop: lax.ppermute(x, AXES, ring_perm(True, hop)),
    )
    total = pieces[0].astype(jnp.float32)
    for hop in (2, 1, 3):
        total = lax.optimization_barrier(total) + pieces[hop].astype(jnp.float32)
    result = total[0]
    for hop in (2, 1, 3):
        got = lax.ppermute(total[hop].astype(jnp.bfloat16), AXES, ring_perm(False, hop))
        result = result + got.astype(jnp.float32)
    result = result.astype(jnp.bfloat16)
    mine = result[:rows]
    theirs = core_swap(result[rows:])
    return jnp.where(
        core == 0, jnp.concatenate([mine, theirs], axis=1), jnp.concatenate([theirs, mine], axis=1)
    )


def solution(mesh):
    in_specs = (P(("seq", "mod"), None), P(("seq", "mod"), "tp"), P("mod", None, None, "tp"), P())
    out_specs = P(("seq", "mod"), "tp")
    return jax.shard_map(
        per_device, mesh=mesh, in_specs=in_specs, out_specs=out_specs, check_vma=False
    )
```

```python
import functools

import jax
import jax.numpy as jnp
from jax import lax
from jax.experimental import pallas as pl
from jax.experimental.pallas import tpu as pltpu
from jax.sharding import PartitionSpec as P

HD = 128
NH = 3
RING = 4
SCALE = HD**-0.5
AXES = ("seq", "mod", "tp")
MIB = 1024 * 1024


def core_swap(x):
    return lax.ppermute(x, "mod", [(0, 1), (1, 0)])


def weight_block(w_ref, i):
    size = 4 * w_ref.shape[3]
    return jnp.concatenate([w_ref[c, 2 * i : 2 * i + 2].reshape(size, NH * HD) for c in range(3)], axis=1)


def own_kernel(where_ref, place_ref, mod_ref, a_hbm, w_hbm, part_ref, w_ref, a_s, a_sem, w_sem):
    chunks = w_ref.shape[1] // 2
    block = 4 * w_ref.shape[3]

    def fetch(i):
        pair = slice(2 * i, 2 * i + 2)
        return (
            pltpu.make_async_copy(a_hbm.at[:, pl.ds(i * block, block)], a_s.at[i], a_sem.at[i]),
            pltpu.make_async_copy(w_hbm.at[:, pair], w_ref.at[:, pair], w_sem.at[i]),
        )

    for i in range(chunks):
        for copy in fetch(i):
            copy.start()
    for i in range(chunks):
        for copy in fetch(i):
            copy.wait()
        part = jnp.dot(a_s[i], weight_block(w_ref, i), preferred_element_type=jnp.float32)
        if i == 0:
            part_ref[...] = part
        else:
            part_ref[...] += part


def project_own(small, a, w5, early):
    rows = a.shape[0]
    block = 4 * w5.shape[3]
    smem = pl.BlockSpec(memory_space=pltpu.SMEM)
    vmem = pl.BlockSpec(memory_space=pltpu.VMEM)
    hbm = pl.BlockSpec(memory_space=pltpu.HBM)
    return pl.pallas_call(
        own_kernel,
        in_specs=[smem, smem, vmem, hbm, hbm],
        out_specs=[vmem, vmem],
        out_shape=[
            jax.ShapeDtypeStruct((rows, 9 * HD), jnp.float32),
            pltpu.VMEM((3, 2 * early) + w5.shape[2:], jnp.bfloat16),
        ],
        scratch_shapes=[
            pltpu.VMEM((early, rows, block), jnp.bfloat16),
            pltpu.SemaphoreType.DMA((early,)),
            pltpu.SemaphoreType.DMA((early,)),
        ],
        compiler_params=pltpu.CompilerParams(vmem_limit_bytes=20 * MIB),
        cost_estimate=pl.CostEstimate(flops=4 * 10**9, bytes_accessed=10**7, transcendentals=0),
        name="project_own",
    )(*small, a, w5)


def project_kernel(
    early, where_ref, part_ref, own_hbm, oth_ref, w_ref, w_hbm, g_ref, own_out, send_out, half_hbm, a_s, w_s, acc_ref,
    own_sem, w_sem, half_sem
):
    rows = part_ref.shape[0]
    chunks = half_hbm.shape[1] // 2
    block = 4 * w_ref.shape[3]
    side = 1 - where_ref[1]

    def fetch_own(i):
        return pltpu.make_async_copy(own_hbm.at[:, pl.ds(i * block, block)], a_s.at[i - early], own_sem.at[i])

    def other(i):
        return oth_ref[:, i * block : (i + 1) * block]

    def fetch_weights(i):
        src = w_hbm.at[:, 2 * i : 2 * i + 2]
        return pltpu.make_async_copy(src, w_s.at[:, 2 * (i - early) : 2 * (i - early) + 2], w_sem.at[i])

    def put_half(i):
        if i < early:
            src = w_ref.at[:, 2 * i : 2 * i + 2, side]
        else:
            src = w_s.at[:, 2 * (i - early) : 2 * (i - early) + 2, side]
        return pltpu.make_async_copy(src, half_hbm.at[:, 2 * i : 2 * i + 2], half_sem.at[i])

    for i in range(early, chunks):
        fetch_weights(i).start()
        fetch_own(i).start()
    for i in range(early):
        put_half(i).start()
    acc_ref[0:rows] = part_ref[...]
    for i in range(chunks):
        if i < early:
            part = jnp.dot(other(i), weight_block(w_ref, i), preferred_element_type=jnp.float32)
            if i == 0:
                acc_ref[rows:] = part
            else:
                acc_ref[rows:] += part
        else:
            fetch_own(i).wait()
            fetch_weights(i).wait()
            put_half(i).start()
            a = jnp.concatenate([a_s[i - early], other(i)], axis=0)
            acc_ref[...] += jnp.dot(a, weight_block(w_s, i - early), preferred_element_type=jnp.float32)
    for h in range(NH):
        for c in range(3):
            lo = c * NH * HD + h * HD
            to = slice((h * 3 + c) * HD, (h * 3 + c + 1) * HD)
            x = acc_ref[:, lo : lo + HD].astype(jnp.bfloat16)
            own_out[:, to] = x[0:rows]
            send_out[:, to] = x[rows:]
    theirs = pair_head(where_ref[0], side)
    send_out[:, 9 * HD : 12 * HD] = own_out[:, head_columns(theirs, 3)]
    send_out[:, 12 * HD :] = g_ref[:, head_columns(theirs, 1)]
    for i in range(chunks):
        put_half(i).wait()


def project(where, part, own, other, w_early, w5, g):
    rows, depth = own.shape
    chunks = w5.shape[1] // 2
    early = w_early.shape[1] // 2
    vmem = pl.BlockSpec(memory_space=pltpu.VMEM)
    hbm = pl.BlockSpec(memory_space=pltpu.HBM)
    dma = pltpu.SemaphoreType.DMA((chunks,))
    return pl.pallas_call(
        functools.partial(project_kernel, early),
        in_specs=[pl.BlockSpec(memory_space=pltpu.SMEM), vmem, hbm, vmem, vmem, hbm, vmem],
        out_specs=[vmem, vmem, hbm],
        out_shape=[
            jax.ShapeDtypeStruct((rows, 9 * HD), jnp.bfloat16),
            jax.ShapeDtypeStruct((rows, 13 * HD), jnp.bfloat16),
            pltpu.HBM((3,) + w5.shape[1:2] + w5.shape[3:], jnp.bfloat16),
        ],
        scratch_shapes=[
            pltpu.VMEM((chunks - early, rows, depth // chunks), jnp.bfloat16),
            pltpu.VMEM((3, 2 * (chunks - early)) + w5.shape[2:], jnp.bfloat16),
            pltpu.VMEM((2 * rows, 9 * HD), jnp.float32),
            dma,
            dma,
            dma,
        ],
        compiler_params=pltpu.CompilerParams(vmem_limit_bytes=26 * MIB),
        cost_estimate=pl.CostEstimate(flops=7 * 10**9, bytes_accessed=10**7, transcendentals=0),
        name="project",
    )(where, part, own, other, w_early, w5, g)


def pair_head(chip, core):
    return jnp.minimum((chip + 1 + 2 * core) % RING, NH - 1)


def head_columns(head, width):
    return pl.ds(pl.multiple_of(head * (width * HD), width * HD), width * HD)


def section_rows(mod_ref, block, core):
    rows = mod_ref.shape[1]
    mine = (mod_ref[pl.ds(block, 1), :] == core).astype(jnp.float32)
    row = lax.broadcasted_iota(jnp.int32, (rows, rows), 0)
    col = lax.broadcasted_iota(jnp.int32, (rows, rows), 1)
    return jnp.sum(jnp.where(row == col, mine, 0.0), axis=1, keepdims=True)


def route_kernel(where_ref, mod_ref, own_ref, sent_ref, got_ref, g_ref, pair_out, far_out, stay_out):
    chip, core = where_ref[0], where_ref[1]
    mine = section_rows(mod_ref, 2 * chip + core, core) > 0
    others = section_rows(mod_ref, 2 * chip + 1 - core, core) > 0

    def own_rows(head):
        cols = head_columns(head, 3)
        return jnp.where(mine, own_ref[:, cols], got_ref[:, cols]), g_ref[:, head_columns(head, 1)]

    head = pair_head(chip, core)
    pair_out[0, :, : 3 * HD], pair_out[0, :, 3 * HD :] = own_rows(head)
    pair_out[1, :, : 3 * HD] = jnp.where(others, sent_ref[:, head_columns(head, 3)], got_ref[:, 9 * HD : 12 * HD])
    pair_out[1, :, 3 * HD :] = got_ref[:, 12 * HD :]
    far_out[:, : 3 * HD], far_out[:, 3 * HD :] = own_rows(jnp.minimum((chip + 2) % RING, NH - 1))
    stay_out[:, : 3 * HD], stay_out[:, 3 * HD :] = own_rows(jnp.minimum(chip, NH - 1))


def small_call(kernel, name, where, operands, out_shape):
    vmem = pl.BlockSpec(memory_space=pltpu.VMEM)
    return pl.pallas_call(
        kernel,
        in_specs=[pl.BlockSpec(memory_space=pltpu.SMEM)] + [vmem] * len(operands),
        out_specs=[vmem] * len(out_shape),
        out_shape=out_shape,
        compiler_params=pltpu.CompilerParams(vmem_limit_bytes=16 * MIB),
        cost_estimate=pl.CostEstimate(flops=10**6, bytes_accessed=3 * 10**6, transcendentals=0),
        name=name,
    )(where, *operands)


def attention_kernel(
    where_ref, stay, far, pair, stay_o, far_o, pair_o, keep_ref, send_ref, q_s, g_s, k_s, v_s, dq_s, dk_s, dv_s
):
    chip = where_ref[0]
    core = where_ref[1]
    rows = stay.shape[0]
    both = 2 * rows
    near = (chip + 3 + 2 * core) % RING
    across = (chip + 1 + 2 * core) % RING
    opposite = (chip + 2) % RING

    def block_rows(shard, side):
        return pl.ds(pl.multiple_of((2 * shard + side) * rows, rows), rows)

    for shard, r, o in (
        (chip, stay, stay_o),
        (opposite, far, far_o),
        (near, pair.at[0], pair.at[1]),
        (across, pair_o.at[1], pair_o.at[0]),
    ):
        q_s[shard] = r[:, 0:HD]
        g_s[shard] = r[:, 3 * HD : 4 * HD]
        k_s[block_rows(shard, core), :] = r[:, HD : 2 * HD]
        v_s[block_rows(shard, core), :] = r[:, 2 * HD : 3 * HD]
        k_s[block_rows(shard, 1 - core), :] = o[:, HD : 2 * HD]
        v_s[block_rows(shard, 1 - core), :] = o[:, 2 * HD : 3 * HD]
    nt = (((1,), (1,)), ((), ()))
    tn = (((0,), (0,)), ((), ()))
    for s in range(RING - 1, -1, -1):
        width = both * (s + 1)
        q = q_s[s]
        g = g_s[s]
        kk = k_s[0:width, :]
        vv = v_s[0:width, :]
        scores = lax.dot_general(q, kk, nt, preferred_element_type=jnp.float32) * SCALE
        row = lax.broadcasted_iota(jnp.int32, (rows, width), 0) + (2 * s + core) * rows
        col = lax.broadcasted_iota(jnp.int32, (rows, width), 1)
        scores = jnp.where(col <= row, scores, -jnp.inf)
        lifted = jnp.exp(scores - jnp.max(scores, axis=1, keepdims=True))
        probs = lifted / jnp.sum(lifted, axis=1, keepdims=True)
        low = probs.astype(jnp.bfloat16)
        dprobs = lax.dot_general(g, vv, nt, preferred_element_type=jnp.float32)
        row_dot = jnp.sum(probs * dprobs, axis=1, keepdims=True)
        ds = (probs * (dprobs - row_dot)).astype(jnp.bfloat16)
        dq = jnp.dot(ds, kk, preferred_element_type=jnp.float32) * SCALE
        dk = lax.dot_general(ds, q, tn, preferred_element_type=jnp.float32) * SCALE
        dv = lax.dot_general(low, g, tn, preferred_element_type=jnp.float32)
        if s == RING - 1:
            dk_s[...] = dk
            dv_s[...] = dv
        else:
            dk_s[0:width, :] += dk
            dv_s[0:width, :] += dv
        dq_s[s] = dq
    col = 0
    for shard, whole in ((near, True), (near, False), (chip, True), (opposite, True)):
        if whole:
            keep_ref[:, col : col + HD] = dq_s[shard]
            col += HD
        side = core if whole else 1 - core
        keep_ref[:, col : col + HD] = dk_s[block_rows(shard, side), :]
        keep_ref[:, col + HD : col + 2 * HD] = dv_s[block_rows(shard, side), :]
        col += 2 * HD
    col = 0
    for shard, whole in ((across, True), (across, False), (chip, False), (opposite, False)):
        if whole:
            send_ref[:, col : col + HD] = dq_s[shard].astype(jnp.bfloat16)
            col += HD
        side = core if whole else 1 - core
        send_ref[:, col : col + HD] = dk_s[block_rows(shard, side), :].astype(jnp.bfloat16)
        send_ref[:, col + HD : col + 2 * HD] = dv_s[block_rows(shard, side), :].astype(jnp.bfloat16)
        col += 2 * HD


def attention(where, parts):
    rows = parts[0].shape[0]
    total = 2 * RING * rows
    vmem = pl.BlockSpec(memory_space=pltpu.VMEM)
    return pl.pallas_call(
        attention_kernel,
        in_specs=[pl.BlockSpec(memory_space=pltpu.SMEM)] + [vmem] * 6,
        out_specs=[vmem, vmem],
        out_shape=[
            jax.ShapeDtypeStruct((rows, 11 * HD), jnp.float32),
            jax.ShapeDtypeStruct((rows, 9 * HD), jnp.bfloat16),
        ],
        scratch_shapes=[
            pltpu.VMEM((RING, rows, HD), jnp.bfloat16),
            pltpu.VMEM((RING, rows, HD), jnp.bfloat16),
            pltpu.VMEM((total, HD), jnp.bfloat16),
            pltpu.VMEM((total, HD), jnp.bfloat16),
            pltpu.VMEM((RING, rows, HD), jnp.float32),
            pltpu.VMEM((total, HD), jnp.float32),
            pltpu.VMEM((total, HD), jnp.float32),
        ],
        compiler_params=pltpu.CompilerParams(vmem_limit_bytes=32 * MIB),
        cost_estimate=pl.CostEstimate(flops=10**9, bytes_accessed=4 * 10**6, transcendentals=10**6),
        name="attention",
    )(where, *parts)


def combine_kernel(where_ref, keep, got, pair_out, far_out, stay_out):
    def put(out, query, kept, partner):
        out[:, 0:HD] = query.astype(jnp.bfloat16)
        kv = keep[:, kept : kept + 2 * HD] + got[:, partner : partner + 2 * HD].astype(jnp.float32)
        out[:, HD : 3 * HD] = kv.astype(jnp.bfloat16)

    put(pair_out.at[0], keep[:, 0:HD], HD, 3 * HD)
    put(pair_out.at[1], got[:, 0:HD], 3 * HD, HD)
    put(stay_out, keep[:, 5 * HD : 6 * HD], 6 * HD, 5 * HD)
    put(far_out, keep[:, 8 * HD : 9 * HD], 9 * HD, 7 * HD)


def gather(where, mod_ref, parts, out_ref):
    chip, core = where
    stay, far, pair, stay_o, far_o, pair_o = parts
    rows = stay.shape[0]
    mine = [section_rows(mod_ref, 2 * chip + core, core), section_rows(mod_ref, 2 * chip + 1 - core, core)]
    for head, refs in (
        (chip, (stay, stay_o)),
        ((chip + 2) % RING, (far, far_o)),
        ((chip + 1 + 2 * core) % RING, (pair.at[0], pair.at[1])),
        ((chip + 3 + 2 * core) % RING, (pair_o.at[1], pair_o.at[0])),
    ):

        @pl.when(head < NH)
        def _():
            for block, x_ref in enumerate(refs):
                x = x_ref[...]
                zero = jnp.zeros_like(x)
                for side in range(2):
                    kept = jnp.where(mine[block] == 1.0 - side, x, zero)
                    for c in range(3):
                        lo = pl.multiple_of(((side * 3 + c) * NH + head) * HD, HD)
                        out_ref[block * rows : (block + 1) * rows, pl.ds(lo, HD)] = kept[:, c * HD : (c + 1) * HD]


def weight_copies(place_ref, own_hbm, other_hbm, to_ref, sem, hop):
    core = place_ref[RING * RING]
    copies = []
    for j in range(RING):
        dest = place_ref[hop * RING + j]
        copies.append(pltpu.make_async_copy(own_hbm.at[:, dest, core], to_ref.at[0, :, j], sem.at[0, j]))
        copies.append(pltpu.make_async_copy(other_hbm.at[:, dest], to_ref.at[1, :, j], sem.at[1, j]))
    return copies


def fetch_kernel(hops, place_ref, after_ref, own_hbm, other_hbm, *refs):
    copies = []
    for i, hop in enumerate(hops):
        copies += weight_copies(place_ref, own_hbm, other_hbm, refs[i], refs[len(hops) + i], hop)
    for copy in copies:
        copy.start()
    for copy in copies:
        copy.wait()


def fetch_weights(place, after, w5, other_half, hops):
    vmem = pl.BlockSpec(memory_space=pltpu.VMEM)
    hbm = pl.BlockSpec(memory_space=pltpu.HBM)
    anywhere = pl.BlockSpec(memory_space=pl.ANY)
    return pl.pallas_call(
        functools.partial(fetch_kernel, hops),
        in_specs=[pl.BlockSpec(memory_space=pltpu.SMEM), vmem, hbm, anywhere],
        out_specs=[vmem for _ in hops],
        out_shape=[pltpu.VMEM((2, 3, RING) + w5.shape[3:], jnp.bfloat16) for _ in hops],
        scratch_shapes=[pltpu.SemaphoreType.DMA((2, RING)) for _ in hops],
        compiler_params=pltpu.CompilerParams(vmem_limit_bytes=20 * MIB),
        cost_estimate=pl.CostEstimate(flops=10**6, bytes_accessed=10**7, transcendentals=0),
        name="fetch_weights",
    )(place, after, w5, other_half)


def product(g_ref, w_ref, out_ref, j, count):
    cols = w_ref.shape[3]
    w = [w_ref[side, c, j : j + count].reshape(count * cols, NH * HD) for side in range(2) for c in range(3)]
    res = lax.dot_general(
        g_ref[...], jnp.concatenate(w, axis=1), (((1,), (1,)), ((), ())), preferred_element_type=jnp.float32
    ).astype(jnp.bfloat16)
    for i in range(count):
        out_ref[j + i] = res[:, i * cols : (i + 1) * cols]


def back_first_kernel(following, place_ref, mod_ref, *refs):
    *parts, w_ref, own_hbm, other_hbm, out_ref, g_ref, next_ref, sem = refs
    for copy in weight_copies(place_ref, own_hbm, other_hbm, next_ref, sem, following):
        copy.start()
    gather((place_ref[RING * RING + 1], place_ref[RING * RING]), mod_ref, parts, g_ref)
    product(g_ref, w_ref, out_ref, 0, RING)
    for copy in weight_copies(place_ref, own_hbm, other_hbm, next_ref, sem, following):
        copy.wait()


def back_middle_kernel(g_ref, w_ref, out_ref):
    product(g_ref, w_ref, out_ref, 0, RING)


def back_last_kernel(hop, place_ref, g_ref, own_hbm, other_hbm, out_ref, w_s, sem):
    copies = weight_copies(place_ref, own_hbm, other_hbm, w_s, sem, hop)
    for copy in copies:
        copy.start()
    for j in range(0, RING, 2):
        for copy in copies[2 * j : 2 * j + 4]:
            copy.wait()
        product(g_ref, w_s, out_ref, j, 2)


def back_call(kernel, operands, in_specs, out_shape, scratch):
    vmem = pl.BlockSpec(memory_space=pltpu.VMEM)
    return pl.pallas_call(
        kernel,
        in_specs=in_specs,
        out_specs=[vmem] * len(out_shape),
        out_shape=out_shape,
        scratch_shapes=scratch,
        compiler_params=pltpu.CompilerParams(vmem_limit_bytes=24 * MIB),
        cost_estimate=pl.CostEstimate(flops=10**6, bytes_accessed=10**4, transcendentals=0),
        name="back",
    )(*operands)


def back_products(place, mod, parts, weights, w5, other_half, send):
    rows = 2 * parts[0].shape[0]
    cols = w5.shape[3]
    smem = pl.BlockSpec(memory_space=pltpu.SMEM)
    vmem = pl.BlockSpec(memory_space=pltpu.VMEM)
    hbm = pl.BlockSpec(memory_space=pltpu.HBM)
    anywhere = pl.BlockSpec(memory_space=pl.ANY)
    piece = jax.ShapeDtypeStruct((RING, rows, cols), jnp.bfloat16)
    w_shape = (2, 3, RING) + w5.shape[3:]
    sem = pltpu.SemaphoreType.DMA((2, RING))
    w_two, w_one = weights
    x, g, w_three = back_call(
        functools.partial(back_first_kernel, 3),
        (place, mod, *parts, w_two, w5, other_half),
        [smem] + [vmem] * 8 + [hbm, anywhere],
        [piece, pltpu.VMEM((rows, 18 * HD), jnp.bfloat16), pltpu.VMEM(w_shape, jnp.bfloat16)],
        [sem],
    )
    g = pltpu.with_memory_space_constraint(g, pltpu.VMEM)
    w_three = pltpu.with_memory_space_constraint(w_three, pltpu.VMEM)
    pieces = {2: send(x, 2)}
    for hop, w in ((1, w_one), (3, w_three)):
        (x,) = back_call(back_middle_kernel, (g, w), [vmem, vmem], [piece], [])
        pieces[hop] = send(x, hop)
    (pieces[0],) = back_call(
        functools.partial(back_last_kernel, 0),
        (place, g, w5, other_half),
        [smem, vmem, hbm, anywhere],
        [piece],
        [pltpu.VMEM(w_shape, jnp.bfloat16), sem],
    )
    return pieces


def ring_perm(first, hop):
    pairs = []
    for s in range(RING):
        for m in range(2):
            for y in range(RING):
                for z in range(RING):
                    if (m == 0) == first:
                        to = (y, (z + hop) % RING)
                    else:
                        to = ((y + hop) % RING, z)
                    base = (s * 2 + m) * RING * RING
                    pairs.append((base + y * RING + z, base + to[0] * RING + to[1]))
    return pairs


def pair_perm(step):
    pairs = []
    for s in range(RING):
        for m in range(2):
            head = (s + (1 if m == 0 else -1)) % RING
            if step > 0 and head < NH:
                pairs.append((2 * s + m, 2 * head + m))
            if step < 0 and s < NH:
                pairs.append((2 * s + m, 2 * ((s + (-1 if m == 0 else 1)) % RING) + m))
    return pairs


def per_device(activations, grad_attn, weights, modality):
    rows, depth = activations.shape
    chip = lax.axis_index("seq")
    core = lax.axis_index("mod")
    tp = lax.axis_index("tp")
    where = jnp.stack([chip, core]).astype(jnp.int32)
    dests = RING * RING
    cols = depth // dests // 2
    w5 = jnp.transpose(weights[0], (1, 0, 2)).reshape(3, dests, 2, cols, NH * HD)

    mod = modality.reshape(2 * RING, rows)
    w5 = pltpu.with_memory_space_constraint(w5, pltpu.HBM)
    activations = pltpu.with_memory_space_constraint(activations, pltpu.HBM)
    i = jnp.arange(dests, dtype=jnp.int32) // RING
    j = jnp.arange(dests, dtype=jnp.int32) % RING
    y, z = tp // RING, tp % RING
    place = jnp.where(
        core == 0,
        (y + j) % RING * RING + (z + i) % RING,
        (y + i) % RING * RING + (z + j) % RING,
    )
    place = jnp.concatenate([place, jnp.stack([core, chip])]).astype(jnp.int32)

    act_other = pltpu.with_memory_space_constraint(core_swap(activations), pltpu.VMEM)
    part, w_early = project_own((where, place, mod), activations, w5, 4)
    w_early = pltpu.with_memory_space_constraint(w_early, pltpu.VMEM)
    proj_own, sent, half = project(where, part, activations, act_other, w_early, w5, grad_attn)
    got = core_swap(sent)
    got, half = lax.optimization_barrier((got, half))
    other_half = core_swap(half)

    def part_shapes(width):
        block = jax.ShapeDtypeStruct((rows, width), jnp.bfloat16)
        return [jax.ShapeDtypeStruct((2, rows, width), jnp.bfloat16), block, block]

    pair, far, stay = small_call(
        route_kernel, "route", where, (mod, proj_own, sent, got, grad_attn), part_shapes(4 * HD)
    )
    pair = lax.ppermute(pair, ("seq", "mod"), pair_perm(1))
    far = lax.ppermute(far, "seq", [(i, (i + 2) % RING) for i in range(RING) if (i + 2) % RING < NH])
    parts = [stay, far, pair]
    keep, send = attention(where, parts + [core_swap(x) for x in parts])
    pair, far, stay = small_call(combine_kernel, "combine", where, (keep, core_swap(send)), part_shapes(3 * HD))

    w_first = fetch_weights(place, stay, w5, other_half, (2, 1))
    w_first = [pltpu.with_memory_space_constraint(w, pltpu.VMEM) for w in w_first]
    pair = lax.ppermute(pair, ("seq", "mod"), pair_perm(-1))
    far = lax.ppermute(far, "seq", [(i, (i + 2) % RING) for i in range(NH)])
    pair, far, w_first = lax.optimization_barrier((pair, far, w_first))
    parts = [stay, far, pair]
    parts += [core_swap(x) for x in parts]

    pieces = back_products(
        place,
        mod,
        parts,
        w_first,
        w5,
        other_half,
        lambda x, hop: lax.ppermute(x, AXES, ring_perm(True, hop)),
    )
    total = pieces[0].astype(jnp.float32)
    for hop in (2, 1, 3):
        total = lax.optimization_barrier(total) + pieces[hop].astype(jnp.float32)
    result = total[0]
    for hop in (2, 1, 3):
        got = lax.ppermute(total[hop].astype(jnp.bfloat16), AXES, ring_perm(False, hop))
        result = result + got.astype(jnp.float32)
    result = result.astype(jnp.bfloat16)
    mine = result[:rows]
    theirs = core_swap(result[rows:])
    return jnp.where(
        core == 0, jnp.concatenate([mine, theirs], axis=1), jnp.concatenate([theirs, mine], axis=1)
    )


def solution(mesh):
    in_specs = (P(("seq", "mod"), None), P(("seq", "mod"), "tp"), P("mod", None, None, "tp"), P())
    out_specs = P(("seq", "mod"), "tp")
    return jax.shard_map(
        per_device, mesh=mesh, in_specs=in_specs, out_specs=out_specs, check_vma=False
    )
```

```python
import functools

import jax
import jax.numpy as jnp
from jax import lax
from jax.experimental import pallas as pl
from jax.experimental.pallas import tpu as pltpu
from jax.sharding import PartitionSpec as P

HD = 128
NH = 3
RING = 4
SCALE = HD**-0.5
AXES = ("seq", "mod", "tp")
MIB = 1024 * 1024


def core_swap(x):
    return lax.ppermute(x, "mod", [(0, 1), (1, 0)])


def weight_block(w_ref, i):
    size = 4 * w_ref.shape[3]
    return jnp.concatenate([w_ref[c, 2 * i : 2 * i + 2].reshape(size, NH * HD) for c in range(3)], axis=1)


def own_kernel(a_hbm, w_hbm, part_ref, w_ref, a_s, a_sem, w_sem):
    chunks = w_ref.shape[1] // 2
    block = 4 * w_ref.shape[3]

    def fetch(i):
        pair = slice(2 * i, 2 * i + 2)
        return (
            pltpu.make_async_copy(a_hbm.at[:, pl.ds(i * block, block)], a_s.at[i], a_sem.at[i]),
            pltpu.make_async_copy(w_hbm.at[:, pair], w_ref.at[:, pair], w_sem.at[i]),
        )

    for i in range(chunks):
        for copy in fetch(i):
            copy.start()
    for i in range(chunks):
        for copy in fetch(i):
            copy.wait()
        part = jnp.dot(a_s[i], weight_block(w_ref, i), preferred_element_type=jnp.float32)
        if i == 0:
            part_ref[...] = part
        else:
            part_ref[...] += part


def project_own(a, w5, early):
    rows = a.shape[0]
    block = 4 * w5.shape[3]
    vmem = pl.BlockSpec(memory_space=pltpu.VMEM)
    hbm = pl.BlockSpec(memory_space=pltpu.HBM)
    return pl.pallas_call(
        own_kernel,
        in_specs=[hbm, hbm],
        out_specs=[vmem, vmem],
        out_shape=[
            jax.ShapeDtypeStruct((rows, 9 * HD), jnp.float32),
            pltpu.VMEM((3, 2 * early) + w5.shape[2:], jnp.bfloat16),
        ],
        scratch_shapes=[
            pltpu.VMEM((early, rows, block), jnp.bfloat16),
            pltpu.SemaphoreType.DMA((early,)),
            pltpu.SemaphoreType.DMA((early,)),
        ],
        compiler_params=pltpu.CompilerParams(vmem_limit_bytes=20 * MIB),
        cost_estimate=pl.CostEstimate(flops=4 * 10**9, bytes_accessed=10**7, transcendentals=0),
        name="project_own",
    )(a, w5)


def project_kernel(
    early, where_ref, part_ref, own_hbm, oth_ref, w_ref, w_hbm, g_ref, own_out, send_out, half_hbm, a_s, w_s, acc_ref,
    own_sem, w_sem, half_sem
):
    rows = part_ref.shape[0]
    chunks = half_hbm.shape[1] // 2
    block = 4 * w_ref.shape[3]
    side = 1 - where_ref[1]

    def fetch_own(i):
        return pltpu.make_async_copy(own_hbm.at[:, pl.ds(i * block, block)], a_s.at[i - early], own_sem.at[i])

    def other(i):
        return oth_ref[:, i * block : (i + 1) * block]

    def fetch_weights(i):
        src = w_hbm.at[:, 2 * i : 2 * i + 2]
        return pltpu.make_async_copy(src, w_s.at[:, 2 * (i - early) : 2 * (i - early) + 2], w_sem.at[i])

    def put_half(i):
        if i < early:
            src = w_ref.at[:, 2 * i : 2 * i + 2, side]
        else:
            src = w_s.at[:, 2 * (i - early) : 2 * (i - early) + 2, side]
        return pltpu.make_async_copy(src, half_hbm.at[:, 2 * i : 2 * i + 2], half_sem.at[i])

    for i in range(early, chunks):
        fetch_weights(i).start()
        fetch_own(i).start()
    for i in range(early):
        put_half(i).start()
    acc_ref[0:rows] = part_ref[...]
    for i in range(chunks):
        if i < early:
            part = jnp.dot(other(i), weight_block(w_ref, i), preferred_element_type=jnp.float32)
            if i == 0:
                acc_ref[rows:] = part
            else:
                acc_ref[rows:] += part
        else:
            fetch_own(i).wait()
            fetch_weights(i).wait()
            put_half(i).start()
            a = jnp.concatenate([a_s[i - early], other(i)], axis=0)
            acc_ref[...] += jnp.dot(a, weight_block(w_s, i - early), preferred_element_type=jnp.float32)
    for h in range(NH):
        for c in range(3):
            lo = c * NH * HD + h * HD
            to = slice((h * 3 + c) * HD, (h * 3 + c + 1) * HD)
            x = acc_ref[:, lo : lo + HD].astype(jnp.bfloat16)
            own_out[:, to] = x[0:rows]
            send_out[:, to] = x[rows:]
    theirs = pair_head(where_ref[0], side)
    send_out[:, 9 * HD : 12 * HD] = own_out[:, head_columns(theirs, 3)]
    send_out[:, 12 * HD :] = g_ref[:, head_columns(theirs, 1)]
    for i in range(chunks):
        put_half(i).wait()


def project(where, part, own, other, w_early, w5, g):
    rows, depth = own.shape
    chunks = w5.shape[1] // 2
    early = w_early.shape[1] // 2
    vmem = pl.BlockSpec(memory_space=pltpu.VMEM)
    hbm = pl.BlockSpec(memory_space=pltpu.HBM)
    dma = pltpu.SemaphoreType.DMA((chunks,))
    return pl.pallas_call(
        functools.partial(project_kernel, early),
        in_specs=[pl.BlockSpec(memory_space=pltpu.SMEM), vmem, hbm, vmem, vmem, hbm, vmem],
        out_specs=[vmem, vmem, hbm],
        out_shape=[
            jax.ShapeDtypeStruct((rows, 9 * HD), jnp.bfloat16),
            jax.ShapeDtypeStruct((rows, 13 * HD), jnp.bfloat16),
            pltpu.HBM((3,) + w5.shape[1:2] + w5.shape[3:], jnp.bfloat16),
        ],
        scratch_shapes=[
            pltpu.VMEM((chunks - early, rows, depth // chunks), jnp.bfloat16),
            pltpu.VMEM((3, 2 * (chunks - early)) + w5.shape[2:], jnp.bfloat16),
            pltpu.VMEM((2 * rows, 9 * HD), jnp.float32),
            dma,
            dma,
            dma,
        ],
        compiler_params=pltpu.CompilerParams(vmem_limit_bytes=26 * MIB),
        cost_estimate=pl.CostEstimate(flops=7 * 10**9, bytes_accessed=10**7, transcendentals=0),
        name="project",
    )(where, part, own, other, w_early, w5, g)


def pair_head(chip, core):
    return jnp.minimum((chip + 1 + 2 * core) % RING, NH - 1)


def head_columns(head, width):
    return pl.ds(pl.multiple_of(head * (width * HD), width * HD), width * HD)


def section_rows(mod_ref, block, core, rows):
    lines = mod_ref.shape[0]
    mine = (mod_ref[...] == core).astype(jnp.float32)
    line = (lax.broadcasted_iota(jnp.int32, (rows, lines), 0) + block * rows) // HD
    place = (lax.broadcasted_iota(jnp.int32, (rows, HD), 0) + block * rows) % HD
    spread = jnp.dot(
        (line == lax.broadcasted_iota(jnp.int32, (rows, lines), 1)).astype(jnp.float32),
        mine,
        preferred_element_type=jnp.float32,
    )
    return jnp.sum(jnp.where(place == lax.broadcasted_iota(jnp.int32, (rows, HD), 1), spread, 0.0), axis=1, keepdims=True)


def route_kernel(where_ref, mod_ref, own_ref, sent_ref, got_ref, g_ref, pair_out, far_out, stay_out):
    chip, core = where_ref[0], where_ref[1]
    rows = own_ref.shape[0]
    mine = section_rows(mod_ref, 2 * chip + core, core, rows) > 0
    others = section_rows(mod_ref, 2 * chip + 1 - core, core, rows) > 0

    def own_rows(head):
        cols = head_columns(head, 3)
        return jnp.where(mine, own_ref[:, cols], got_ref[:, cols]), g_ref[:, head_columns(head, 1)]

    head = pair_head(chip, core)
    pair_out[0, :, : 3 * HD], pair_out[0, :, 3 * HD :] = own_rows(head)
    pair_out[1, :, : 3 * HD] = jnp.where(others, sent_ref[:, head_columns(head, 3)], got_ref[:, 9 * HD : 12 * HD])
    pair_out[1, :, 3 * HD :] = got_ref[:, 12 * HD :]
    far_out[:, : 3 * HD], far_out[:, 3 * HD :] = own_rows(jnp.minimum((chip + 2) % RING, NH - 1))
    stay_out[:, : 3 * HD], stay_out[:, 3 * HD :] = own_rows(jnp.minimum(chip, NH - 1))


def small_call(kernel, name, where, operands, out_shape):
    vmem = pl.BlockSpec(memory_space=pltpu.VMEM)
    return pl.pallas_call(
        kernel,
        in_specs=[pl.BlockSpec(memory_space=pltpu.SMEM)] + [vmem] * len(operands),
        out_specs=[vmem] * len(out_shape),
        out_shape=out_shape,
        compiler_params=pltpu.CompilerParams(vmem_limit_bytes=16 * MIB),
        cost_estimate=pl.CostEstimate(flops=10**6, bytes_accessed=3 * 10**6, transcendentals=0),
        name=name,
    )(where, *operands)


def attention_kernel(
    where_ref, stay, far, pair, stay_o, far_o, pair_o, keep_ref, send_ref, q_s, g_s, k_s, v_s, dq_s, dk_s, dv_s
):
    chip = where_ref[0]
    core = where_ref[1]
    rows = stay.shape[0]
    both = 2 * rows
    near = (chip + 3 + 2 * core) % RING
    across = (chip + 1 + 2 * core) % RING
    opposite = (chip + 2) % RING

    def block_rows(shard, side):
        return pl.ds(pl.multiple_of((2 * shard + side) * rows, rows), rows)

    for shard, r, o in (
        (chip, stay, stay_o),
        (opposite, far, far_o),
        (near, pair.at[0], pair.at[1]),
        (across, pair_o.at[1], pair_o.at[0]),
    ):
        q_s[shard] = r[:, 0:HD]
        g_s[shard] = r[:, 3 * HD : 4 * HD]
        k_s[block_rows(shard, core), :] = r[:, HD : 2 * HD]
        v_s[block_rows(shard, core), :] = r[:, 2 * HD : 3 * HD]
        k_s[block_rows(shard, 1 - core), :] = o[:, HD : 2 * HD]
        v_s[block_rows(shard, 1 - core), :] = o[:, 2 * HD : 3 * HD]
    nt = (((1,), (1,)), ((), ()))
    tn = (((0,), (0,)), ((), ()))
    for s in range(RING - 1, -1, -1):
        width = both * (s + 1)
        q = q_s[s]
        g = g_s[s]
        kk = k_s[0:width, :]
        vv = v_s[0:width, :]
        scores = lax.dot_general(q, kk, nt, preferred_element_type=jnp.float32) * SCALE
        row = lax.broadcasted_iota(jnp.int32, (rows, width), 0) + (2 * s + core) * rows
        col = lax.broadcasted_iota(jnp.int32, (rows, width), 1)
        scores = jnp.where(col <= row, scores, -jnp.inf)
        lifted = jnp.exp(scores - jnp.max(scores, axis=1, keepdims=True))
        probs = lifted / jnp.sum(lifted, axis=1, keepdims=True)
        low = probs.astype(jnp.bfloat16)
        dprobs = lax.dot_general(g, vv, nt, preferred_element_type=jnp.float32)
        row_dot = jnp.sum(probs * dprobs, axis=1, keepdims=True)
        ds = (probs * (dprobs - row_dot)).astype(jnp.bfloat16)
        dq = jnp.dot(ds, kk, preferred_element_type=jnp.float32) * SCALE
        dk = lax.dot_general(ds, q, tn, preferred_element_type=jnp.float32) * SCALE
        dv = lax.dot_general(low, g, tn, preferred_element_type=jnp.float32)
        if s == RING - 1:
            dk_s[...] = dk
            dv_s[...] = dv
        else:
            dk_s[0:width, :] += dk
            dv_s[0:width, :] += dv
        dq_s[s] = dq
    col = 0
    for shard, whole in ((near, True), (near, False), (chip, True), (opposite, True)):
        if whole:
            keep_ref[:, col : col + HD] = dq_s[shard]
            col += HD
        side = core if whole else 1 - core
        keep_ref[:, col : col + HD] = dk_s[block_rows(shard, side), :]
        keep_ref[:, col + HD : col + 2 * HD] = dv_s[block_rows(shard, side), :]
        col += 2 * HD
    col = 0
    for shard, whole in ((across, True), (across, False), (chip, False), (opposite, False)):
        if whole:
            send_ref[:, col : col + HD] = dq_s[shard].astype(jnp.bfloat16)
            col += HD
        side = core if whole else 1 - core
        send_ref[:, col : col + HD] = dk_s[block_rows(shard, side), :].astype(jnp.bfloat16)
        send_ref[:, col + HD : col + 2 * HD] = dv_s[block_rows(shard, side), :].astype(jnp.bfloat16)
        col += 2 * HD


def attention(where, parts):
    rows = parts[0].shape[0]
    total = 2 * RING * rows
    vmem = pl.BlockSpec(memory_space=pltpu.VMEM)
    return pl.pallas_call(
        attention_kernel,
        in_specs=[pl.BlockSpec(memory_space=pltpu.SMEM)] + [vmem] * 6,
        out_specs=[vmem, vmem],
        out_shape=[
            jax.ShapeDtypeStruct((rows, 11 * HD), jnp.float32),
            jax.ShapeDtypeStruct((rows, 9 * HD), jnp.bfloat16),
        ],
        scratch_shapes=[
            pltpu.VMEM((RING, rows, HD), jnp.bfloat16),
            pltpu.VMEM((RING, rows, HD), jnp.bfloat16),
            pltpu.VMEM((total, HD), jnp.bfloat16),
            pltpu.VMEM((total, HD), jnp.bfloat16),
            pltpu.VMEM((RING, rows, HD), jnp.float32),
            pltpu.VMEM((total, HD), jnp.float32),
            pltpu.VMEM((total, HD), jnp.float32),
        ],
        compiler_params=pltpu.CompilerParams(vmem_limit_bytes=32 * MIB),
        cost_estimate=pl.CostEstimate(flops=10**9, bytes_accessed=4 * 10**6, transcendentals=10**6),
        name="attention",
    )(where, *parts)


def combine_kernel(where_ref, keep, got, pair_out, far_out, stay_out):
    def put(out, query, kept, partner):
        out[:, 0:HD] = query.astype(jnp.bfloat16)
        kv = keep[:, kept : kept + 2 * HD] + got[:, partner : partner + 2 * HD].astype(jnp.float32)
        out[:, HD : 3 * HD] = kv.astype(jnp.bfloat16)

    put(pair_out.at[0], keep[:, 0:HD], HD, 3 * HD)
    put(pair_out.at[1], got[:, 0:HD], 3 * HD, HD)
    put(stay_out, keep[:, 5 * HD : 6 * HD], 6 * HD, 5 * HD)
    put(far_out, keep[:, 8 * HD : 9 * HD], 9 * HD, 7 * HD)


def gather(where, mod_ref, parts, out_ref):
    chip, core = where
    stay, far, pair, stay_o, far_o, pair_o = parts
    rows = stay.shape[0]
    mine = [section_rows(mod_ref, 2 * chip + side, core, rows) for side in (core, 1 - core)]
    for head, refs in (
        (chip, (stay, stay_o)),
        ((chip + 2) % RING, (far, far_o)),
        ((chip + 1 + 2 * core) % RING, (pair.at[0], pair.at[1])),
        ((chip + 3 + 2 * core) % RING, (pair_o.at[1], pair_o.at[0])),
    ):

        @pl.when(head < NH)
        def _():
            for block, x_ref in enumerate(refs):
                x = x_ref[...]
                zero = jnp.zeros_like(x)
                for side in range(2):
                    kept = jnp.where(mine[block] == 1.0 - side, x, zero)
                    for c in range(3):
                        lo = pl.multiple_of(((side * 3 + c) * NH + head) * HD, HD)
                        out_ref[block * rows : (block + 1) * rows, pl.ds(lo, HD)] = kept[:, c * HD : (c + 1) * HD]


def destination(where_ref, i, j):
    core, tp = where_ref[1], where_ref[2]
    dy, dz = jnp.where(core == 0, j, i), jnp.where(core == 0, i, j)
    return (tp // RING + dy) % RING * RING + (tp % RING + dz) % RING


def weight_copies(where_ref, own_hbm, other_hbm, to_ref, sem, hop):
    core = where_ref[1]
    copies = []
    for j in range(RING):
        dest = destination(where_ref, hop, j)
        copies.append(pltpu.make_async_copy(own_hbm.at[:, dest, core], to_ref.at[0, :, j], sem.at[0, j]))
        copies.append(pltpu.make_async_copy(other_hbm.at[:, dest], to_ref.at[1, :, j], sem.at[1, j]))
    return copies


def fetch_kernel(hops, where_ref, after_ref, own_hbm, other_hbm, *refs):
    copies = []
    for i, hop in enumerate(hops):
        copies += weight_copies(where_ref, own_hbm, other_hbm, refs[i], refs[len(hops) + i], hop)
    for copy in copies:
        copy.start()
    for copy in copies:
        copy.wait()


def fetch_weights(where, after, w5, other_half, hops):
    vmem = pl.BlockSpec(memory_space=pltpu.VMEM)
    hbm = pl.BlockSpec(memory_space=pltpu.HBM)
    anywhere = pl.BlockSpec(memory_space=pl.ANY)
    return pl.pallas_call(
        functools.partial(fetch_kernel, hops),
        in_specs=[pl.BlockSpec(memory_space=pltpu.SMEM), vmem, hbm, anywhere],
        out_specs=[vmem for _ in hops],
        out_shape=[pltpu.VMEM((2, 3, RING) + w5.shape[3:], jnp.bfloat16) for _ in hops],
        scratch_shapes=[pltpu.SemaphoreType.DMA((2, RING)) for _ in hops],
        compiler_params=pltpu.CompilerParams(vmem_limit_bytes=20 * MIB),
        cost_estimate=pl.CostEstimate(flops=10**6, bytes_accessed=10**7, transcendentals=0),
        name="fetch_weights",
    )(where, after, w5, other_half)


def product(g_ref, w_ref, outs, first=0, count=RING):
    cols = w_ref.shape[3]
    w = [w_ref[side, c, first : first + count].reshape(count * cols, NH * HD) for side in range(2) for c in range(3)]
    res = lax.dot_general(
        g_ref[...], jnp.concatenate(w, axis=1), (((1,), (1,)), ((), ())), preferred_element_type=jnp.float32
    ).astype(jnp.bfloat16)
    for i in range(count):
        outs[(first + i) // 2][(first + i) % 2] = res[:, i * cols : (i + 1) * cols]


def back_first_kernel(following, where_ref, mod_ref, *refs):
    *parts, w_ref, own_hbm, other_hbm, out_a, out_b, g_ref, next_ref, sem = refs
    for copy in weight_copies(where_ref, own_hbm, other_hbm, next_ref, sem, following):
        copy.start()
    gather((where_ref[0], where_ref[1]), mod_ref, parts, g_ref)
    product(g_ref, w_ref, (out_a, out_b))
    for copy in weight_copies(where_ref, own_hbm, other_hbm, next_ref, sem, following):
        copy.wait()


def back_middle_kernel(g_ref, w_ref, out_a, out_b):
    product(g_ref, w_ref, (out_a, out_b))


def back_last_kernel(hop, where_ref, after_a, after_b, g_ref, own_hbm, other_hbm, out_a, out_b, w_s, sem):
    copies = weight_copies(where_ref, own_hbm, other_hbm, w_s, sem, hop)
    for copy in copies:
        copy.start()
    for j in range(0, RING, 2):
        for copy in copies[2 * j : 2 * j + 4]:
            copy.wait()
        product(g_ref, w_s, (out_a, out_b), j, 2)


def back_call(kernel, operands, in_specs, out_shape, scratch):
    vmem = pl.BlockSpec(memory_space=pltpu.VMEM)
    return pl.pallas_call(
        kernel,
        in_specs=in_specs,
        out_specs=[vmem] * len(out_shape),
        out_shape=out_shape,
        scratch_shapes=scratch,
        compiler_params=pltpu.CompilerParams(vmem_limit_bytes=24 * MIB),
        cost_estimate=pl.CostEstimate(flops=10**6, bytes_accessed=10**4, transcendentals=0),
        name="back",
    )(*operands)


def add_kernel(a_ref, b_ref, out_ref):
    out_ref[...] = (a_ref[...].astype(jnp.float32) + b_ref[...].astype(jnp.float32)).astype(jnp.bfloat16)


def add(a, b):
    vmem = pl.BlockSpec(memory_space=pltpu.VMEM)
    return pl.pallas_call(
        add_kernel,
        in_specs=[vmem, vmem],
        out_specs=vmem,
        out_shape=jax.ShapeDtypeStruct(a.shape, jnp.bfloat16),
        compiler_params=pltpu.CompilerParams(vmem_limit_bytes=16 * MIB),
        cost_estimate=pl.CostEstimate(flops=10**5, bytes_accessed=10**4, transcendentals=0),
        name="add",
    )(a, b)


def back_reduced(where, mod, parts, weights, w5, other_half):
    rows = 2 * parts[0].shape[0]
    cols = w5.shape[3]
    smem = pl.BlockSpec(memory_space=pltpu.SMEM)
    vmem = pl.BlockSpec(memory_space=pltpu.VMEM)
    hbm = pl.BlockSpec(memory_space=pltpu.HBM)
    anywhere = pl.BlockSpec(memory_space=pl.ANY)
    halves = [jax.ShapeDtypeStruct((RING // 2, rows, cols), jnp.bfloat16)] * 2
    w_shape = (2, 3, RING) + w5.shape[3:]
    sem = pltpu.SemaphoreType.DMA((2, RING))

    def onward(x):
        return lax.ppermute(x, AXES, ring_perm(True, 1))

    def backward(x):
        return lax.ppermute(x, AXES, ring_perm(True, -1))

    w_two, w_one = weights
    two_a, two_b, g, w_three = back_call(
        functools.partial(back_first_kernel, 3),
        (where, mod, *parts, w_two, w5, other_half),
        [smem] + [vmem] * 8 + [hbm, anywhere],
        halves + [pltpu.VMEM((rows, 18 * HD), jnp.bfloat16), pltpu.VMEM(w_shape, jnp.bfloat16)],
        [sem],
    )
    g = pltpu.with_memory_space_constraint(g, pltpu.VMEM)
    w_three = pltpu.with_memory_space_constraint(w_three, pltpu.VMEM)
    relay_a, relay_b = onward(two_a), backward(two_b)
    one_a, one_b = back_call(back_middle_kernel, (g, w_one), [vmem, vmem], halves, [])
    from_one_b = onward(one_b)
    three_a, three_b = back_call(back_middle_kernel, (g, w_three), [vmem, vmem], halves, [])
    from_three_a = backward(three_a)
    one_a = add(one_a, relay_a)
    three_b = add(three_b, relay_b)
    from_one_a, from_three_b = onward(one_a), backward(three_b)
    own_a, own_b = back_call(
        functools.partial(back_last_kernel, 0),
        (where, one_a, three_b, g, w5, other_half),
        [smem, anywhere, anywhere, vmem, hbm, anywhere],
        halves,
        [pltpu.VMEM(w_shape, jnp.bfloat16), sem],
    )
    sum_b = own_b.astype(jnp.float32) + from_one_b.astype(jnp.float32)
    own_a, sum_b = lax.optimization_barrier((own_a, sum_b))
    sum_a = own_a.astype(jnp.float32) + from_three_a.astype(jnp.float32)
    sum_a, sum_b = lax.optimization_barrier((sum_a, sum_b))
    sum_a = sum_a + from_one_a.astype(jnp.float32)
    sum_a, sum_b = lax.optimization_barrier((sum_a, sum_b))
    sum_b = sum_b + from_three_b.astype(jnp.float32)
    return [sum_a[0], sum_a[1], sum_b[0], sum_b[1]]


def ring_perm(first, hop):
    pairs = []
    for s in range(RING):
        for m in range(2):
            for y in range(RING):
                for z in range(RING):
                    if (m == 0) == first:
                        to = (y, (z + hop) % RING)
                    else:
                        to = ((y + hop) % RING, z)
                    base = (s * 2 + m) * RING * RING
                    pairs.append((base + y * RING + z, base + to[0] * RING + to[1]))
    return pairs


def pair_perm(step):
    pairs = []
    for s in range(RING):
        for m in range(2):
            head = (s + (1 if m == 0 else -1)) % RING
            if step > 0 and head < NH:
                pairs.append((2 * s + m, 2 * head + m))
            if step < 0 and s < NH:
                pairs.append((2 * s + m, 2 * ((s + (-1 if m == 0 else 1)) % RING) + m))
    return pairs


def per_device(activations, grad_attn, weights, modality):
    rows, depth = activations.shape
    chip = lax.axis_index("seq")
    core = lax.axis_index("mod")
    tp = lax.axis_index("tp")
    where = jnp.stack([chip, core, tp]).astype(jnp.int32)
    dests = RING * RING
    cols = depth // dests // 2
    w5 = jnp.transpose(weights[0], (1, 0, 2)).reshape(3, dests, 2, cols, NH * HD)

    mod = modality.reshape(-1, HD)
    w5 = pltpu.with_memory_space_constraint(w5, pltpu.HBM)
    activations = pltpu.with_memory_space_constraint(activations, pltpu.HBM)
    act_other = pltpu.with_memory_space_constraint(core_swap(activations), pltpu.VMEM)
    part, w_early = project_own(activations, w5, 4)
    w_early = pltpu.with_memory_space_constraint(w_early, pltpu.VMEM)
    proj_own, sent, half = project(where, part, activations, act_other, w_early, w5, grad_attn)
    got = core_swap(sent)
    got, half = lax.optimization_barrier((got, half))
    other_half = core_swap(half)

    def part_shapes(width):
        block = jax.ShapeDtypeStruct((rows, width), jnp.bfloat16)
        return [jax.ShapeDtypeStruct((2, rows, width), jnp.bfloat16), block, block]

    pair, far, stay = small_call(
        route_kernel, "route", where, (mod, proj_own, sent, got, grad_attn), part_shapes(4 * HD)
    )
    pair = lax.ppermute(pair, ("seq", "mod"), pair_perm(1))
    far = lax.ppermute(far, "seq", [(i, (i + 2) % RING) for i in range(RING) if (i + 2) % RING < NH])
    parts = [stay, far, pair]
    keep, send = attention(where, parts + [core_swap(x) for x in parts])
    pair, far, stay = small_call(combine_kernel, "combine", where, (keep, core_swap(send)), part_shapes(3 * HD))

    w_first = fetch_weights(where, stay, w5, other_half, (2, 1))
    w_first = [pltpu.with_memory_space_constraint(w, pltpu.VMEM) for w in w_first]
    pair = lax.ppermute(pair, ("seq", "mod"), pair_perm(-1))
    far = lax.ppermute(far, "seq", [(i, (i + 2) % RING) for i in range(NH)])
    pair, far, w_first = lax.optimization_barrier((pair, far, w_first))
    parts = [stay, far, pair]
    parts += [core_swap(x) for x in parts]

    total = back_reduced(where, mod, parts, w_first, w5, other_half)
    result = total[0]
    for hop in (1, 3, 2):
        got = lax.ppermute(total[hop].astype(jnp.bfloat16), AXES, ring_perm(False, hop))
        result = lax.optimization_barrier(result) + got.astype(jnp.float32)
    result = result.astype(jnp.bfloat16)
    mine = result[:rows]
    theirs = core_swap(result[rows:])
    return jnp.where(
        core == 0, jnp.concatenate([mine, theirs], axis=1), jnp.concatenate([theirs, mine], axis=1)
    )


def solution(mesh):
    in_specs = (P(("seq", "mod"), None), P(("seq", "mod"), "tp"), P("mod", None, None, "tp"), P())
    out_specs = P(("seq", "mod"), "tp")
    return jax.shard_map(
        per_device, mesh=mesh, in_specs=in_specs, out_specs=out_specs, check_vma=False
    )
```

```python
import functools

import jax
import jax.numpy as jnp
from jax import lax
from jax.experimental import pallas as pl
from jax.experimental.pallas import tpu as pltpu
from jax.sharding import PartitionSpec as P

HD = 128
NH = 3
RING = 4
SCALE = HD**-0.5
SECOND = (0, 2, 1, 3)
AXES = ("seq", "mod", "tp")
MIB = 1024 * 1024


def core_swap(x):
    return lax.ppermute(x, "mod", [(0, 1), (1, 0)])


def weight_block(w_ref, i, count=1):
    size = 4 * w_ref.shape[3] * count
    rows = slice(2 * i, 2 * (i + count))
    return jnp.concatenate([w_ref[c, rows].reshape(size, NH * HD) for c in range(3)], axis=1)


def own_kernel(a_hbm, w_hbm, part_ref, w_ref, a_s, a_sem, w_sem):
    chunks = w_ref.shape[1] // 2
    block = 4 * w_ref.shape[3]

    def fetch(i):
        pair = slice(2 * i, 2 * i + 2)
        return (
            pltpu.make_async_copy(a_hbm.at[:, pl.ds(i * block, block)], a_s.at[i], a_sem.at[i]),
            pltpu.make_async_copy(w_hbm.at[:, pair], w_ref.at[:, pair], w_sem.at[i]),
        )

    for i in range(chunks):
        for copy in fetch(i):
            copy.start()
    for i in range(chunks):
        for copy in fetch(i):
            copy.wait()
        part = jnp.dot(a_s[i], weight_block(w_ref, i), preferred_element_type=jnp.float32)
        if i == 0:
            part_ref[...] = part
        else:
            part_ref[...] += part


def project_own(a, w5, early):
    rows = a.shape[0]
    block = 4 * w5.shape[3]
    vmem = pl.BlockSpec(memory_space=pltpu.VMEM)
    hbm = pl.BlockSpec(memory_space=pltpu.HBM)
    return pl.pallas_call(
        own_kernel,
        in_specs=[hbm, hbm],
        out_specs=[vmem, vmem],
        out_shape=[
            jax.ShapeDtypeStruct((rows, 9 * HD), jnp.float32),
            pltpu.VMEM((3, 2 * early) + w5.shape[2:], jnp.bfloat16),
        ],
        scratch_shapes=[
            pltpu.VMEM((early, rows, block), jnp.bfloat16),
            pltpu.SemaphoreType.DMA((early,)),
            pltpu.SemaphoreType.DMA((early,)),
        ],
        compiler_params=pltpu.CompilerParams(vmem_limit_bytes=20 * MIB),
        cost_estimate=pl.CostEstimate(flops=4 * 10**9, bytes_accessed=10**7, transcendentals=0),
        name="project_own",
    )(a, w5)


def project_kernel(
    early, where_ref, part_ref, own_hbm, oth_ref, w_ref, w_hbm, g_ref, own_out, send_out, half_hbm, a_s, w_s, acc_ref,
    own_sem, w_sem, half_sem
):
    rows = part_ref.shape[0]
    chunks = half_hbm.shape[1] // 2
    block = 4 * w_ref.shape[3]
    side = 1 - where_ref[1]

    def fetch_own(i):
        return pltpu.make_async_copy(own_hbm.at[:, pl.ds(i * block, block)], a_s.at[:, pl.ds((i - early) * block, block)], own_sem.at[i])

    def other(i):
        return oth_ref[:, i * block : (i + 2) * block]

    def fetch_weights(i):
        src = w_hbm.at[:, 2 * i : 2 * i + 2]
        return pltpu.make_async_copy(src, w_s.at[:, 2 * (i - early) : 2 * (i - early) + 2], w_sem.at[i])

    def put_half(i):
        if i < early:
            src = w_ref.at[:, 2 * i : 2 * i + 2, side]
        else:
            src = w_s.at[:, 2 * (i - early) : 2 * (i - early) + 2, side]
        return pltpu.make_async_copy(src, half_hbm.at[:, 2 * i : 2 * i + 2], half_sem.at[i])

    for i in range(early, chunks):
        fetch_weights(i).start()
        fetch_own(i).start()
    for i in range(early):
        put_half(i).start()
    acc_ref[0:rows] = part_ref[...]
    for i in range(0, chunks, 2):
        if i < early:
            part = jnp.dot(other(i), weight_block(w_ref, i, 2), preferred_element_type=jnp.float32)
            if i == 0:
                acc_ref[rows:] = part
            else:
                acc_ref[rows:] += part
        else:
            for k in (i, i + 1):
                fetch_own(k).wait()
                fetch_weights(k).wait()
                put_half(k).start()
            a = jnp.concatenate([a_s[:, (i - early) * block : (i - early + 2) * block], other(i)], axis=0)
            acc_ref[...] += jnp.dot(a, weight_block(w_s, i - early, 2), preferred_element_type=jnp.float32)
    for h in range(NH):
        for c in range(3):
            lo = c * NH * HD + h * HD
            to = slice((h * 3 + c) * HD, (h * 3 + c + 1) * HD)
            x = acc_ref[:, lo : lo + HD].astype(jnp.bfloat16)
            own_out[:, to] = x[0:rows]
            send_out[:, to] = x[rows:]
    theirs = pair_head(where_ref[0], side)
    send_out[:, 9 * HD : 12 * HD] = own_out[:, head_columns(theirs, 3)]
    send_out[:, 12 * HD :] = g_ref[:, head_columns(theirs, 1)]
    for i in range(chunks):
        put_half(i).wait()


def project(where, part, own, other, w_early, w5, g):
    rows, depth = own.shape
    chunks = w5.shape[1] // 2
    early = w_early.shape[1] // 2
    vmem = pl.BlockSpec(memory_space=pltpu.VMEM)
    hbm = pl.BlockSpec(memory_space=pltpu.HBM)
    dma = pltpu.SemaphoreType.DMA((chunks,))
    return pl.pallas_call(
        functools.partial(project_kernel, early),
        in_specs=[pl.BlockSpec(memory_space=pltpu.SMEM), vmem, hbm, vmem, vmem, hbm, vmem],
        out_specs=[vmem, vmem, hbm],
        out_shape=[
            jax.ShapeDtypeStruct((rows, 9 * HD), jnp.bfloat16),
            jax.ShapeDtypeStruct((rows, 13 * HD), jnp.bfloat16),
            pltpu.HBM((3,) + w5.shape[1:2] + w5.shape[3:], jnp.bfloat16),
        ],
        scratch_shapes=[
            pltpu.VMEM((rows, depth // chunks * (chunks - early)), jnp.bfloat16),
            pltpu.VMEM((3, 2 * (chunks - early)) + w5.shape[2:], jnp.bfloat16),
            pltpu.VMEM((2 * rows, 9 * HD), jnp.float32),
            dma,
            dma,
            dma,
        ],
        compiler_params=pltpu.CompilerParams(vmem_limit_bytes=26 * MIB),
        cost_estimate=pl.CostEstimate(flops=7 * 10**9, bytes_accessed=10**7, transcendentals=0),
        name="project",
    )(where, part, own, other, w_early, w5, g)


def pair_head(chip, core):
    return jnp.minimum((chip + 1 + 2 * core) % RING, NH - 1)


def head_columns(head, width):
    return pl.ds(pl.multiple_of(head * (width * HD), width * HD), width * HD)


def section_rows(mod_ref, block, core, rows):
    lines = mod_ref.shape[0]
    mine = (mod_ref[...] == core).astype(jnp.float32)
    line = (lax.broadcasted_iota(jnp.int32, (rows, lines), 0) + block * rows) // HD
    place = (lax.broadcasted_iota(jnp.int32, (rows, HD), 0) + block * rows) % HD
    spread = jnp.dot(
        (line == lax.broadcasted_iota(jnp.int32, (rows, lines), 1)).astype(jnp.float32),
        mine,
        preferred_element_type=jnp.float32,
    )
    return jnp.sum(jnp.where(place == lax.broadcasted_iota(jnp.int32, (rows, HD), 1), spread, 0.0), axis=1, keepdims=True)


def route_kernel(where_ref, mod_ref, own_ref, sent_ref, got_ref, g_ref, pair_out, far_out, stay_out, mask_out):
    chip, core = where_ref[0], where_ref[1]
    rows = own_ref.shape[0]
    masks = [section_rows(mod_ref, 2 * chip + side, core, rows) for side in (core, 1 - core)]
    mine, others = [mask > 0 for mask in masks]
    for block, mask in enumerate(masks):
        mask_out[block] = jnp.broadcast_to(mask, (rows, HD)).astype(jnp.bfloat16)

    def own_rows(head):
        cols = head_columns(head, 3)
        return jnp.where(mine, own_ref[:, cols], got_ref[:, cols]), g_ref[:, head_columns(head, 1)]

    head = pair_head(chip, core)
    pair_out[0, :, : 3 * HD], pair_out[0, :, 3 * HD :] = own_rows(head)
    pair_out[1, :, : 3 * HD] = jnp.where(others, sent_ref[:, head_columns(head, 3)], got_ref[:, 9 * HD : 12 * HD])
    pair_out[1, :, 3 * HD :] = got_ref[:, 12 * HD :]
    far_out[:, : 3 * HD], far_out[:, 3 * HD :] = own_rows(jnp.minimum((chip + 2) % RING, NH - 1))
    stay_out[:, : 3 * HD], stay_out[:, 3 * HD :] = own_rows(jnp.minimum(chip, NH - 1))


def small_call(kernel, name, where, operands, out_shape):
    vmem = pl.BlockSpec(memory_space=pltpu.VMEM)
    return pl.pallas_call(
        kernel,
        in_specs=[pl.BlockSpec(memory_space=pltpu.SMEM)] + [vmem] * len(operands),
        out_specs=[vmem] * len(out_shape),
        out_shape=out_shape,
        compiler_params=pltpu.CompilerParams(vmem_limit_bytes=16 * MIB),
        cost_estimate=pl.CostEstimate(flops=10**6, bytes_accessed=3 * 10**6, transcendentals=0),
        name=name,
    )(where, *operands)


def attention_kernel(
    where_ref, stay, far, pair, stay_o, far_o, pair_o, keep_ref, send_ref, q_s, g_s, k_s, v_s, dq_s, dk_s, dv_s
):
    chip = where_ref[0]
    core = where_ref[1]
    rows = stay.shape[0]
    both = 2 * rows
    near = (chip + 3 + 2 * core) % RING
    across = (chip + 1 + 2 * core) % RING
    opposite = (chip + 2) % RING

    def block_rows(shard, side):
        return pl.ds(pl.multiple_of((2 * shard + side) * rows, rows), rows)

    for shard, r, o in (
        (chip, stay, stay_o),
        (opposite, far, far_o),
        (near, pair.at[0], pair.at[1]),
        (across, pair_o.at[1], pair_o.at[0]),
    ):
        q_s[shard] = r[:, 0:HD]
        g_s[shard] = r[:, 3 * HD : 4 * HD]
        k_s[block_rows(shard, core), :] = r[:, HD : 2 * HD]
        v_s[block_rows(shard, core), :] = r[:, 2 * HD : 3 * HD]
        k_s[block_rows(shard, 1 - core), :] = o[:, HD : 2 * HD]
        v_s[block_rows(shard, 1 - core), :] = o[:, 2 * HD : 3 * HD]
    nt = (((1,), (1,)), ((), ()))
    tn = (((0,), (0,)), ((), ()))
    for s in range(RING - 1, -1, -1):
        width = both * (s + 1)
        q = q_s[s]
        g = g_s[s]
        kk = k_s[0:width, :]
        vv = v_s[0:width, :]
        scores = lax.dot_general(q, kk, nt, preferred_element_type=jnp.float32) * SCALE
        row = lax.broadcasted_iota(jnp.int32, (rows, width), 0) + (2 * s + core) * rows
        col = lax.broadcasted_iota(jnp.int32, (rows, width), 1)
        scores = jnp.where(col <= row, scores, -jnp.inf)
        lifted = jnp.exp(scores - jnp.max(scores, axis=1, keepdims=True))
        probs = lifted / jnp.sum(lifted, axis=1, keepdims=True)
        low = probs.astype(jnp.bfloat16)
        dprobs = lax.dot_general(g, vv, nt, preferred_element_type=jnp.float32)
        row_dot = jnp.sum(probs * dprobs, axis=1, keepdims=True)
        ds = (probs * (dprobs - row_dot)).astype(jnp.bfloat16)
        dq = jnp.dot(ds, kk, preferred_element_type=jnp.float32) * SCALE
        dk = lax.dot_general(ds, q, tn, preferred_element_type=jnp.float32) * SCALE
        dv = lax.dot_general(low, g, tn, preferred_element_type=jnp.float32)
        if s == RING - 1:
            dk_s[...] = dk
            dv_s[...] = dv
        else:
            dk_s[0:width, :] += dk
            dv_s[0:width, :] += dv
        dq_s[s] = dq
    col = 0
    for shard, whole in ((near, True), (near, False), (chip, True), (opposite, True)):
        if whole:
            keep_ref[:, col : col + HD] = dq_s[shard]
            col += HD
        side = core if whole else 1 - core
        keep_ref[:, col : col + HD] = dk_s[block_rows(shard, side), :]
        keep_ref[:, col + HD : col + 2 * HD] = dv_s[block_rows(shard, side), :]
        col += 2 * HD
    col = 0
    for shard, whole in ((across, True), (across, False), (chip, False), (opposite, False)):
        if whole:
            send_ref[:, col : col + HD] = dq_s[shard].astype(jnp.bfloat16)
            col += HD
        side = core if whole else 1 - core
        send_ref[:, col : col + HD] = dk_s[block_rows(shard, side), :].astype(jnp.bfloat16)
        send_ref[:, col + HD : col + 2 * HD] = dv_s[block_rows(shard, side), :].astype(jnp.bfloat16)
        col += 2 * HD


def attention(where, parts):
    rows = parts[0].shape[0]
    total = 2 * RING * rows
    vmem = pl.BlockSpec(memory_space=pltpu.VMEM)
    return pl.pallas_call(
        attention_kernel,
        in_specs=[pl.BlockSpec(memory_space=pltpu.SMEM)] + [vmem] * 6,
        out_specs=[vmem, vmem],
        out_shape=[
            jax.ShapeDtypeStruct((rows, 11 * HD), jnp.float32),
            jax.ShapeDtypeStruct((rows, 9 * HD), jnp.bfloat16),
        ],
        scratch_shapes=[
            pltpu.VMEM((RING, rows, HD), jnp.bfloat16),
            pltpu.VMEM((RING, rows, HD), jnp.bfloat16),
            pltpu.VMEM((total, HD), jnp.bfloat16),
            pltpu.VMEM((total, HD), jnp.bfloat16),
            pltpu.VMEM((RING, rows, HD), jnp.float32),
            pltpu.VMEM((total, HD), jnp.float32),
            pltpu.VMEM((total, HD), jnp.float32),
        ],
        compiler_params=pltpu.CompilerParams(vmem_limit_bytes=32 * MIB),
        cost_estimate=pl.CostEstimate(flops=10**9, bytes_accessed=4 * 10**6, transcendentals=10**6),
        name="attention",
    )(where, *parts)


def combine_kernel(where_ref, keep, got, pair_out, far_out, stay_out):
    def put(out, query, kept, partner):
        out[:, 0:HD] = query.astype(jnp.bfloat16)
        kv = keep[:, kept : kept + 2 * HD] + got[:, partner : partner + 2 * HD].astype(jnp.float32)
        out[:, HD : 3 * HD] = kv.astype(jnp.bfloat16)

    put(pair_out.at[0], keep[:, 0:HD], HD, 3 * HD)
    put(pair_out.at[1], got[:, 0:HD], 3 * HD, HD)
    put(stay_out, keep[:, 5 * HD : 6 * HD], 6 * HD, 5 * HD)
    put(far_out, keep[:, 8 * HD : 9 * HD], 9 * HD, 7 * HD)


def gather(where, mask_ref, parts, out_ref):
    chip, core = where
    stay, far, pair, stay_o, far_o, pair_o = parts
    rows = stay.shape[0]
    for head, refs in (
        (chip, (stay, stay_o)),
        ((chip + 2) % RING, (far, far_o)),
        ((chip + 1 + 2 * core) % RING, (pair.at[0], pair.at[1])),
        ((chip + 3 + 2 * core) % RING, (pair_o.at[1], pair_o.at[0])),
    ):

        @pl.when(head < NH)
        def _():
            for block, x_ref in enumerate(refs):
                for c in range(3):
                    x = x_ref[:, c * HD : (c + 1) * HD]
                    mine = x * mask_ref[block]
                    for side, kept in enumerate((mine, x - mine)):
                        lo = pl.multiple_of(((side * 3 + c) * NH + head) * HD, HD)
                        out_ref[block * rows : (block + 1) * rows, pl.ds(lo, HD)] = kept


def destination(where_ref, i, j):
    core, tp = where_ref[1], where_ref[2]
    dy, dz = jnp.where(core == 0, j, i), jnp.where(core == 0, i, j)
    return (tp // RING + dy) % RING * RING + (tp % RING + dz) % RING


def weight_copies(where_ref, own_hbm, other_hbm, to_ref, sem, hop):
    core = where_ref[1]
    copies = []
    for j in range(RING):
        dest = destination(where_ref, hop, SECOND[j])
        copies.append(pltpu.make_async_copy(own_hbm.at[:, dest, core], to_ref.at[0, :, j], sem.at[0, j]))
        copies.append(pltpu.make_async_copy(other_hbm.at[:, dest], to_ref.at[1, :, j], sem.at[1, j]))
    return copies


def fetch_kernel(hops, where_ref, after_ref, own_hbm, other_hbm, *refs):
    copies = []
    for i, hop in enumerate(hops):
        copies += weight_copies(where_ref, own_hbm, other_hbm, refs[i], refs[len(hops) + i], hop)
    for copy in copies:
        copy.start()
    for copy in copies:
        copy.wait()


def fetch_weights(where, after, w5, other_half, hops):
    vmem = pl.BlockSpec(memory_space=pltpu.VMEM)
    hbm = pl.BlockSpec(memory_space=pltpu.HBM)
    anywhere = pl.BlockSpec(memory_space=pl.ANY)
    return pl.pallas_call(
        functools.partial(fetch_kernel, hops),
        in_specs=[pl.BlockSpec(memory_space=pltpu.SMEM), vmem, hbm, anywhere],
        out_specs=[vmem for _ in hops],
        out_shape=[pltpu.VMEM((2, 3, RING) + w5.shape[3:], jnp.bfloat16) for _ in hops],
        scratch_shapes=[pltpu.SemaphoreType.DMA((2, RING)) for _ in hops],
        compiler_params=pltpu.CompilerParams(vmem_limit_bytes=20 * MIB),
        cost_estimate=pl.CostEstimate(flops=10**6, bytes_accessed=10**7, transcendentals=0),
        name="fetch_weights",
    )(where, after, w5, other_half)


def product(g_ref, w_ref, outs, first=0, count=RING):
    cols = w_ref.shape[3]
    w = [w_ref[side, c, first : first + count].reshape(count * cols, NH * HD) for side in range(2) for c in range(3)]
    res = lax.dot_general(
        g_ref[...], jnp.concatenate(w, axis=1), (((1,), (1,)), ((), ())), preferred_element_type=jnp.float32
    ).astype(jnp.bfloat16)
    for i in range(count):
        outs[(first + i) // 2][(first + i) % 2] = res[:, i * cols : (i + 1) * cols]


def back_first_kernel(following, where_ref, mask_ref, *refs):
    *parts, w_ref, own_hbm, other_hbm, out_a, out_b, g_ref, next_ref, sem = refs
    for copy in weight_copies(where_ref, own_hbm, other_hbm, next_ref, sem, following):
        copy.start()
    gather((where_ref[0], where_ref[1]), mask_ref, parts, g_ref)
    product(g_ref, w_ref, (out_a, out_b))
    for copy in weight_copies(where_ref, own_hbm, other_hbm, next_ref, sem, following):
        copy.wait()


def back_middle_kernel(g_ref, w_ref, out_a, out_b):
    product(g_ref, w_ref, (out_a, out_b))


def back_last_kernel(hop, where_ref, after_a, after_b, g_ref, own_hbm, other_hbm, out_a, out_b, w_s, sem):
    copies = weight_copies(where_ref, own_hbm, other_hbm, w_s, sem, hop)
    for copy in copies:
        copy.start()
    for j in range(0, RING, 2):
        for copy in copies[2 * j : 2 * j + 4]:
            copy.wait()
        product(g_ref, w_s, (out_a, out_b), j, 2)


def back_call(kernel, operands, in_specs, out_shape, scratch):
    vmem = pl.BlockSpec(memory_space=pltpu.VMEM)
    return pl.pallas_call(
        kernel,
        in_specs=in_specs,
        out_specs=[vmem] * len(out_shape),
        out_shape=out_shape,
        scratch_shapes=scratch,
        compiler_params=pltpu.CompilerParams(vmem_limit_bytes=24 * MIB),
        cost_estimate=pl.CostEstimate(flops=10**6, bytes_accessed=10**4, transcendentals=0),
        name="back",
    )(*operands)


def add_kernel(a_ref, b_ref, out_ref):
    out_ref[...] = (a_ref[...].astype(jnp.float32) + b_ref[...].astype(jnp.float32)).astype(jnp.bfloat16)


def add(a, b):
    vmem = pl.BlockSpec(memory_space=pltpu.VMEM)
    return pl.pallas_call(
        add_kernel,
        in_specs=[vmem, vmem],
        out_specs=vmem,
        out_shape=jax.ShapeDtypeStruct(a.shape, jnp.bfloat16),
        compiler_params=pltpu.CompilerParams(vmem_limit_bytes=16 * MIB),
        cost_estimate=pl.CostEstimate(flops=10**5, bytes_accessed=10**4, transcendentals=0),
        name="add",
    )(a, b)


def back_reduced(where, masks, parts, weights, w5, other_half):
    rows = 2 * parts[0].shape[0]
    cols = w5.shape[3]
    smem = pl.BlockSpec(memory_space=pltpu.SMEM)
    vmem = pl.BlockSpec(memory_space=pltpu.VMEM)
    hbm = pl.BlockSpec(memory_space=pltpu.HBM)
    anywhere = pl.BlockSpec(memory_space=pl.ANY)
    halves = [jax.ShapeDtypeStruct((RING // 2, rows, cols), jnp.bfloat16)] * 2
    w_shape = (2, 3, RING) + w5.shape[3:]
    sem = pltpu.SemaphoreType.DMA((2, RING))

    def onward(x):
        return lax.ppermute(x, AXES, ring_perm(True, 1))

    def backward(x):
        return lax.ppermute(x, AXES, ring_perm(True, -1))

    w_two, w_one = weights
    two_a, two_b, g, w_three = back_call(
        functools.partial(back_first_kernel, 3),
        (where, masks, *parts, w_two, w5, other_half),
        [smem] + [vmem] * 8 + [hbm, anywhere],
        halves + [pltpu.VMEM((rows, 18 * HD), jnp.bfloat16), pltpu.VMEM(w_shape, jnp.bfloat16)],
        [sem],
    )
    g = pltpu.with_memory_space_constraint(g, pltpu.VMEM)
    w_three = pltpu.with_memory_space_constraint(w_three, pltpu.VMEM)
    relay_a, relay_b = onward(two_a), backward(two_b)
    one_a, one_b = back_call(back_middle_kernel, (g, w_one), [vmem, vmem], halves, [])
    from_one_b = onward(one_b)
    three_a, three_b = back_call(back_middle_kernel, (g, w_three), [vmem, vmem], halves, [])
    from_three_a = backward(three_a)
    one_a = add(one_a, relay_a)
    three_b = add(three_b, relay_b)
    from_one_a, from_three_b = onward(one_a), backward(three_b)
    own_a, own_b = back_call(
        functools.partial(back_last_kernel, 0),
        (where, one_a, three_b, g, w5, other_half),
        [smem, anywhere, anywhere, vmem, hbm, anywhere],
        halves,
        [pltpu.VMEM(w_shape, jnp.bfloat16), sem],
    )
    sum_b = own_b.astype(jnp.float32) + from_one_b.astype(jnp.float32)
    own_a, sum_b = lax.optimization_barrier((own_a, sum_b))
    sum_a = own_a.astype(jnp.float32) + from_three_a.astype(jnp.float32)
    sum_a, sum_b = lax.optimization_barrier((sum_a, sum_b))
    sum_a = sum_a + from_one_a.astype(jnp.float32)
    sum_a, sum_b = lax.optimization_barrier((sum_a, sum_b))
    sum_b = sum_b + from_three_b.astype(jnp.float32)
    return dict(zip(SECOND, (sum_a[0], sum_a[1], sum_b[0], sum_b[1])))


def ring_perm(first, hop):
    pairs = []
    for s in range(RING):
        for m in range(2):
            for y in range(RING):
                for z in range(RING):
                    if (m == 0) == first:
                        to = (y, (z + hop) % RING)
                    else:
                        to = ((y + hop) % RING, z)
                    base = (s * 2 + m) * RING * RING
                    pairs.append((base + y * RING + z, base + to[0] * RING + to[1]))
    return pairs


def pair_perm(step):
    pairs = []
    for s in range(RING):
        for m in range(2):
            head = (s + (1 if m == 0 else -1)) % RING
            if step > 0 and head < NH:
                pairs.append((2 * s + m, 2 * head + m))
            if step < 0 and s < NH:
                pairs.append((2 * s + m, 2 * ((s + (-1 if m == 0 else 1)) % RING) + m))
    return pairs


def per_device(activations, grad_attn, weights, modality):
    rows, depth = activations.shape
    chip = lax.axis_index("seq")
    core = lax.axis_index("mod")
    tp = lax.axis_index("tp")
    where = jnp.stack([chip, core, tp]).astype(jnp.int32)
    dests = RING * RING
    cols = depth // dests // 2
    w5 = jnp.transpose(weights[0], (1, 0, 2)).reshape(3, dests, 2, cols, NH * HD)

    mod = modality.reshape(-1, HD)
    w5 = pltpu.with_memory_space_constraint(w5, pltpu.HBM)
    activations = pltpu.with_memory_space_constraint(activations, pltpu.HBM)
    act_other = pltpu.with_memory_space_constraint(core_swap(activations), pltpu.VMEM)
    part, w_early = project_own(activations, w5, 4)
    w_early = pltpu.with_memory_space_constraint(w_early, pltpu.VMEM)
    proj_own, sent, half = project(where, part, activations, act_other, w_early, w5, grad_attn)
    got = core_swap(sent)
    got, half = lax.optimization_barrier((got, half))
    other_half = core_swap(half)

    def part_shapes(width):
        block = jax.ShapeDtypeStruct((rows, width), jnp.bfloat16)
        return [jax.ShapeDtypeStruct((2, rows, width), jnp.bfloat16), block, block]

    pair, far, stay, masks = small_call(
        route_kernel,
        "route",
        where,
        (mod, proj_own, sent, got, grad_attn),
        part_shapes(4 * HD) + [jax.ShapeDtypeStruct((2, rows, HD), jnp.bfloat16)],
    )
    pair = lax.ppermute(pair, ("seq", "mod"), pair_perm(1))
    far = lax.ppermute(far, "seq", [(i, (i + 2) % RING) for i in range(RING) if (i + 2) % RING < NH])
    parts = [stay, far, pair]
    keep, send = attention(where, parts + [core_swap(x) for x in parts])
    pair, far, stay = small_call(combine_kernel, "combine", where, (keep, core_swap(send)), part_shapes(3 * HD))

    w_first = fetch_weights(where, stay, w5, other_half, (2, 1))
    w_first = [pltpu.with_memory_space_constraint(w, pltpu.VMEM) for w in w_first]
    pair = lax.ppermute(pair, ("seq", "mod"), pair_perm(-1))
    far = lax.ppermute(far, "seq", [(i, (i + 2) % RING) for i in range(NH)])
    far, w_first = lax.optimization_barrier((far, w_first))
    parts = [stay, far, pair]
    parts += [core_swap(x) for x in parts]

    total = back_reduced(where, masks, parts, w_first, w5, other_half)
    result = total[0]
    for hop in SECOND[1:]:
        got = lax.ppermute(total[hop].astype(jnp.bfloat16), AXES, ring_perm(False, hop))
        result = lax.optimization_barrier(result) + got.astype(jnp.float32)
    result = result.astype(jnp.bfloat16)
    mine = result[:rows]
    theirs = core_swap(result[rows:])
    return jnp.where(
        core == 0, jnp.concatenate([mine, theirs], axis=1), jnp.concatenate([theirs, mine], axis=1)
    )


def solution(mesh):
    in_specs = (P(("seq", "mod"), None), P(("seq", "mod"), "tp"), P("mod", None, None, "tp"), P())
    out_specs = P(("seq", "mod"), "tp")
    return jax.shard_map(
        per_device, mesh=mesh, in_specs=in_specs, out_specs=out_specs, check_vma=False
    )
```

```python
import functools

import jax
import jax.numpy as jnp
from jax import lax
from jax.experimental import pallas as pl
from jax.experimental.pallas import tpu as pltpu
from jax.sharding import PartitionSpec as P

HD = 128
NH = 3
RING = 4
SCALE = HD**-0.5
AXES = ("seq", "mod", "tp")
MIB = 1024 * 1024


def core_swap(x):
    return lax.ppermute(x, "mod", [(0, 1), (1, 0)])


def weight_block(w_ref, i):
    size = 4 * w_ref.shape[3]
    return jnp.concatenate([w_ref[c, 2 * i : 2 * i + 2].reshape(size, NH * HD) for c in range(3)], axis=1)


def own_kernel(a_hbm, w_hbm, part_ref, w_ref, a_s, a_sem, w_sem):
    chunks = w_ref.shape[1] // 2
    block = 4 * w_ref.shape[3]

    def fetch(i):
        pair = slice(2 * i, 2 * i + 2)
        return (
            pltpu.make_async_copy(a_hbm.at[:, pl.ds(i * block, block)], a_s.at[i], a_sem.at[i]),
            pltpu.make_async_copy(w_hbm.at[:, pair], w_ref.at[:, pair], w_sem.at[i]),
        )

    for i in range(chunks):
        for copy in fetch(i):
            copy.start()
    for i in range(chunks):
        for copy in fetch(i):
            copy.wait()
        part = jnp.dot(a_s[i], weight_block(w_ref, i), preferred_element_type=jnp.float32)
        if i == 0:
            part_ref[...] = part
        else:
            part_ref[...] += part


def project_own(a, w5, early):
    rows = a.shape[0]
    block = 4 * w5.shape[3]
    vmem = pl.BlockSpec(memory_space=pltpu.VMEM)
    hbm = pl.BlockSpec(memory_space=pltpu.HBM)
    return pl.pallas_call(
        own_kernel,
        in_specs=[hbm, hbm],
        out_specs=[vmem, vmem],
        out_shape=[
            jax.ShapeDtypeStruct((rows, 9 * HD), jnp.float32),
            pltpu.VMEM((3, 2 * early) + w5.shape[2:], jnp.bfloat16),
        ],
        scratch_shapes=[
            pltpu.VMEM((early, rows, block), jnp.bfloat16),
            pltpu.SemaphoreType.DMA((early,)),
            pltpu.SemaphoreType.DMA((early,)),
        ],
        compiler_params=pltpu.CompilerParams(vmem_limit_bytes=20 * MIB),
        cost_estimate=pl.CostEstimate(flops=4 * 10**9, bytes_accessed=10**7, transcendentals=0),
        name="project_own",
    )(a, w5)


def project_kernel(
    early, where_ref, part_ref, own_hbm, oth_ref, w_ref, w_hbm, g_ref, own_out, send_out, half_hbm, a_s, w_s, acc_ref,
    own_sem, w_sem, half_sem
):
    rows = part_ref.shape[0]
    chunks = half_hbm.shape[1] // 2
    block = 4 * w_ref.shape[3]
    side = 1 - where_ref[1]

    def fetch_own(i):
        return pltpu.make_async_copy(own_hbm.at[:, pl.ds(i * block, block)], a_s.at[i - early], own_sem.at[i])

    def other(i):
        return oth_ref[:, i * block : (i + 1) * block]

    def fetch_weights(i):
        src = w_hbm.at[:, 2 * i : 2 * i + 2]
        return pltpu.make_async_copy(src, w_s.at[:, 2 * (i - early) : 2 * (i - early) + 2], w_sem.at[i])

    def put_half(i):
        if i < early:
            src = w_ref.at[:, 2 * i : 2 * i + 2, side]
        else:
            src = w_s.at[:, 2 * (i - early) : 2 * (i - early) + 2, side]
        return pltpu.make_async_copy(src, half_hbm.at[:, 2 * i : 2 * i + 2], half_sem.at[i])

    for i in range(early, chunks):
        fetch_weights(i).start()
        fetch_own(i).start()
    for i in range(early):
        put_half(i).start()
    acc_ref[0:rows] = part_ref[...]
    for i in range(chunks):
        if i < early:
            part = jnp.dot(other(i), weight_block(w_ref, i), preferred_element_type=jnp.float32)
            if i == 0:
                acc_ref[rows:] = part
            else:
                acc_ref[rows:] += part
        else:
            fetch_own(i).wait()
            fetch_weights(i).wait()
            put_half(i).start()
            a = jnp.concatenate([a_s[i - early], other(i)], axis=0)
            acc_ref[...] += jnp.dot(a, weight_block(w_s, i - early), preferred_element_type=jnp.float32)
    for h in range(NH):
        for c in range(3):
            lo = c * NH * HD + h * HD
            to = slice((h * 3 + c) * HD, (h * 3 + c + 1) * HD)
            x = acc_ref[:, lo : lo + HD].astype(jnp.bfloat16)
            own_out[:, to] = x[0:rows]
            send_out[:, to] = x[rows:]
    theirs = pair_head(where_ref[0], side)
    send_out[:, 9 * HD : 12 * HD] = own_out[:, head_columns(theirs, 3)]
    send_out[:, 12 * HD :] = g_ref[:, head_columns(theirs, 1)]
    for i in range(chunks):
        put_half(i).wait()


def project(where, part, own, other, w_early, w5, g):
    rows, depth = own.shape
    chunks = w5.shape[1] // 2
    early = w_early.shape[1] // 2
    vmem = pl.BlockSpec(memory_space=pltpu.VMEM)
    hbm = pl.BlockSpec(memory_space=pltpu.HBM)
    dma = pltpu.SemaphoreType.DMA((chunks,))
    return pl.pallas_call(
        functools.partial(project_kernel, early),
        in_specs=[pl.BlockSpec(memory_space=pltpu.SMEM), vmem, hbm, vmem, vmem, hbm, vmem],
        out_specs=[vmem, vmem, hbm],
        out_shape=[
            jax.ShapeDtypeStruct((rows, 9 * HD), jnp.bfloat16),
            jax.ShapeDtypeStruct((rows, 13 * HD), jnp.bfloat16),
            pltpu.HBM((3,) + w5.shape[1:2] + w5.shape[3:], jnp.bfloat16),
        ],
        scratch_shapes=[
            pltpu.VMEM((chunks - early, rows, depth // chunks), jnp.bfloat16),
            pltpu.VMEM((3, 2 * (chunks - early)) + w5.shape[2:], jnp.bfloat16),
            pltpu.VMEM((2 * rows, 9 * HD), jnp.float32),
            dma,
            dma,
            dma,
        ],
        compiler_params=pltpu.CompilerParams(vmem_limit_bytes=26 * MIB),
        cost_estimate=pl.CostEstimate(flops=7 * 10**9, bytes_accessed=10**7, transcendentals=0),
        name="project",
    )(where, part, own, other, w_early, w5, g)


def pair_head(chip, core):
    return jnp.minimum((chip + 1 + 2 * core) % RING, NH - 1)


def head_columns(head, width):
    return pl.ds(pl.multiple_of(head * (width * HD), width * HD), width * HD)


def section_rows(mod_ref, block, core, rows):
    lines = mod_ref.shape[0]
    mine = (mod_ref[...] == core).astype(jnp.float32)
    line = (lax.broadcasted_iota(jnp.int32, (rows, lines), 0) + block * rows) // HD
    place = (lax.broadcasted_iota(jnp.int32, (rows, HD), 0) + block * rows) % HD
    spread = jnp.dot(
        (line == lax.broadcasted_iota(jnp.int32, (rows, lines), 1)).astype(jnp.float32),
        mine,
        preferred_element_type=jnp.float32,
    )
    return jnp.sum(jnp.where(place == lax.broadcasted_iota(jnp.int32, (rows, HD), 1), spread, 0.0), axis=1, keepdims=True)


def route_kernel(where_ref, mod_ref, own_ref, sent_ref, got_ref, g_ref, pair_out, far_out, stay_out, mask_out):
    chip, core = where_ref[0], where_ref[1]
    rows = own_ref.shape[0]
    masks = [section_rows(mod_ref, 2 * chip + side, core, rows) for side in (core, 1 - core)]
    mine, others = [mask > 0 for mask in masks]
    for block, mask in enumerate(masks):
        mask_out[block] = jnp.broadcast_to(mask, (rows, HD)).astype(jnp.bfloat16)

    def own_rows(head):
        cols = head_columns(head, 3)
        return jnp.where(mine, own_ref[:, cols], got_ref[:, cols]), g_ref[:, head_columns(head, 1)]

    head = pair_head(chip, core)
    pair_out[0, :, : 3 * HD], pair_out[0, :, 3 * HD :] = own_rows(head)
    pair_out[1, :, : 3 * HD] = jnp.where(others, sent_ref[:, head_columns(head, 3)], got_ref[:, 9 * HD : 12 * HD])
    pair_out[1, :, 3 * HD :] = got_ref[:, 12 * HD :]
    far_out[:, : 3 * HD], far_out[:, 3 * HD :] = own_rows(jnp.minimum((chip + 2) % RING, NH - 1))
    stay_out[:, : 3 * HD], stay_out[:, 3 * HD :] = own_rows(jnp.minimum(chip, NH - 1))


def small_call(kernel, name, where, operands, out_shape):
    vmem = pl.BlockSpec(memory_space=pltpu.VMEM)
    return pl.pallas_call(
        kernel,
        in_specs=[pl.BlockSpec(memory_space=pltpu.SMEM)] + [vmem] * len(operands),
        out_specs=[vmem] * len(out_shape),
        out_shape=out_shape,
        compiler_params=pltpu.CompilerParams(vmem_limit_bytes=16 * MIB),
        cost_estimate=pl.CostEstimate(flops=10**6, bytes_accessed=3 * 10**6, transcendentals=0),
        name=name,
    )(where, *operands)


def attention_kernel(
    where_ref, stay, far, pair, stay_o, far_o, pair_o, keep_ref, send_ref, q_s, g_s, k_s, v_s, dq_s, dk_s, dv_s
):
    chip = where_ref[0]
    core = where_ref[1]
    rows = stay.shape[0]
    both = 2 * rows
    near = (chip + 3 + 2 * core) % RING
    across = (chip + 1 + 2 * core) % RING
    opposite = (chip + 2) % RING

    def block_rows(shard, side):
        return pl.ds(pl.multiple_of((2 * shard + side) * rows, rows), rows)

    for shard, r, o in (
        (chip, stay, stay_o),
        (opposite, far, far_o),
        (near, pair.at[0], pair.at[1]),
        (across, pair_o.at[1], pair_o.at[0]),
    ):
        q_s[shard] = r[:, 0:HD]
        g_s[shard] = r[:, 3 * HD : 4 * HD]
        k_s[block_rows(shard, core), :] = r[:, HD : 2 * HD]
        v_s[block_rows(shard, core), :] = r[:, 2 * HD : 3 * HD]
        k_s[block_rows(shard, 1 - core), :] = o[:, HD : 2 * HD]
        v_s[block_rows(shard, 1 - core), :] = o[:, 2 * HD : 3 * HD]
    nt = (((1,), (1,)), ((), ()))
    tn = (((0,), (0,)), ((), ()))
    for s in range(RING - 1, -1, -1):
        width = both * (s + 1)
        q = q_s[s]
        g = g_s[s]
        kk = k_s[0:width, :]
        vv = v_s[0:width, :]
        scores = lax.dot_general(q, kk, nt, preferred_element_type=jnp.float32) * SCALE
        row = lax.broadcasted_iota(jnp.int32, (rows, width), 0) + (2 * s + core) * rows
        col = lax.broadcasted_iota(jnp.int32, (rows, width), 1)
        scores = jnp.where(col <= row, scores, -jnp.inf)
        lifted = jnp.exp(scores - jnp.max(scores, axis=1, keepdims=True))
        probs = lifted / jnp.sum(lifted, axis=1, keepdims=True)
        low = probs.astype(jnp.bfloat16)
        dprobs = lax.dot_general(g, vv, nt, preferred_element_type=jnp.float32)
        row_dot = jnp.sum(probs * dprobs, axis=1, keepdims=True)
        ds = (probs * (dprobs - row_dot)).astype(jnp.bfloat16)
        dq = jnp.dot(ds, kk, preferred_element_type=jnp.float32) * SCALE
        dk = lax.dot_general(ds, q, tn, preferred_element_type=jnp.float32) * SCALE
        dv = lax.dot_general(low, g, tn, preferred_element_type=jnp.float32)
        if s == RING - 1:
            dk_s[...] = dk
            dv_s[...] = dv
        else:
            dk_s[0:width, :] += dk
            dv_s[0:width, :] += dv
        dq_s[s] = dq
    col = 0
    for shard, whole in ((near, True), (near, False), (chip, True), (opposite, True)):
        if whole:
            keep_ref[:, col : col + HD] = dq_s[shard]
            col += HD
        side = core if whole else 1 - core
        keep_ref[:, col : col + HD] = dk_s[block_rows(shard, side), :]
        keep_ref[:, col + HD : col + 2 * HD] = dv_s[block_rows(shard, side), :]
        col += 2 * HD
    col = 0
    for shard, whole in ((across, True), (across, False), (chip, False), (opposite, False)):
        if whole:
            send_ref[:, col : col + HD] = dq_s[shard].astype(jnp.bfloat16)
            col += HD
        side = core if whole else 1 - core
        send_ref[:, col : col + HD] = dk_s[block_rows(shard, side), :].astype(jnp.bfloat16)
        send_ref[:, col + HD : col + 2 * HD] = dv_s[block_rows(shard, side), :].astype(jnp.bfloat16)
        col += 2 * HD


def attention(where, parts):
    rows = parts[0].shape[0]
    total = 2 * RING * rows
    vmem = pl.BlockSpec(memory_space=pltpu.VMEM)
    return pl.pallas_call(
        attention_kernel,
        in_specs=[pl.BlockSpec(memory_space=pltpu.SMEM)] + [vmem] * 6,
        out_specs=[vmem, vmem],
        out_shape=[
            jax.ShapeDtypeStruct((rows, 11 * HD), jnp.float32),
            jax.ShapeDtypeStruct((rows, 9 * HD), jnp.bfloat16),
        ],
        scratch_shapes=[
            pltpu.VMEM((RING, rows, HD), jnp.bfloat16),
            pltpu.VMEM((RING, rows, HD), jnp.bfloat16),
            pltpu.VMEM((total, HD), jnp.bfloat16),
            pltpu.VMEM((total, HD), jnp.bfloat16),
            pltpu.VMEM((RING, rows, HD), jnp.float32),
            pltpu.VMEM((total, HD), jnp.float32),
            pltpu.VMEM((total, HD), jnp.float32),
        ],
        compiler_params=pltpu.CompilerParams(vmem_limit_bytes=32 * MIB),
        cost_estimate=pl.CostEstimate(flops=10**9, bytes_accessed=4 * 10**6, transcendentals=10**6),
        name="attention",
    )(where, *parts)


def combine_kernel(where_ref, keep, got, pair_out, far_out, stay_out):
    def put(out, query, kept, partner):
        out[:, 0:HD] = query.astype(jnp.bfloat16)
        kv = keep[:, kept : kept + 2 * HD] + got[:, partner : partner + 2 * HD].astype(jnp.float32)
        out[:, HD : 3 * HD] = kv.astype(jnp.bfloat16)

    put(pair_out.at[0], keep[:, 0:HD], HD, 3 * HD)
    put(pair_out.at[1], got[:, 0:HD], 3 * HD, HD)
    put(stay_out, keep[:, 5 * HD : 6 * HD], 6 * HD, 5 * HD)
    put(far_out, keep[:, 8 * HD : 9 * HD], 9 * HD, 7 * HD)


def gather(where, mask_ref, parts, out_ref):
    chip, core = where
    stay, far, pair, stay_o, far_o, pair_o = parts
    rows = stay.shape[0]
    for head, refs in (
        (chip, (stay, stay_o)),
        ((chip + 2) % RING, (far, far_o)),
        ((chip + 1 + 2 * core) % RING, (pair.at[0], pair.at[1])),
        ((chip + 3 + 2 * core) % RING, (pair_o.at[1], pair_o.at[0])),
    ):

        @pl.when(head < NH)
        def _():
            for block, x_ref in enumerate(refs):
                for c in range(3):
                    x = x_ref[:, c * HD : (c + 1) * HD]
                    mine = x * mask_ref[block]
                    for side, kept in enumerate((mine, x - mine)):
                        lo = pl.multiple_of(((side * 3 + c) * NH + head) * HD, HD)
                        out_ref[block * rows : (block + 1) * rows, pl.ds(lo, HD)] = kept


def destination(where_ref, i, j):
    core, tp = where_ref[1], where_ref[2]
    dy, dz = jnp.where(core == 0, j, i), jnp.where(core == 0, i, j)
    return (tp // RING + dy) % RING * RING + (tp % RING + dz) % RING


def weight_copies(where_ref, own_hbm, other_hbm, to_ref, sem, hop):
    core = where_ref[1]
    copies = []
    for j in range(RING):
        dest = destination(where_ref, hop, j)
        copies.append(pltpu.make_async_copy(own_hbm.at[:, dest, core], to_ref.at[0, :, j], sem.at[0, j]))
        copies.append(pltpu.make_async_copy(other_hbm.at[:, dest], to_ref.at[1, :, j], sem.at[1, j]))
    return copies


def fetch_kernel(hops, where_ref, after_ref, own_hbm, other_hbm, *refs):
    copies = []
    for i, hop in enumerate(hops):
        copies += weight_copies(where_ref, own_hbm, other_hbm, refs[i], refs[len(hops) + i], hop)
    for copy in copies:
        copy.start()
    for copy in copies:
        copy.wait()


def fetch_weights(where, after, w5, other_half, hops):
    vmem = pl.BlockSpec(memory_space=pltpu.VMEM)
    hbm = pl.BlockSpec(memory_space=pltpu.HBM)
    anywhere = pl.BlockSpec(memory_space=pl.ANY)
    return pl.pallas_call(
        functools.partial(fetch_kernel, hops),
        in_specs=[pl.BlockSpec(memory_space=pltpu.SMEM), vmem, hbm, anywhere],
        out_specs=[vmem for _ in hops],
        out_shape=[pltpu.VMEM((2, 3, RING) + w5.shape[3:], jnp.bfloat16) for _ in hops],
        scratch_shapes=[pltpu.SemaphoreType.DMA((2, RING)) for _ in hops],
        compiler_params=pltpu.CompilerParams(vmem_limit_bytes=20 * MIB),
        cost_estimate=pl.CostEstimate(flops=10**6, bytes_accessed=10**7, transcendentals=0),
        name="fetch_weights",
    )(where, after, w5, other_half)


def product(g_ref, w_ref, outs):
    cols = w_ref.shape[3]
    w = [w_ref[side, c].reshape(RING * cols, NH * HD) for side in range(2) for c in range(3)]
    res = lax.dot_general(
        g_ref[...], jnp.concatenate(w, axis=1), (((1,), (1,)), ((), ())), preferred_element_type=jnp.float32
    ).astype(jnp.bfloat16)
    for i in range(RING):
        outs[i // 2][i % 2] = res[:, i * cols : (i + 1) * cols]


def back_first_kernel(following, where_ref, mask_ref, *refs):
    *parts, w_ref, own_hbm, other_hbm, out_a, out_b, g_ref, next_ref, sem = refs
    for copy in weight_copies(where_ref, own_hbm, other_hbm, next_ref, sem, following):
        copy.start()
    gather((where_ref[0], where_ref[1]), mask_ref, parts, g_ref)
    product(g_ref, w_ref, (out_a, out_b))
    for copy in weight_copies(where_ref, own_hbm, other_hbm, next_ref, sem, following):
        copy.wait()


def back_middle_kernel(g_ref, w_ref, out_a, out_b):
    product(g_ref, w_ref, (out_a, out_b))


def back_last_kernel(after_a, after_b, g_ref, w_ref, out_a, out_b):
    product(g_ref, w_ref, (out_a, out_b))


def back_call(kernel, operands, in_specs, out_shape, scratch):
    vmem = pl.BlockSpec(memory_space=pltpu.VMEM)
    return pl.pallas_call(
        kernel,
        in_specs=in_specs,
        out_specs=[vmem] * len(out_shape),
        out_shape=out_shape,
        scratch_shapes=scratch,
        compiler_params=pltpu.CompilerParams(vmem_limit_bytes=16 * MIB),
        cost_estimate=pl.CostEstimate(flops=10**6, bytes_accessed=10**4, transcendentals=0),
        name="back",
    )(*operands)


def add_kernel(a_ref, b_ref, out_ref):
    out_ref[...] = (a_ref[...].astype(jnp.float32) + b_ref[...].astype(jnp.float32)).astype(jnp.bfloat16)


def add(a, b):
    vmem = pl.BlockSpec(memory_space=pltpu.VMEM)
    return pl.pallas_call(
        add_kernel,
        in_specs=[vmem, vmem],
        out_specs=vmem,
        out_shape=jax.ShapeDtypeStruct(a.shape, jnp.bfloat16),
        compiler_params=pltpu.CompilerParams(vmem_limit_bytes=16 * MIB),
        cost_estimate=pl.CostEstimate(flops=10**5, bytes_accessed=10**4, transcendentals=0),
        name="add",
    )(a, b)


def back_reduced(where, masks, parts, weights, w5, other_half):
    rows = 2 * parts[0].shape[0]
    cols = w5.shape[3]
    smem = pl.BlockSpec(memory_space=pltpu.SMEM)
    vmem = pl.BlockSpec(memory_space=pltpu.VMEM)
    hbm = pl.BlockSpec(memory_space=pltpu.HBM)
    anywhere = pl.BlockSpec(memory_space=pl.ANY)
    halves = [jax.ShapeDtypeStruct((RING // 2, rows, cols), jnp.bfloat16)] * 2
    w_shape = (2, 3, RING) + w5.shape[3:]
    sem = pltpu.SemaphoreType.DMA((2, RING))

    def onward(x):
        return lax.ppermute(x, AXES, ring_perm(True, 1))

    def backward(x):
        return lax.ppermute(x, AXES, ring_perm(True, -1))

    w_two, w_one, w_zero = weights
    two_a, two_b, g, w_three = back_call(
        functools.partial(back_first_kernel, 3),
        (where, masks, *parts, w_two, w5, other_half),
        [smem] + [vmem] * 8 + [hbm, anywhere],
        halves + [pltpu.VMEM((rows, 18 * HD), jnp.bfloat16), pltpu.VMEM(w_shape, jnp.bfloat16)],
        [sem],
    )
    g = pltpu.with_memory_space_constraint(g, pltpu.VMEM)
    w_three = pltpu.with_memory_space_constraint(w_three, pltpu.VMEM)
    relay_a, relay_b = onward(two_a), backward(two_b)
    one_a, one_b = back_call(back_middle_kernel, (g, w_one), [vmem, vmem], halves, [])
    from_one_b = onward(one_b)
    three_a, three_b = back_call(back_middle_kernel, (g, w_three), [vmem, vmem], halves, [])
    from_three_a = backward(three_a)
    one_a = add(one_a, relay_a)
    three_b = add(three_b, relay_b)
    from_one_a, from_three_b = onward(one_a), backward(three_b)
    own_a, own_b = back_call(
        back_last_kernel, (one_a, three_b, g, w_zero), [anywhere, anywhere, vmem, vmem], halves, []
    )
    sum_b = own_b.astype(jnp.float32) + from_one_b.astype(jnp.float32)
    own_a, sum_b = lax.optimization_barrier((own_a, sum_b))
    sum_a = own_a.astype(jnp.float32) + from_three_a.astype(jnp.float32)
    sum_a, sum_b = lax.optimization_barrier((sum_a, sum_b))
    sum_a = sum_a + from_one_a.astype(jnp.float32)
    sum_a, sum_b = lax.optimization_barrier((sum_a, sum_b))
    sum_b = sum_b + from_three_b.astype(jnp.float32)
    return [sum_a[0], sum_a[1], sum_b[0], sum_b[1]]


def ring_perm(first, hop):
    pairs = []
    for s in range(RING):
        for m in range(2):
            for y in range(RING):
                for z in range(RING):
                    if (m == 0) == first:
                        to = (y, (z + hop) % RING)
                    else:
                        to = ((y + hop) % RING, z)
                    base = (s * 2 + m) * RING * RING
                    pairs.append((base + y * RING + z, base + to[0] * RING + to[1]))
    return pairs


def pair_perm(step):
    pairs = []
    for s in range(RING):
        for m in range(2):
            head = (s + (1 if m == 0 else -1)) % RING
            if step > 0 and head < NH:
                pairs.append((2 * s + m, 2 * head + m))
            if step < 0 and s < NH:
                pairs.append((2 * s + m, 2 * ((s + (-1 if m == 0 else 1)) % RING) + m))
    return pairs


def per_device(activations, grad_attn, weights, modality):
    rows, depth = activations.shape
    chip = lax.axis_index("seq")
    core = lax.axis_index("mod")
    tp = lax.axis_index("tp")
    where = jnp.stack([chip, core, tp]).astype(jnp.int32)
    dests = RING * RING
    cols = depth // dests // 2
    w5 = jnp.transpose(weights[0], (1, 0, 2)).reshape(3, dests, 2, cols, NH * HD)

    mod = modality.reshape(-1, HD)
    w5 = pltpu.with_memory_space_constraint(w5, pltpu.HBM)
    activations = pltpu.with_memory_space_constraint(activations, pltpu.HBM)
    act_other = pltpu.with_memory_space_constraint(core_swap(activations), pltpu.VMEM)
    part, w_early = project_own(activations, w5, 4)
    w_early = pltpu.with_memory_space_constraint(w_early, pltpu.VMEM)
    proj_own, sent, half = project(where, part, activations, act_other, w_early, w5, grad_attn)
    got = core_swap(sent)
    got, half = lax.optimization_barrier((got, half))
    other_half = core_swap(half)

    def part_shapes(width):
        block = jax.ShapeDtypeStruct((rows, width), jnp.bfloat16)
        return [jax.ShapeDtypeStruct((2, rows, width), jnp.bfloat16), block, block]

    pair, far, stay, masks = small_call(
        route_kernel,
        "route",
        where,
        (mod, proj_own, sent, got, grad_attn),
        part_shapes(4 * HD) + [jax.ShapeDtypeStruct((2, rows, HD), jnp.bfloat16)],
    )
    pair = lax.ppermute(pair, ("seq", "mod"), pair_perm(1))
    far = lax.ppermute(far, "seq", [(i, (i + 2) % RING) for i in range(RING) if (i + 2) % RING < NH])
    parts = [stay, far, pair]
    keep, send = attention(where, parts + [core_swap(x) for x in parts])
    pair, far, stay = small_call(combine_kernel, "combine", where, (keep, core_swap(send)), part_shapes(3 * HD))

    w_first = fetch_weights(where, stay, w5, other_half, (2, 1, 0))
    w_first = [pltpu.with_memory_space_constraint(w, pltpu.VMEM) for w in w_first]
    pair = lax.ppermute(pair, ("seq", "mod"), pair_perm(-1))
    far = lax.ppermute(far, "seq", [(i, (i + 2) % RING) for i in range(NH)])
    pair, far, w_first = lax.optimization_barrier((pair, far, w_first))
    parts = [stay, far, pair]
    parts += [core_swap(x) for x in parts]

    total = back_reduced(where, masks, parts, w_first, w5, other_half)
    result = total[0]
    for hop in (1, 3, 2):
        got = lax.ppermute(total[hop].astype(jnp.bfloat16), AXES, ring_perm(False, hop))
        result = lax.optimization_barrier(result) + got.astype(jnp.float32)
    result = result.astype(jnp.bfloat16)
    mine = result[:rows]
    theirs = core_swap(result[rows:])
    return jnp.where(
        core == 0, jnp.concatenate([mine, theirs], axis=1), jnp.concatenate([theirs, mine], axis=1)
    )


def solution(mesh):
    in_specs = (P(("seq", "mod"), None), P(("seq", "mod"), "tp"), P("mod", None, None, "tp"), P())
    out_specs = P(("seq", "mod"), "tp")
    return jax.shard_map(
        per_device, mesh=mesh, in_specs=in_specs, out_specs=out_specs, check_vma=False
    )
```

```python
import functools

import jax
import jax.numpy as jnp
from jax import lax
from jax.experimental import pallas as pl
from jax.experimental.pallas import tpu as pltpu
from jax.sharding import PartitionSpec as P

HD = 128
NH = 3
RING = 4
SCALE = HD**-0.5
SECOND = (2, 0, 1, 3)
AXES = ("seq", "mod", "tp")
MIB = 1024 * 1024


def core_swap(x):
    return lax.ppermute(x, "mod", [(0, 1), (1, 0)])


def weight_block(w_ref, i):
    size = 4 * w_ref.shape[3]
    return jnp.concatenate([w_ref[c, 2 * i : 2 * i + 2].reshape(size, NH * HD) for c in range(3)], axis=1)


def own_kernel(a_hbm, w_hbm, part_ref, w_ref, a_s, a_sem, w_sem):
    chunks = w_ref.shape[1] // 2
    block = 4 * w_ref.shape[3]

    def fetch(i):
        pair = slice(2 * i, 2 * i + 2)
        return (
            pltpu.make_async_copy(a_hbm.at[:, pl.ds(i * block, block)], a_s.at[i], a_sem.at[i]),
            pltpu.make_async_copy(w_hbm.at[:, pair], w_ref.at[:, pair], w_sem.at[i]),
        )

    for i in range(chunks):
        for copy in fetch(i):
            copy.start()
    for i in range(chunks):
        for copy in fetch(i):
            copy.wait()
        part = jnp.dot(a_s[i], weight_block(w_ref, i), preferred_element_type=jnp.float32)
        if i == 0:
            part_ref[...] = part
        else:
            part_ref[...] += part


def project_own(a, w5, early):
    rows = a.shape[0]
    block = 4 * w5.shape[3]
    vmem = pl.BlockSpec(memory_space=pltpu.VMEM)
    hbm = pl.BlockSpec(memory_space=pltpu.HBM)
    return pl.pallas_call(
        own_kernel,
        in_specs=[hbm, hbm],
        out_specs=[vmem, vmem],
        out_shape=[
            jax.ShapeDtypeStruct((rows, 9 * HD), jnp.float32),
            pltpu.VMEM((3, 2 * early) + w5.shape[2:], jnp.bfloat16),
        ],
        scratch_shapes=[
            pltpu.VMEM((early, rows, block), jnp.bfloat16),
            pltpu.SemaphoreType.DMA((early,)),
            pltpu.SemaphoreType.DMA((early,)),
        ],
        compiler_params=pltpu.CompilerParams(vmem_limit_bytes=20 * MIB),
        cost_estimate=pl.CostEstimate(flops=4 * 10**9, bytes_accessed=10**7, transcendentals=0),
        name="project_own",
    )(a, w5)


def project_kernel(
    early, where_ref, part_ref, own_hbm, oth_ref, w_ref, w_hbm, g_ref, own_out, send_out, half_hbm, a_s, w_s, acc_ref,
    own_sem, w_sem, half_sem
):
    rows = part_ref.shape[0]
    chunks = half_hbm.shape[1] // 2
    block = 4 * w_ref.shape[3]
    side = 1 - where_ref[1]

    def fetch_own(i):
        return pltpu.make_async_copy(own_hbm.at[:, pl.ds(i * block, block)], a_s.at[i - early], own_sem.at[i])

    def other(i):
        return oth_ref[:, i * block : (i + 1) * block]

    def fetch_weights(i):
        src = w_hbm.at[:, 2 * i : 2 * i + 2]
        return pltpu.make_async_copy(src, w_s.at[:, 2 * (i - early) : 2 * (i - early) + 2], w_sem.at[i])

    def put_half(i):
        if i < early:
            src = w_ref.at[:, 2 * i : 2 * i + 2, side]
        else:
            src = w_s.at[:, 2 * (i - early) : 2 * (i - early) + 2, side]
        return pltpu.make_async_copy(src, half_hbm.at[:, 2 * i : 2 * i + 2], half_sem.at[i])

    for i in range(early, chunks):
        fetch_weights(i).start()
        fetch_own(i).start()
    for i in range(early):
        put_half(i).start()
    acc_ref[0:rows] = part_ref[...]
    for i in range(chunks):
        if i < early:
            part = jnp.dot(other(i), weight_block(w_ref, i), preferred_element_type=jnp.float32)
            if i == 0:
                acc_ref[rows:] = part
            else:
                acc_ref[rows:] += part
        else:
            fetch_own(i).wait()
            fetch_weights(i).wait()
            put_half(i).start()
            a = jnp.concatenate([a_s[i - early], other(i)], axis=0)
            acc_ref[...] += jnp.dot(a, weight_block(w_s, i - early), preferred_element_type=jnp.float32)
    for h in range(NH):
        for c in range(3):
            lo = c * NH * HD + h * HD
            to = slice((h * 3 + c) * HD, (h * 3 + c + 1) * HD)
            x = acc_ref[:, lo : lo + HD].astype(jnp.bfloat16)
            own_out[:, to] = x[0:rows]
            send_out[:, to] = x[rows:]
    theirs = pair_head(where_ref[0], side)
    send_out[:, 9 * HD : 12 * HD] = own_out[:, head_columns(theirs, 3)]
    send_out[:, 12 * HD :] = g_ref[:, head_columns(theirs, 1)]
    for i in range(chunks):
        put_half(i).wait()


def project(where, part, own, other, w_early, w5, g):
    rows, depth = own.shape
    chunks = w5.shape[1] // 2
    early = w_early.shape[1] // 2
    vmem = pl.BlockSpec(memory_space=pltpu.VMEM)
    hbm = pl.BlockSpec(memory_space=pltpu.HBM)
    dma = pltpu.SemaphoreType.DMA((chunks,))
    return pl.pallas_call(
        functools.partial(project_kernel, early),
        in_specs=[pl.BlockSpec(memory_space=pltpu.SMEM), vmem, hbm, vmem, vmem, hbm, vmem],
        out_specs=[vmem, vmem, hbm],
        out_shape=[
            jax.ShapeDtypeStruct((rows, 9 * HD), jnp.bfloat16),
            jax.ShapeDtypeStruct((rows, 13 * HD), jnp.bfloat16),
            pltpu.HBM((3,) + w5.shape[1:2] + w5.shape[3:], jnp.bfloat16),
        ],
        scratch_shapes=[
            pltpu.VMEM((chunks - early, rows, depth // chunks), jnp.bfloat16),
            pltpu.VMEM((3, 2 * (chunks - early)) + w5.shape[2:], jnp.bfloat16),
            pltpu.VMEM((2 * rows, 9 * HD), jnp.float32),
            dma,
            dma,
            dma,
        ],
        compiler_params=pltpu.CompilerParams(vmem_limit_bytes=26 * MIB),
        cost_estimate=pl.CostEstimate(flops=7 * 10**9, bytes_accessed=10**7, transcendentals=0),
        name="project",
    )(where, part, own, other, w_early, w5, g)


def pair_head(chip, core):
    return jnp.minimum((chip + 1 + 2 * core) % RING, NH - 1)


def head_columns(head, width):
    return pl.ds(pl.multiple_of(head * (width * HD), width * HD), width * HD)


def section_rows(mod_ref, block, core, rows):
    lines = mod_ref.shape[0]
    mine = (mod_ref[...] == core).astype(jnp.float32)
    line = (lax.broadcasted_iota(jnp.int32, (rows, lines), 0) + block * rows) // HD
    place = (lax.broadcasted_iota(jnp.int32, (rows, HD), 0) + block * rows) % HD
    spread = jnp.dot(
        (line == lax.broadcasted_iota(jnp.int32, (rows, lines), 1)).astype(jnp.float32),
        mine,
        preferred_element_type=jnp.float32,
    )
    return jnp.sum(jnp.where(place == lax.broadcasted_iota(jnp.int32, (rows, HD), 1), spread, 0.0), axis=1, keepdims=True)


def route_kernel(where_ref, mod_ref, own_ref, sent_ref, got_ref, g_ref, pair_out, far_out, stay_out, mask_out):
    chip, core = where_ref[0], where_ref[1]
    rows = own_ref.shape[0]
    masks = [section_rows(mod_ref, 2 * chip + side, core, rows) for side in (core, 1 - core)]
    mine, others = [mask > 0 for mask in masks]
    for block, mask in enumerate(masks):
        mask_out[block] = jnp.broadcast_to(mask, (rows, HD)).astype(jnp.bfloat16)

    def own_rows(head):
        cols = head_columns(head, 3)
        return jnp.where(mine, own_ref[:, cols], got_ref[:, cols]), g_ref[:, head_columns(head, 1)]

    head = pair_head(chip, core)
    pair_out[0, :, : 3 * HD], pair_out[0, :, 3 * HD :] = own_rows(head)
    pair_out[1, :, : 3 * HD] = jnp.where(others, sent_ref[:, head_columns(head, 3)], got_ref[:, 9 * HD : 12 * HD])
    pair_out[1, :, 3 * HD :] = got_ref[:, 12 * HD :]
    far_out[:, : 3 * HD], far_out[:, 3 * HD :] = own_rows(jnp.minimum((chip + 2) % RING, NH - 1))
    stay_out[:, : 3 * HD], stay_out[:, 3 * HD :] = own_rows(jnp.minimum(chip, NH - 1))


def small_call(kernel, name, where, operands, out_shape):
    vmem = pl.BlockSpec(memory_space=pltpu.VMEM)
    return pl.pallas_call(
        kernel,
        in_specs=[pl.BlockSpec(memory_space=pltpu.SMEM)] + [vmem] * len(operands),
        out_specs=[vmem] * len(out_shape),
        out_shape=out_shape,
        compiler_params=pltpu.CompilerParams(vmem_limit_bytes=16 * MIB),
        cost_estimate=pl.CostEstimate(flops=10**6, bytes_accessed=3 * 10**6, transcendentals=0),
        name=name,
    )(where, *operands)


def attention_kernel(
    where_ref, stay, far, pair, stay_o, far_o, pair_o, keep_ref, send_ref, q_s, g_s, k_s, v_s, dq_s, dk_s, dv_s
):
    chip = where_ref[0]
    core = where_ref[1]
    rows = stay.shape[0]
    both = 2 * rows
    near = (chip + 3 + 2 * core) % RING
    across = (chip + 1 + 2 * core) % RING
    opposite = (chip + 2) % RING

    def block_rows(shard, side):
        return pl.ds(pl.multiple_of((2 * shard + side) * rows, rows), rows)

    for shard, r, o in (
        (chip, stay, stay_o),
        (opposite, far, far_o),
        (near, pair.at[0], pair.at[1]),
        (across, pair_o.at[1], pair_o.at[0]),
    ):
        q_s[shard] = r[:, 0:HD]
        g_s[shard] = r[:, 3 * HD : 4 * HD]
        k_s[block_rows(shard, core), :] = r[:, HD : 2 * HD]
        v_s[block_rows(shard, core), :] = r[:, 2 * HD : 3 * HD]
        k_s[block_rows(shard, 1 - core), :] = o[:, HD : 2 * HD]
        v_s[block_rows(shard, 1 - core), :] = o[:, 2 * HD : 3 * HD]
    nt = (((1,), (1,)), ((), ()))
    tn = (((0,), (0,)), ((), ()))
    for s in range(RING - 1, -1, -1):
        width = both * (s + 1)
        q = q_s[s]
        g = g_s[s]
        kk = k_s[0:width, :]
        vv = v_s[0:width, :]
        scores = lax.dot_general(q, kk, nt, preferred_element_type=jnp.float32) * SCALE
        row = lax.broadcasted_iota(jnp.int32, (rows, width), 0) + (2 * s + core) * rows
        col = lax.broadcasted_iota(jnp.int32, (rows, width), 1)
        scores = jnp.where(col <= row, scores, -jnp.inf)
        lifted = jnp.exp(scores - jnp.max(scores, axis=1, keepdims=True))
        probs = lifted / jnp.sum(lifted, axis=1, keepdims=True)
        low = probs.astype(jnp.bfloat16)
        dprobs = lax.dot_general(g, vv, nt, preferred_element_type=jnp.float32)
        row_dot = jnp.sum(probs * dprobs, axis=1, keepdims=True)
        ds = (probs * (dprobs - row_dot)).astype(jnp.bfloat16)
        dq = jnp.dot(ds, kk, preferred_element_type=jnp.float32) * SCALE
        dk = lax.dot_general(ds, q, tn, preferred_element_type=jnp.float32) * SCALE
        dv = lax.dot_general(low, g, tn, preferred_element_type=jnp.float32)
        if s == RING - 1:
            dk_s[...] = dk
            dv_s[...] = dv
        else:
            dk_s[0:width, :] += dk
            dv_s[0:width, :] += dv
        dq_s[s] = dq
    col = 0
    for shard, whole in ((near, True), (near, False), (chip, True), (opposite, True)):
        if whole:
            keep_ref[:, col : col + HD] = dq_s[shard]
            col += HD
        side = core if whole else 1 - core
        keep_ref[:, col : col + HD] = dk_s[block_rows(shard, side), :]
        keep_ref[:, col + HD : col + 2 * HD] = dv_s[block_rows(shard, side), :]
        col += 2 * HD
    col = 0
    for shard, whole in ((across, True), (across, False), (chip, False), (opposite, False)):
        if whole:
            send_ref[:, col : col + HD] = dq_s[shard].astype(jnp.bfloat16)
            col += HD
        side = core if whole else 1 - core
        send_ref[:, col : col + HD] = dk_s[block_rows(shard, side), :].astype(jnp.bfloat16)
        send_ref[:, col + HD : col + 2 * HD] = dv_s[block_rows(shard, side), :].astype(jnp.bfloat16)
        col += 2 * HD


def attention(where, parts):
    rows = parts[0].shape[0]
    total = 2 * RING * rows
    vmem = pl.BlockSpec(memory_space=pltpu.VMEM)
    return pl.pallas_call(
        attention_kernel,
        in_specs=[pl.BlockSpec(memory_space=pltpu.SMEM)] + [vmem] * 6,
        out_specs=[vmem, vmem],
        out_shape=[
            jax.ShapeDtypeStruct((rows, 11 * HD), jnp.float32),
            jax.ShapeDtypeStruct((rows, 9 * HD), jnp.bfloat16),
        ],
        scratch_shapes=[
            pltpu.VMEM((RING, rows, HD), jnp.bfloat16),
            pltpu.VMEM((RING, rows, HD), jnp.bfloat16),
            pltpu.VMEM((total, HD), jnp.bfloat16),
            pltpu.VMEM((total, HD), jnp.bfloat16),
            pltpu.VMEM((RING, rows, HD), jnp.float32),
            pltpu.VMEM((total, HD), jnp.float32),
            pltpu.VMEM((total, HD), jnp.float32),
        ],
        compiler_params=pltpu.CompilerParams(vmem_limit_bytes=32 * MIB),
        cost_estimate=pl.CostEstimate(flops=10**9, bytes_accessed=4 * 10**6, transcendentals=10**6),
        name="attention",
    )(where, *parts)


def combine_kernel(where_ref, keep, got, pair_out, far_out, stay_out):
    def put(out, query, kept, partner):
        out[:, 0:HD] = query.astype(jnp.bfloat16)
        kv = keep[:, kept : kept + 2 * HD] + got[:, partner : partner + 2 * HD].astype(jnp.float32)
        out[:, HD : 3 * HD] = kv.astype(jnp.bfloat16)

    put(pair_out.at[0], keep[:, 0:HD], HD, 3 * HD)
    put(pair_out.at[1], got[:, 0:HD], 3 * HD, HD)
    put(stay_out, keep[:, 5 * HD : 6 * HD], 6 * HD, 5 * HD)
    put(far_out, keep[:, 8 * HD : 9 * HD], 9 * HD, 7 * HD)


def gather(where, mask_ref, parts, out_ref):
    chip, core = where
    stay, far, pair, stay_o, far_o, pair_o = parts
    rows = stay.shape[0]
    for head, refs in (
        (chip, (stay, stay_o)),
        ((chip + 2) % RING, (far, far_o)),
        ((chip + 1 + 2 * core) % RING, (pair.at[0], pair.at[1])),
        ((chip + 3 + 2 * core) % RING, (pair_o.at[1], pair_o.at[0])),
    ):

        @pl.when(head < NH)
        def _():
            for block, x_ref in enumerate(refs):
                for c in range(3):
                    x = x_ref[:, c * HD : (c + 1) * HD]
                    mine = x * mask_ref[block]
                    for side, kept in enumerate((mine, x - mine)):
                        lo = pl.multiple_of(((side * 3 + c) * NH + head) * HD, HD)
                        out_ref[block * rows : (block + 1) * rows, pl.ds(lo, HD)] = kept


def destination(where_ref, i, j):
    core, tp = where_ref[1], where_ref[2]
    dy, dz = jnp.where(core == 0, j, i), jnp.where(core == 0, i, j)
    return (tp // RING + dy) % RING * RING + (tp % RING + dz) % RING


def weight_copies(where_ref, own_hbm, other_hbm, to_ref, sem, hop):
    core = where_ref[1]
    copies = []
    for j in range(RING):
        dest = destination(where_ref, hop, SECOND[j])
        copies.append(pltpu.make_async_copy(own_hbm.at[:, dest, core], to_ref.at[0, :, j], sem.at[0, j]))
        copies.append(pltpu.make_async_copy(other_hbm.at[:, dest], to_ref.at[1, :, j], sem.at[1, j]))
    return copies


def fetch_kernel(hops, where_ref, after_ref, own_hbm, other_hbm, *refs):
    copies = []
    for i, hop in enumerate(hops):
        copies += weight_copies(where_ref, own_hbm, other_hbm, refs[i], refs[len(hops) + i], hop)
    for copy in copies:
        copy.start()
    for copy in copies:
        copy.wait()


def fetch_weights(where, after, w5, other_half, hops):
    vmem = pl.BlockSpec(memory_space=pltpu.VMEM)
    hbm = pl.BlockSpec(memory_space=pltpu.HBM)
    anywhere = pl.BlockSpec(memory_space=pl.ANY)
    return pl.pallas_call(
        functools.partial(fetch_kernel, hops),
        in_specs=[pl.BlockSpec(memory_space=pltpu.SMEM), vmem, hbm, anywhere],
        out_specs=[vmem for _ in hops],
        out_shape=[pltpu.VMEM((2, 3, RING) + w5.shape[3:], jnp.bfloat16) for _ in hops],
        scratch_shapes=[pltpu.SemaphoreType.DMA((2, RING)) for _ in hops],
        compiler_params=pltpu.CompilerParams(vmem_limit_bytes=20 * MIB),
        cost_estimate=pl.CostEstimate(flops=10**6, bytes_accessed=10**7, transcendentals=0),
        name="fetch_weights",
    )(where, after, w5, other_half)


def product(g_ref, w_ref, outs):
    cols = w_ref.shape[3]
    w = [w_ref[side, c].reshape(RING * cols, NH * HD) for side in range(2) for c in range(3)]
    res = lax.dot_general(
        g_ref[...], jnp.concatenate(w, axis=1), (((1,), (1,)), ((), ())), preferred_element_type=jnp.float32
    ).astype(jnp.bfloat16)
    for i in range(RING):
        outs[i // 2][i % 2] = res[:, i * cols : (i + 1) * cols]


def back_first_kernel(following, where_ref, mask_ref, *refs):
    *parts, w_ref, own_hbm, other_hbm, out_a, out_b, g_ref, next_ref, sem = refs
    for copy in weight_copies(where_ref, own_hbm, other_hbm, next_ref, sem, following):
        copy.start()
    gather((where_ref[0], where_ref[1]), mask_ref, parts, g_ref)
    product(g_ref, w_ref, (out_a, out_b))
    for copy in weight_copies(where_ref, own_hbm, other_hbm, next_ref, sem, following):
        copy.wait()


def back_middle_kernel(g_ref, w_ref, out_a, out_b):
    product(g_ref, w_ref, (out_a, out_b))


def back_last_kernel(after_a, after_b, g_ref, w_ref, out_a, out_b):
    product(g_ref, w_ref, (out_a, out_b))


def back_call(kernel, operands, in_specs, out_shape, scratch):
    vmem = pl.BlockSpec(memory_space=pltpu.VMEM)
    return pl.pallas_call(
        kernel,
        in_specs=in_specs,
        out_specs=[vmem] * len(out_shape),
        out_shape=out_shape,
        scratch_shapes=scratch,
        compiler_params=pltpu.CompilerParams(vmem_limit_bytes=16 * MIB),
        cost_estimate=pl.CostEstimate(flops=10**6, bytes_accessed=10**4, transcendentals=0),
        name="back",
    )(*operands)


def add_kernel(a_ref, b_ref, out_ref):
    out_ref[...] = (a_ref[...].astype(jnp.float32) + b_ref[...].astype(jnp.float32)).astype(jnp.bfloat16)


def add(a, b):
    vmem = pl.BlockSpec(memory_space=pltpu.VMEM)
    return pl.pallas_call(
        add_kernel,
        in_specs=[vmem, vmem],
        out_specs=vmem,
        out_shape=jax.ShapeDtypeStruct(a.shape, jnp.bfloat16),
        compiler_params=pltpu.CompilerParams(vmem_limit_bytes=16 * MIB),
        cost_estimate=pl.CostEstimate(flops=10**5, bytes_accessed=10**4, transcendentals=0),
        name="add",
    )(a, b)


def back_reduced(where, masks, parts, weights, w5, other_half):
    rows = 2 * parts[0].shape[0]
    cols = w5.shape[3]
    smem = pl.BlockSpec(memory_space=pltpu.SMEM)
    vmem = pl.BlockSpec(memory_space=pltpu.VMEM)
    hbm = pl.BlockSpec(memory_space=pltpu.HBM)
    anywhere = pl.BlockSpec(memory_space=pl.ANY)
    halves = [jax.ShapeDtypeStruct((RING // 2, rows, cols), jnp.bfloat16)] * 2
    w_shape = (2, 3, RING) + w5.shape[3:]
    sem = pltpu.SemaphoreType.DMA((2, RING))

    def onward(x):
        return lax.ppermute(x, AXES, ring_perm(True, 1))

    def backward(x):
        return lax.ppermute(x, AXES, ring_perm(True, -1))

    w_two, w_one, w_zero = weights
    two_a, two_b, g, w_three = back_call(
        functools.partial(back_first_kernel, 3),
        (where, masks, *parts, w_two, w5, other_half),
        [smem] + [vmem] * 8 + [hbm, anywhere],
        halves + [pltpu.VMEM((rows, 18 * HD), jnp.bfloat16), pltpu.VMEM(w_shape, jnp.bfloat16)],
        [sem],
    )
    g = pltpu.with_memory_space_constraint(g, pltpu.VMEM)
    w_three = pltpu.with_memory_space_constraint(w_three, pltpu.VMEM)
    relay_a, relay_b = onward(two_a), backward(two_b)
    one_a, one_b = back_call(back_middle_kernel, (g, w_one), [vmem, vmem], halves, [])
    from_one_b = onward(one_b)
    three_a, three_b = back_call(back_middle_kernel, (g, w_three), [vmem, vmem], halves, [])
    from_three_a = backward(three_a)
    one_a = add(one_a, relay_a)
    three_b = add(three_b, relay_b)
    from_one_a, from_three_b = onward(one_a), backward(three_b)
    own_a, own_b = back_call(
        back_last_kernel, (one_a, three_b, g, w_zero), [anywhere, anywhere, vmem, vmem], halves, []
    )
    sum_b = own_b.astype(jnp.float32) + from_one_b.astype(jnp.float32)
    own_a, sum_b = lax.optimization_barrier((own_a, sum_b))
    sum_a = own_a.astype(jnp.float32) + from_three_a.astype(jnp.float32)
    sum_a, sum_b = lax.optimization_barrier((sum_a, sum_b))
    sum_a = sum_a + from_one_a.astype(jnp.float32)
    sum_a, sum_b = lax.optimization_barrier((sum_a, sum_b))
    sum_b = sum_b + from_three_b.astype(jnp.float32)
    return dict(zip(SECOND, (sum_a[0], sum_a[1], sum_b[0], sum_b[1])))


def ring_perm(first, hop):
    pairs = []
    for s in range(RING):
        for m in range(2):
            for y in range(RING):
                for z in range(RING):
                    if (m == 0) == first:
                        to = (y, (z + hop) % RING)
                    else:
                        to = ((y + hop) % RING, z)
                    base = (s * 2 + m) * RING * RING
                    pairs.append((base + y * RING + z, base + to[0] * RING + to[1]))
    return pairs


def pair_perm(step):
    pairs = []
    for s in range(RING):
        for m in range(2):
            head = (s + (1 if m == 0 else -1)) % RING
            if step > 0 and head < NH:
                pairs.append((2 * s + m, 2 * head + m))
            if step < 0 and s < NH:
                pairs.append((2 * s + m, 2 * ((s + (-1 if m == 0 else 1)) % RING) + m))
    return pairs


def per_device(activations, grad_attn, weights, modality):
    rows, depth = activations.shape
    chip = lax.axis_index("seq")
    core = lax.axis_index("mod")
    tp = lax.axis_index("tp")
    where = jnp.stack([chip, core, tp]).astype(jnp.int32)
    dests = RING * RING
    cols = depth // dests // 2
    w5 = jnp.transpose(weights[0], (1, 0, 2)).reshape(3, dests, 2, cols, NH * HD)

    mod = modality.reshape(-1, HD)
    w5 = pltpu.with_memory_space_constraint(w5, pltpu.HBM)
    activations = pltpu.with_memory_space_constraint(activations, pltpu.HBM)
    act_other = pltpu.with_memory_space_constraint(core_swap(activations), pltpu.VMEM)
    part, w_early = project_own(activations, w5, 4)
    w_early = pltpu.with_memory_space_constraint(w_early, pltpu.VMEM)
    proj_own, sent, half = project(where, part, activations, act_other, w_early, w5, grad_attn)
    got = core_swap(sent)
    got, half = lax.optimization_barrier((got, half))
    other_half = core_swap(half)

    def part_shapes(width):
        block = jax.ShapeDtypeStruct((rows, width), jnp.bfloat16)
        return [jax.ShapeDtypeStruct((2, rows, width), jnp.bfloat16), block, block]

    pair, far, stay, masks = small_call(
        route_kernel,
        "route",
        where,
        (mod, proj_own, sent, got, grad_attn),
        part_shapes(4 * HD) + [jax.ShapeDtypeStruct((2, rows, HD), jnp.bfloat16)],
    )
    pair = lax.ppermute(pair, ("seq", "mod"), pair_perm(1))
    far = lax.ppermute(far, "seq", [(i, (i + 2) % RING) for i in range(RING) if (i + 2) % RING < NH])
    parts = [stay, far, pair]
    keep, send = attention(where, parts + [core_swap(x) for x in parts])
    pair, far, stay = small_call(combine_kernel, "combine", where, (keep, core_swap(send)), part_shapes(3 * HD))

    w_first = fetch_weights(where, stay, w5, other_half, (2, 1, 0))
    w_first = [pltpu.with_memory_space_constraint(w, pltpu.VMEM) for w in w_first]
    pair = lax.ppermute(pair, ("seq", "mod"), pair_perm(-1))
    far = lax.ppermute(far, "seq", [(i, (i + 2) % RING) for i in range(NH)])
    pair, far, w_first = lax.optimization_barrier((pair, far, w_first))
    parts = [stay, far, pair]
    parts += [core_swap(x) for x in parts]

    total = back_reduced(where, masks, parts, w_first, w5, other_half)
    two = total[2].astype(jnp.bfloat16)
    relay_a = lax.ppermute(two[:rows], AXES, ring_perm(False, 1))
    relay_b = lax.ppermute(two[rows:], AXES, ring_perm(False, -1))
    one = jnp.concatenate([total[1][:rows] + relay_a.astype(jnp.float32), total[1][rows:]], axis=0)
    three = jnp.concatenate([total[3][:rows], total[3][rows:] + relay_b.astype(jnp.float32)], axis=0)
    from_one = lax.ppermute(one.astype(jnp.bfloat16), AXES, ring_perm(False, 1))
    from_three = lax.ppermute(three.astype(jnp.bfloat16), AXES, ring_perm(False, -1))
    result = total[0] + from_one.astype(jnp.float32) + from_three.astype(jnp.float32)
    result = result.astype(jnp.bfloat16)
    mine = result[:rows]
    theirs = core_swap(result[rows:])
    return jnp.where(
        core == 0, jnp.concatenate([mine, theirs], axis=1), jnp.concatenate([theirs, mine], axis=1)
    )


def solution(mesh):
    in_specs = (P(("seq", "mod"), None), P(("seq", "mod"), "tp"), P("mod", None, None, "tp"), P())
    out_specs = P(("seq", "mod"), "tp")
    return jax.shard_map(
        per_device, mesh=mesh, in_specs=in_specs, out_specs=out_specs, check_vma=False
    )
```

```python
import functools

import jax
import jax.numpy as jnp
from jax import lax
from jax.experimental import pallas as pl
from jax.experimental.pallas import tpu as pltpu
from jax.sharding import PartitionSpec as P

HD = 128
NH = 3
RING = 4
SCALE = HD**-0.5
AXES = ("seq", "mod", "tp")
MIB = 1024 * 1024


def core_swap(x):
    return lax.ppermute(x, "mod", [(0, 1), (1, 0)])


def weight_block(w_ref, i):
    size = 4 * w_ref.shape[3]
    return jnp.concatenate([w_ref[c, 2 * i : 2 * i + 2].reshape(size, NH * HD) for c in range(3)], axis=1)


def own_kernel(a_hbm, w_hbm, part_ref, w_ref, a_s, a_sem, w_sem):
    chunks = w_ref.shape[1] // 2
    block = 4 * w_ref.shape[3]

    def fetch(i):
        pair = slice(2 * i, 2 * i + 2)
        return (
            pltpu.make_async_copy(a_hbm.at[:, pl.ds(i * block, block)], a_s.at[i], a_sem.at[i]),
            pltpu.make_async_copy(w_hbm.at[:, pair], w_ref.at[:, pair], w_sem.at[i]),
        )

    for i in range(chunks):
        for copy in fetch(i):
            copy.start()
    for i in range(chunks):
        for copy in fetch(i):
            copy.wait()
        part = jnp.dot(a_s[i], weight_block(w_ref, i), preferred_element_type=jnp.float32)
        if i == 0:
            part_ref[...] = part
        else:
            part_ref[...] += part


def project_own(a, w5, early):
    rows = a.shape[0]
    block = 4 * w5.shape[3]
    vmem = pl.BlockSpec(memory_space=pltpu.VMEM)
    hbm = pl.BlockSpec(memory_space=pltpu.HBM)
    return pl.pallas_call(
        own_kernel,
        in_specs=[hbm, hbm],
        out_specs=[vmem, vmem],
        out_shape=[
            jax.ShapeDtypeStruct((rows, 9 * HD), jnp.float32),
            pltpu.VMEM((3, 2 * early) + w5.shape[2:], jnp.bfloat16),
        ],
        scratch_shapes=[
            pltpu.VMEM((early, rows, block), jnp.bfloat16),
            pltpu.SemaphoreType.DMA((early,)),
            pltpu.SemaphoreType.DMA((early,)),
        ],
        compiler_params=pltpu.CompilerParams(vmem_limit_bytes=20 * MIB),
        cost_estimate=pl.CostEstimate(flops=4 * 10**9, bytes_accessed=10**7, transcendentals=0),
        name="project_own",
    )(a, w5)


def project_kernel(
    early, where_ref, part_ref, own_hbm, oth_ref, w_ref, w_hbm, g_ref, own_out, send_out, half_hbm, a_s, w_s, acc_ref,
    own_sem, w_sem, half_sem
):
    rows = part_ref.shape[0]
    chunks = half_hbm.shape[1] // 2
    block = 4 * w_ref.shape[3]
    side = 1 - where_ref[1]

    def fetch_own(i):
        return pltpu.make_async_copy(own_hbm.at[:, pl.ds(i * block, block)], a_s.at[i - early], own_sem.at[i])

    def other(i):
        return oth_ref[:, i * block : (i + 1) * block]

    def fetch_weights(i):
        src = w_hbm.at[:, 2 * i : 2 * i + 2]
        return pltpu.make_async_copy(src, w_s.at[:, 2 * (i - early) : 2 * (i - early) + 2], w_sem.at[i])

    def put_half(i):
        if i < early:
            src = w_ref.at[:, 2 * i : 2 * i + 2, side]
        else:
            src = w_s.at[:, 2 * (i - early) : 2 * (i - early) + 2, side]
        return pltpu.make_async_copy(src, half_hbm.at[:, 2 * i : 2 * i + 2], half_sem.at[i])

    for i in range(early, chunks):
        fetch_weights(i).start()
        fetch_own(i).start()
    for i in range(early):
        put_half(i).start()
    acc_ref[0:rows] = part_ref[...]
    for i in range(chunks):
        if i < early:
            part = jnp.dot(other(i), weight_block(w_ref, i), preferred_element_type=jnp.float32)
            if i == 0:
                acc_ref[rows:] = part
            else:
                acc_ref[rows:] += part
        else:
            fetch_own(i).wait()
            fetch_weights(i).wait()
            put_half(i).start()
            a = jnp.concatenate([a_s[i - early], other(i)], axis=0)
            acc_ref[...] += jnp.dot(a, weight_block(w_s, i - early), preferred_element_type=jnp.float32)
    for h in range(NH):
        for c in range(3):
            lo = c * NH * HD + h * HD
            to = slice((h * 3 + c) * HD, (h * 3 + c + 1) * HD)
            x = acc_ref[:, lo : lo + HD].astype(jnp.bfloat16)
            own_out[:, to] = x[0:rows]
            send_out[:, to] = x[rows:]
    theirs = pair_head(where_ref[0], side)
    send_out[:, 9 * HD : 12 * HD] = own_out[:, head_columns(theirs, 3)]
    send_out[:, 12 * HD :] = g_ref[:, head_columns(theirs, 1)]
    for i in range(chunks):
        put_half(i).wait()


def project(where, part, own, other, w_early, w5, g):
    rows, depth = own.shape
    chunks = w5.shape[1] // 2
    early = w_early.shape[1] // 2
    vmem = pl.BlockSpec(memory_space=pltpu.VMEM)
    hbm = pl.BlockSpec(memory_space=pltpu.HBM)
    dma = pltpu.SemaphoreType.DMA((chunks,))
    return pl.pallas_call(
        functools.partial(project_kernel, early),
        in_specs=[pl.BlockSpec(memory_space=pltpu.SMEM), vmem, hbm, vmem, vmem, hbm, vmem],
        out_specs=[vmem, vmem, hbm],
        out_shape=[
            jax.ShapeDtypeStruct((rows, 9 * HD), jnp.bfloat16),
            jax.ShapeDtypeStruct((rows, 13 * HD), jnp.bfloat16),
            pltpu.HBM((3,) + w5.shape[1:2] + w5.shape[3:], jnp.bfloat16),
        ],
        scratch_shapes=[
            pltpu.VMEM((chunks - early, rows, depth // chunks), jnp.bfloat16),
            pltpu.VMEM((3, 2 * (chunks - early)) + w5.shape[2:], jnp.bfloat16),
            pltpu.VMEM((2 * rows, 9 * HD), jnp.float32),
            dma,
            dma,
            dma,
        ],
        compiler_params=pltpu.CompilerParams(vmem_limit_bytes=26 * MIB),
        cost_estimate=pl.CostEstimate(flops=7 * 10**9, bytes_accessed=10**7, transcendentals=0),
        name="project",
    )(where, part, own, other, w_early, w5, g)


def pair_head(chip, core):
    return jnp.minimum((chip + 1 + 2 * core) % RING, NH - 1)


def head_columns(head, width):
    return pl.ds(pl.multiple_of(head * (width * HD), width * HD), width * HD)


def section_rows(mod_ref, block, core, rows):
    lines = mod_ref.shape[0]
    mine = (mod_ref[...] == core).astype(jnp.float32)
    line = (lax.broadcasted_iota(jnp.int32, (rows, lines), 0) + block * rows) // HD
    place = (lax.broadcasted_iota(jnp.int32, (rows, HD), 0) + block * rows) % HD
    spread = jnp.dot(
        (line == lax.broadcasted_iota(jnp.int32, (rows, lines), 1)).astype(jnp.float32),
        mine,
        preferred_element_type=jnp.float32,
    )
    return jnp.sum(jnp.where(place == lax.broadcasted_iota(jnp.int32, (rows, HD), 1), spread, 0.0), axis=1, keepdims=True)


def route_kernel(where_ref, mod_ref, own_ref, sent_ref, got_ref, g_ref, pair_out, far_out, stay_out, mask_out):
    chip, core = where_ref[0], where_ref[1]
    rows = own_ref.shape[0]
    masks = [section_rows(mod_ref, 2 * chip + side, core, rows) for side in (core, 1 - core)]
    mine, others = [mask > 0 for mask in masks]
    for block, mask in enumerate(masks):
        mask_out[block] = jnp.broadcast_to(mask, (rows, HD)).astype(jnp.bfloat16)

    def own_rows(head):
        cols = head_columns(head, 3)
        return jnp.where(mine, own_ref[:, cols], got_ref[:, cols]), g_ref[:, head_columns(head, 1)]

    head = pair_head(chip, core)
    pair_out[0, :, : 3 * HD], pair_out[0, :, 3 * HD :] = own_rows(head)
    pair_out[1, :, : 3 * HD] = jnp.where(others, sent_ref[:, head_columns(head, 3)], got_ref[:, 9 * HD : 12 * HD])
    pair_out[1, :, 3 * HD :] = got_ref[:, 12 * HD :]
    far_out[:, : 3 * HD], far_out[:, 3 * HD :] = own_rows(jnp.minimum((chip + 2) % RING, NH - 1))
    stay_out[:, : 3 * HD], stay_out[:, 3 * HD :] = own_rows(jnp.minimum(chip, NH - 1))


def small_call(kernel, name, where, operands, out_shape):
    vmem = pl.BlockSpec(memory_space=pltpu.VMEM)
    return pl.pallas_call(
        kernel,
        in_specs=[pl.BlockSpec(memory_space=pltpu.SMEM)] + [vmem] * len(operands),
        out_specs=[vmem] * len(out_shape),
        out_shape=out_shape,
        compiler_params=pltpu.CompilerParams(vmem_limit_bytes=16 * MIB),
        cost_estimate=pl.CostEstimate(flops=10**6, bytes_accessed=3 * 10**6, transcendentals=0),
        name=name,
    )(where, *operands)


def attention_kernel(
    where_ref, stay, far, pair, stay_o, far_o, pair_o, keep_ref, send_ref, q_s, g_s, k_s, v_s, dq_s, dk_s, dv_s
):
    chip = where_ref[0]
    core = where_ref[1]
    rows = stay.shape[0]
    both = 2 * rows
    near = (chip + 3 + 2 * core) % RING
    across = (chip + 1 + 2 * core) % RING
    opposite = (chip + 2) % RING

    def block_rows(shard, side):
        return pl.ds(pl.multiple_of((2 * shard + side) * rows, rows), rows)

    for shard, r, o in (
        (chip, stay, stay_o),
        (opposite, far, far_o),
        (near, pair.at[0], pair.at[1]),
        (across, pair_o.at[1], pair_o.at[0]),
    ):
        q_s[shard] = r[:, 0:HD]
        g_s[shard] = r[:, 3 * HD : 4 * HD]
        k_s[block_rows(shard, core), :] = r[:, HD : 2 * HD]
        v_s[block_rows(shard, core), :] = r[:, 2 * HD : 3 * HD]
        k_s[block_rows(shard, 1 - core), :] = o[:, HD : 2 * HD]
        v_s[block_rows(shard, 1 - core), :] = o[:, 2 * HD : 3 * HD]
    nt = (((1,), (1,)), ((), ()))
    tn = (((0,), (0,)), ((), ()))
    for s in range(RING - 1, -1, -1):
        width = both * (s + 1)
        q = q_s[s]
        g = g_s[s]
        kk = k_s[0:width, :]
        vv = v_s[0:width, :]
        scores = lax.dot_general(q, kk, nt, preferred_element_type=jnp.float32) * SCALE
        row = lax.broadcasted_iota(jnp.int32, (rows, width), 0) + (2 * s + core) * rows
        col = lax.broadcasted_iota(jnp.int32, (rows, width), 1)
        scores = jnp.where(col <= row, scores, -jnp.inf)
        lifted = jnp.exp(scores - jnp.max(scores, axis=1, keepdims=True))
        probs = lifted / jnp.sum(lifted, axis=1, keepdims=True)
        low = probs.astype(jnp.bfloat16)
        dprobs = lax.dot_general(g, vv, nt, preferred_element_type=jnp.float32)
        row_dot = jnp.sum(probs * dprobs, axis=1, keepdims=True)
        ds = (probs * (dprobs - row_dot)).astype(jnp.bfloat16)
        dq = jnp.dot(ds, kk, preferred_element_type=jnp.float32) * SCALE
        dk = lax.dot_general(ds, q, tn, preferred_element_type=jnp.float32) * SCALE
        dv = lax.dot_general(low, g, tn, preferred_element_type=jnp.float32)
        if s == RING - 1:
            dk_s[...] = dk
            dv_s[...] = dv
        else:
            dk_s[0:width, :] += dk
            dv_s[0:width, :] += dv
        dq_s[s] = dq
    col = 0
    for shard, whole in ((near, True), (near, False), (chip, True), (opposite, True)):
        if whole:
            keep_ref[:, col : col + HD] = dq_s[shard]
            col += HD
        side = core if whole else 1 - core
        keep_ref[:, col : col + HD] = dk_s[block_rows(shard, side), :]
        keep_ref[:, col + HD : col + 2 * HD] = dv_s[block_rows(shard, side), :]
        col += 2 * HD
    col = 0
    for shard, whole in ((across, True), (across, False), (chip, False), (opposite, False)):
        if whole:
            send_ref[:, col : col + HD] = dq_s[shard].astype(jnp.bfloat16)
            col += HD
        side = core if whole else 1 - core
        send_ref[:, col : col + HD] = dk_s[block_rows(shard, side), :].astype(jnp.bfloat16)
        send_ref[:, col + HD : col + 2 * HD] = dv_s[block_rows(shard, side), :].astype(jnp.bfloat16)
        col += 2 * HD


def attention(where, parts):
    rows = parts[0].shape[0]
    total = 2 * RING * rows
    vmem = pl.BlockSpec(memory_space=pltpu.VMEM)
    return pl.pallas_call(
        attention_kernel,
        in_specs=[pl.BlockSpec(memory_space=pltpu.SMEM)] + [vmem] * 6,
        out_specs=[vmem, vmem],
        out_shape=[
            jax.ShapeDtypeStruct((rows, 11 * HD), jnp.float32),
            jax.ShapeDtypeStruct((rows, 9 * HD), jnp.bfloat16),
        ],
        scratch_shapes=[
            pltpu.VMEM((RING, rows, HD), jnp.bfloat16),
            pltpu.VMEM((RING, rows, HD), jnp.bfloat16),
            pltpu.VMEM((total, HD), jnp.bfloat16),
            pltpu.VMEM((total, HD), jnp.bfloat16),
            pltpu.VMEM((RING, rows, HD), jnp.float32),
            pltpu.VMEM((total, HD), jnp.float32),
            pltpu.VMEM((total, HD), jnp.float32),
        ],
        compiler_params=pltpu.CompilerParams(vmem_limit_bytes=32 * MIB),
        cost_estimate=pl.CostEstimate(flops=10**9, bytes_accessed=4 * 10**6, transcendentals=10**6),
        name="attention",
    )(where, *parts)


def combine_kernel(where_ref, keep, got, pair_out, far_out, stay_out):
    def put(out, query, kept, partner):
        out[:, 0:HD] = query.astype(jnp.bfloat16)
        kv = keep[:, kept : kept + 2 * HD] + got[:, partner : partner + 2 * HD].astype(jnp.float32)
        out[:, HD : 3 * HD] = kv.astype(jnp.bfloat16)

    put(pair_out.at[0], keep[:, 0:HD], HD, 3 * HD)
    put(pair_out.at[1], got[:, 0:HD], 3 * HD, HD)
    put(stay_out, keep[:, 5 * HD : 6 * HD], 6 * HD, 5 * HD)
    put(far_out, keep[:, 8 * HD : 9 * HD], 9 * HD, 7 * HD)


def gather(where, mask_ref, parts, out_ref):
    chip, core = where
    stay, far, pair, stay_o, far_o, pair_o = parts
    rows = stay.shape[0]
    for head, refs in (
        (chip, (stay, stay_o)),
        ((chip + 2) % RING, (far, far_o)),
        ((chip + 1 + 2 * core) % RING, (pair.at[0], pair.at[1])),
        ((chip + 3 + 2 * core) % RING, (pair_o.at[1], pair_o.at[0])),
    ):

        @pl.when(head < NH)
        def _():
            for block, x_ref in enumerate(refs):
                for c in range(3):
                    x = x_ref[:, c * HD : (c + 1) * HD]
                    mine = x * mask_ref[block]
                    for side, kept in enumerate((mine, x - mine)):
                        lo = pl.multiple_of(((side * 3 + c) * NH + head) * HD, HD)
                        out_ref[block * rows : (block + 1) * rows, pl.ds(lo, HD)] = kept


def destination(where_ref, i, j):
    core, tp = where_ref[1], where_ref[2]
    dy, dz = jnp.where(core == 0, j, i), jnp.where(core == 0, i, j)
    return (tp // RING + dy) % RING * RING + (tp % RING + dz) % RING


def weight_copies(where_ref, own_hbm, other_hbm, to_ref, sem, hop):
    core = where_ref[1]
    copies = []
    for j in range(RING):
        dest = destination(where_ref, hop, j)
        copies.append(pltpu.make_async_copy(own_hbm.at[:, dest, core], to_ref.at[0, :, j], sem.at[0, j]))
        copies.append(pltpu.make_async_copy(other_hbm.at[:, dest], to_ref.at[1, :, j], sem.at[1, j]))
    return copies


def fetch_kernel(hops, where_ref, after_ref, own_hbm, other_hbm, *refs):
    copies = []
    for i, hop in enumerate(hops):
        copies += weight_copies(where_ref, own_hbm, other_hbm, refs[i], refs[len(hops) + i], hop)
    for copy in copies:
        copy.start()
    for copy in copies:
        copy.wait()


def fetch_weights(where, after, w5, other_half, hops):
    vmem = pl.BlockSpec(memory_space=pltpu.VMEM)
    hbm = pl.BlockSpec(memory_space=pltpu.HBM)
    anywhere = pl.BlockSpec(memory_space=pl.ANY)
    return pl.pallas_call(
        functools.partial(fetch_kernel, hops),
        in_specs=[pl.BlockSpec(memory_space=pltpu.SMEM), vmem, hbm, anywhere],
        out_specs=[vmem for _ in hops],
        out_shape=[pltpu.VMEM((2, 3, RING) + w5.shape[3:], jnp.bfloat16) for _ in hops],
        scratch_shapes=[pltpu.SemaphoreType.DMA((2, RING)) for _ in hops],
        compiler_params=pltpu.CompilerParams(vmem_limit_bytes=20 * MIB),
        cost_estimate=pl.CostEstimate(flops=10**6, bytes_accessed=10**7, transcendentals=0),
        name="fetch_weights",
    )(where, after, w5, other_half)


def product(g_ref, w_ref, outs):
    cols = w_ref.shape[3]
    w = [w_ref[side, c].reshape(RING * cols, NH * HD) for side in range(2) for c in range(3)]
    res = lax.dot_general(
        g_ref[...], jnp.concatenate(w, axis=1), (((1,), (1,)), ((), ())), preferred_element_type=jnp.float32
    ).astype(jnp.bfloat16)
    for i in range(RING):
        outs[i // 2][i % 2] = res[:, i * cols : (i + 1) * cols]


def back_first_kernel(following, where_ref, mask_ref, *refs):
    *parts, w_ref, own_hbm, other_hbm, out_a, out_b, g_ref, next_ref, sem = refs
    for copy in weight_copies(where_ref, own_hbm, other_hbm, next_ref, sem, following):
        copy.start()
    gather((where_ref[0], where_ref[1]), mask_ref, parts, g_ref)
    product(g_ref, w_ref, (out_a, out_b))
    for copy in weight_copies(where_ref, own_hbm, other_hbm, next_ref, sem, following):
        copy.wait()


def back_middle_kernel(g_ref, w_ref, out_a, out_b):
    product(g_ref, w_ref, (out_a, out_b))


def back_last_kernel(after_a, after_b, g_ref, w_ref, out_a, out_b):
    product(g_ref, w_ref, (out_a, out_b))


def back_call(kernel, operands, in_specs, out_shape, scratch):
    vmem = pl.BlockSpec(memory_space=pltpu.VMEM)
    return pl.pallas_call(
        kernel,
        in_specs=in_specs,
        out_specs=[vmem] * len(out_shape),
        out_shape=out_shape,
        scratch_shapes=scratch,
        compiler_params=pltpu.CompilerParams(vmem_limit_bytes=16 * MIB),
        cost_estimate=pl.CostEstimate(flops=10**6, bytes_accessed=10**4, transcendentals=0),
        name="back",
    )(*operands)


def add_kernel(a_ref, b_ref, out_ref):
    out_ref[...] = (a_ref[...].astype(jnp.float32) + b_ref[...].astype(jnp.float32)).astype(jnp.bfloat16)


def add(a, b):
    vmem = pl.BlockSpec(memory_space=pltpu.VMEM)
    return pl.pallas_call(
        add_kernel,
        in_specs=[vmem, vmem],
        out_specs=vmem,
        out_shape=jax.ShapeDtypeStruct(a.shape, jnp.bfloat16),
        compiler_params=pltpu.CompilerParams(vmem_limit_bytes=16 * MIB),
        cost_estimate=pl.CostEstimate(flops=10**5, bytes_accessed=10**4, transcendentals=0),
        name="add",
    )(a, b)


def back_reduced(where, masks, parts, weights, w5, other_half):
    rows = 2 * parts[0].shape[0]
    cols = w5.shape[3]
    smem = pl.BlockSpec(memory_space=pltpu.SMEM)
    vmem = pl.BlockSpec(memory_space=pltpu.VMEM)
    hbm = pl.BlockSpec(memory_space=pltpu.HBM)
    anywhere = pl.BlockSpec(memory_space=pl.ANY)
    halves = [jax.ShapeDtypeStruct((RING // 2, rows, cols), jnp.bfloat16)] * 2
    w_shape = (2, 3, RING) + w5.shape[3:]
    sem = pltpu.SemaphoreType.DMA((2, RING))

    def onward(x):
        return lax.ppermute(x, AXES, ring_perm(True, 1))

    def backward(x):
        return lax.ppermute(x, AXES, ring_perm(True, -1))

    w_two, w_one, w_zero = weights
    two_a, two_b, g, w_three = back_call(
        functools.partial(back_first_kernel, 3),
        (where, masks, *parts, w_two, w5, other_half),
        [smem] + [vmem] * 8 + [hbm, anywhere],
        halves + [pltpu.VMEM((rows, 18 * HD), jnp.bfloat16), pltpu.VMEM(w_shape, jnp.bfloat16)],
        [sem],
    )
    g = pltpu.with_memory_space_constraint(g, pltpu.VMEM)
    w_three = pltpu.with_memory_space_constraint(w_three, pltpu.VMEM)
    relay_a, relay_b = onward(two_a), backward(two_b)
    one_a, one_b = back_call(back_middle_kernel, (g, w_one), [vmem, vmem], halves, [])
    from_one_b = onward(one_b)
    three_a, three_b = back_call(back_middle_kernel, (g, w_three), [vmem, vmem], halves, [])
    from_three_a = backward(three_a)
    one_a = add(one_a, relay_a)
    three_b = add(three_b, relay_b)
    from_one_a, from_three_b = onward(one_a), backward(three_b)
    own_a, own_b = back_call(
        back_last_kernel, (one_a, three_b, g, w_zero), [anywhere, anywhere, vmem, vmem], halves, []
    )
    sum_b = own_b.astype(jnp.float32) + from_one_b.astype(jnp.float32)
    own_a, sum_b = lax.optimization_barrier((own_a, sum_b))
    sum_a = own_a.astype(jnp.float32) + from_three_a.astype(jnp.float32)
    sum_a, sum_b = lax.optimization_barrier((sum_a, sum_b))
    sum_a = sum_a + from_one_a.astype(jnp.float32)
    sum_a, sum_b = lax.optimization_barrier((sum_a, sum_b))
    sum_b = sum_b + from_three_b.astype(jnp.float32)
    return [sum_a[0], sum_a[1], sum_b[0], sum_b[1]]


def ring_perm(first, hop):
    pairs = []
    for s in range(RING):
        for m in range(2):
            for y in range(RING):
                for z in range(RING):
                    if (m == 0) == first:
                        to = (y, (z + hop) % RING)
                    else:
                        to = ((y + hop) % RING, z)
                    base = (s * 2 + m) * RING * RING
                    pairs.append((base + y * RING + z, base + to[0] * RING + to[1]))
    return pairs


def pair_perm(step):
    pairs = []
    for s in range(RING):
        for m in range(2):
            head = (s + (1 if m == 0 else -1)) % RING
            if step > 0 and head < NH:
                pairs.append((2 * s + m, 2 * head + m))
            if step < 0 and s < NH:
                pairs.append((2 * s + m, 2 * ((s + (-1 if m == 0 else 1)) % RING) + m))
    return pairs


def per_device(activations, grad_attn, weights, modality):
    rows, depth = activations.shape
    chip = lax.axis_index("seq")
    core = lax.axis_index("mod")
    tp = lax.axis_index("tp")
    where = jnp.stack([chip, core, tp]).astype(jnp.int32)
    dests = RING * RING
    cols = depth // dests // 2
    w5 = jnp.transpose(weights[0], (1, 0, 2)).reshape(3, dests, 2, cols, NH * HD)

    mod = modality.reshape(-1, HD)
    w5 = pltpu.with_memory_space_constraint(w5, pltpu.HBM)
    activations = pltpu.with_memory_space_constraint(activations, pltpu.HBM)
    act_other = pltpu.with_memory_space_constraint(core_swap(activations), pltpu.VMEM)
    part, w_early = project_own(activations, w5, 5)
    w_early = pltpu.with_memory_space_constraint(w_early, pltpu.VMEM)
    proj_own, sent, half = project(where, part, activations, act_other, w_early, w5, grad_attn)
    got = core_swap(sent)
    got, half = lax.optimization_barrier((got, half))
    other_half = core_swap(half)

    def part_shapes(width):
        block = jax.ShapeDtypeStruct((rows, width), jnp.bfloat16)
        return [jax.ShapeDtypeStruct((2, rows, width), jnp.bfloat16), block, block]

    pair, far, stay, masks = small_call(
        route_kernel,
        "route",
        where,
        (mod, proj_own, sent, got, grad_attn),
        part_shapes(4 * HD) + [jax.ShapeDtypeStruct((2, rows, HD), jnp.bfloat16)],
    )
    pair = lax.ppermute(pair, ("seq", "mod"), pair_perm(1))
    far = lax.ppermute(far, "seq", [(i, (i + 2) % RING) for i in range(RING) if (i + 2) % RING < NH])
    parts = [stay, far, pair]
    keep, send = attention(where, parts + [core_swap(x) for x in parts])
    pair, far, stay = small_call(combine_kernel, "combine", where, (keep, core_swap(send)), part_shapes(3 * HD))

    w_first = fetch_weights(where, stay, w5, other_half, (2, 1, 0))
    w_first = [pltpu.with_memory_space_constraint(w, pltpu.VMEM) for w in w_first]
    pair = lax.ppermute(pair, ("seq", "mod"), pair_perm(-1))
    far = lax.ppermute(far, "seq", [(i, (i + 2) % RING) for i in range(NH)])
    pair, far, w_first = lax.optimization_barrier((pair, far, w_first))
    parts = [stay, far, pair]
    parts += [core_swap(x) for x in parts]

    total = back_reduced(where, masks, parts, w_first, w5, other_half)
    result = total[0]
    for hop in (1, 3, 2):
        got = lax.ppermute(total[hop].astype(jnp.bfloat16), AXES, ring_perm(False, hop))
        result = lax.optimization_barrier(result) + got.astype(jnp.float32)
    result = result.astype(jnp.bfloat16)
    mine = result[:rows]
    theirs = core_swap(result[rows:])
    return jnp.where(
        core == 0, jnp.concatenate([mine, theirs], axis=1), jnp.concatenate([theirs, mine], axis=1)
    )


def solution(mesh):
    in_specs = (P(("seq", "mod"), None), P(("seq", "mod"), "tp"), P("mod", None, None, "tp"), P())
    out_specs = P(("seq", "mod"), "tp")
    return jax.shard_map(
        per_device, mesh=mesh, in_specs=in_specs, out_specs=out_specs, check_vma=False
    )
```
